128 devices in a mesh: dp: 4 (over y), seq: 8 (over z, core), mp: 4 (over x).
Axes of the slice: x: 4, y: 4, z: 4, core: 2. Of those that a mesh axis runs over, the one named last changes fastest.
Arguments:
- tokens: bfloat16 [4, 4096, 1024], P('dp', 'seq'), may hold values from -6 to 6
- states: bfloat16 [4, 8, 512, 1024], P('dp', 'seq'), may hold values from -6 to 6
- doc_lengths: int32 [4, 4], P('dp'), may hold values from 1 to 3840, 4096 in all within a row
- w_query: bfloat16 [1024, 1024], P(('dp', 'seq'), 'mp'), may hold values from -0.1875 to 0.1875
- w_key: bfloat16 [1024, 1024], P(('dp', 'seq'), 'mp'), may hold values from -0.1875 to 0.1875
- w_value: bfloat16 [1024, 1024], P(('dp', 'seq'), 'mp'), may hold values from -0.1875 to 0.1875
- w_output: bfloat16 [1024, 1024], P('mp', ('dp', 'seq')), may hold values from -6 to 6
- w_gate: bfloat16 [1024, 4096], P(('dp', 'seq'), 'mp'), may hold values from -0.1875 to 0.1875
- w_up: bfloat16 [1024, 4096], P(('dp', 'seq'), 'mp'), may hold values from -0.1875 to 0.1875
- w_down: bfloat16 [4096, 1024], P('mp', ('dp', 'seq')), may hold values from -0.09375 to 0.09375
- attention_gain: bfloat16 [1024], P(('dp', 'seq')), may hold values from 0.5 to 1.5
- state_gain: bfloat16 [1024], P(('dp', 'seq')), may hold values from 0.5 to 1.5
- forward_gain: bfloat16 [1024], P(('dp', 'seq')), may hold values from 0.5 to 1.5
- forget_bias: bfloat16 [1024], P(('dp', 'seq')), may hold values from -6 to 6
- d_output: bfloat16 [4, 4096, 1024], P('dp', 'seq'), may hold values from -6 to 6
- d_new_states: bfloat16 [4, 8, 512, 1024], P('dp', 'seq'), may hold values from -6 to 6
Outputs:
- result: bfloat16 [4, 4096, 1024], P('dp', 'seq')
- new_states: bfloat16 [4, 8, 512, 1024], P('dp', 'seq')
- d_tokens: float32 [4, 4096, 1024], P('dp', 'seq')
- d_states: float32 [4, 8, 512, 1024], P('dp', 'seq')
- d_query: float32 [1024, 1024], P(('dp', 'seq'), 'mp')
- d_key: float32 [1024, 1024], P(('dp', 'seq'), 'mp')
- d_value: float32 [1024, 1024], P(('dp', 'seq'), 'mp')
- d_outproj: float32 [1024, 1024], P('mp', ('dp', 'seq'))
- d_gate: float32 [1024, 4096], P(('dp', 'seq'), 'mp')
- d_upproj: float32 [1024, 4096], P(('dp', 'seq'), 'mp')
- d_down: float32 [4096, 1024], P('mp', ('dp', 'seq'))
- d_attention_gain: float32 [1024], P(('dp', 'seq'))
- d_state_gain: float32 [1024], P(('dp', 'seq'))
- d_forward_gain: float32 [1024], P(('dp', 'seq'))
- d_forget_bias: float32 [1024], P(('dp', 'seq'))
The draws below stay inside these ranges and needn't reach their ends.
Inputs may be any that keep to these rules, and one draw needn't show every extreme that they name: `doc_lengths`: the 4 document lengths of a segment sum to 4096, and one of them is exactly 3840.
All inputs are finite; a program needn't handle non-finite values.
Results may differ from the reference program's by a relative error of at most 0.03.
Values may be sent and summed in bfloat16 or wider, within the bound.
No kernel may reach another device: no remote copies, remote signals or barrier semaphores. Data moves between devices by JAX's collectives and lax.ppermute only.
A program may use at most 128 MiB of HBM per device.

```python
import math
import jax
import jax.numpy as jnp
import numpy as np
from jax import lax

D = 1024
HEADS = 8
HD = 128
FF = 4096
W = 512
NS = 512
NDOC = 4
NWIN = 8
L = 4096
B = 4


def steps_of(stream_key, dims, shards, smallest, largest):
    loudness, own = 1.0, jax.random.fold_in(stream_key, 6)
    for dim, blocks in shards:
        draws = jnp.exp(jax.random.uniform(jax.random.fold_in(own, dim), (blocks,), jnp.float32, smallest / len(shards), largest / len(shards)))
        loudness = loudness * jnp.repeat(draws, dims[dim] // blocks).reshape([-1 if axis == dim else 1 for axis in range(len(dims))])
    return loudness


def split_up(amount, total, limit, slope):
    loads = [(1 << 20) // math.isqrt(rank ** slope) + 1 for rank in range(2, amount + 1)]
    surplus, holding = total - limit - (amount - 1), [1] * (amount - 1)
    while surplus > 0:
        movable = [i for i in range(amount - 1) if holding[i] < limit]
        whole, budget = sum([loads[i] for i in movable]), surplus
        for i in movable:
            addition = min(limit - holding[i], max(1, budget * loads[i] // whole), surplus)
            holding[i] = holding[i] + addition
            surplus = surplus - addition
    return np.array([limit] + holding)


def uneven(own_key, amount, total, limit, skew):
    if amount == 2:
        one = jax.random.randint(own_key, (), max(1, total - limit), min(limit, total - 1) + 1)
        return jnp.stack([one, total - one])
    sizes = jnp.asarray(split_up(amount, total, limit, skew), jnp.int32)
    pairs = (amount - 1) // 2
    source_of, taker = sizes[1:1 + 2 * pairs:2], sizes[2:2 + 2 * pairs:2]
    margin = jnp.minimum(source_of - 1, limit - taker)
    moved = jax.random.randint(jax.random.fold_in(own_key, 1), (pairs,), 0, 1 << 20) % (margin + 1)
    sizes = sizes.at[1:1 + 2 * pairs:2].set(source_of - moved).at[2:2 + 2 * pairs:2].set(taker + moved)
    return sizes[jax.random.permutation(jax.random.fold_in(own_key, 2), amount)]


def normal_values(rng, shape, deviation, reach, shards=(), kind=jnp.bfloat16):
    entries = jax.random.normal(rng, shape, jnp.float32) * deviation
    if len(shards) > 0:
        entries = steps_of(rng, shape, shards, -0.22, 0.18) * entries
    return jnp.clip(entries, min=-reach, max=reach).astype(kind)


def setup_inputs(seed: int = 0) -> dict:
    seeds = jax.random.split(jax.random.key(seed), 17)
    tokens = normal_values(seeds[0], (B, L, D), 1.0, 6.0, ((0, 4), (1, 8)))
    states = normal_values(seeds[1], (B, NWIN, NS, D), 1.0, 6.0, ((0, 4), (1, 8)))
    doc_lengths = jax.vmap(lambda own: uneven(own, NDOC, L, L - W // 2, 0))(jax.random.split(seeds[2], B)).reshape((B, NDOC)).astype(jnp.int32)
    w_query = normal_values(seeds[3], (D, HEADS * HD), D ** -0.5, 0.1875, ((0, 32), (1, 4)))
    w_key = normal_values(seeds[4], (D, HEADS * HD), D ** -0.5, 0.1875, ((0, 32), (1, 4)))
    w_value = normal_values(seeds[5], (D, HEADS * HD), D ** -0.5, 0.1875, ((0, 32), (1, 4)))
    w_output = normal_values(seeds[6], (HEADS * HD, D), (max(1, HEADS * HD // (2 * W))) ** -0.5, 6.0, ((0, 4), (1, 32)))
    w_gate = normal_values(seeds[7], (D, FF), D ** -0.5, 0.1875, ((0, 32), (1, 4)))
    w_up = normal_values(seeds[8], (D, FF), D ** -0.5, 0.1875, ((0, 32), (1, 4)))
    w_down = normal_values(seeds[9], (FF, D), FF ** -0.5, 0.09375, ((0, 4), (1, 32)))
    attention_gain = jnp.clip(1.0 + 0.1 * jax.random.normal(seeds[10], (D,), jnp.float32), 0.5, 1.5).astype(jnp.bfloat16)
    state_gain = jnp.clip(1.0 + 0.1 * jax.random.normal(seeds[11], (D,), jnp.float32), 0.5, 1.5).astype(jnp.bfloat16)
    forward_gain = jnp.clip(1.0 + 0.1 * jax.random.normal(seeds[12], (D,), jnp.float32), 0.5, 1.5).astype(jnp.bfloat16)
    forget_bias = normal_values(seeds[13], (D,), 2.0, 6.0, ((0, 32),))
    d_output = normal_values(seeds[14], (B, L, D), 1.0, 6.0, ((0, 4), (1, 8)))
    d_new_states = normal_values(seeds[15], (B, NWIN, NS, D), 1.0, 6.0, ((0, 4), (1, 8)))
    return dict(tokens=tokens, states=states, doc_lengths=doc_lengths, w_query=w_query, w_key=w_key, w_value=w_value, w_output=w_output, w_gate=w_gate, w_up=w_up, w_down=w_down, attention_gain=attention_gain, state_gain=state_gain, forward_gain=forward_gain, forget_bias=forget_bias, d_output=d_output, d_new_states=d_new_states)


EPS = 1e-05
NEG = -1e+30
HIGH = lax.Precision.HIGHEST

@jax.custom_vjp
def low(v):
    return lax.optimization_barrier(v.astype(jnp.bfloat16)).astype(jnp.float32)

@jax.custom_vjp
def low_back(v):
    return v

def low_keep(v):
    return (low(v), None)

def low_pass(kept, grad):
    return (grad,)

def back_keep(v):
    return (v, None)

def back_low(kept, grad):
    return (low(grad),)
low.defvjp(low_keep, low_pass)
low_back.defvjp(back_keep, back_low)

def product(left, right):
    return jnp.dot(left, right, precision=HIGH, preferred_element_type=jnp.float32)

def normed(values, gain):
    return values * lax.rsqrt(lax.optimization_barrier(jnp.mean(values * values, axis=-1, keepdims=True)) + EPS) * gain

def attend(queries, keys, values, mask):
    raw = jnp.einsum('qhd,khd->hqk', queries, keys, precision=HIGH) * HD ** (-0.5)
    scores = jnp.where(mask[None], low_back(raw), NEG)
    probs = low(jax.nn.softmax(scores, axis=-1))
    return low_back(low(jnp.einsum('hqk,khd->qhd', probs, values, precision=HIGH)))

def segment(token_rows, state_rows, seg_lengths, query_w, key_w, value_w, output_w, gate_w, up_w, down_w, gain_attn, gain_state, gain_forward, bias_forget):
    length = token_rows.shape[0]
    window_count = state_rows.shape[0]
    flat_states = state_rows.reshape(window_count * NS, D)
    normed_rows = jnp.concatenate([low(normed(token_rows, gain_attn)), low(normed(flat_states, gain_state))], axis=0)
    queries = low_back(low(product(normed_rows, query_w)))
    keys = low_back(low(product(normed_rows, key_w)))
    values = low_back(low(product(normed_rows, value_w)))
    key_tok, value_tok = (keys[:length], values[:length])
    key_state, value_state = (keys[length:], values[length:])
    query_tok, query_state = (queries[:length], queries[length:])
    padding = jnp.zeros((W, HEADS * HD), jnp.float32)
    key_pad = jnp.concatenate([padding, key_tok], axis=0)
    value_pad = jnp.concatenate([padding, value_tok], axis=0)
    ends = jnp.cumsum(seg_lengths)
    positions = jnp.arange(length, dtype=jnp.int32)
    documents = lax.optimization_barrier(jnp.sum((positions[:, None] >= ends[None, :]).astype(jnp.int32), axis=1, dtype=jnp.int32))
    doc_pad = jnp.concatenate([jnp.zeros((W,), jnp.int32), documents], axis=0)

    def window(index):
        start = index * W
        query_win = lax.dynamic_slice_in_dim(query_tok, start, W, 0).reshape(W, HEADS, HD)
        key_win = jnp.concatenate([lax.dynamic_slice_in_dim(key_pad, start, 2 * W, 0), lax.dynamic_slice_in_dim(key_state, index * NS, NS, 0)], axis=0).reshape(-1, HEADS, HD)
        value_win = jnp.concatenate([lax.dynamic_slice_in_dim(value_pad, start, 2 * W, 0), lax.dynamic_slice_in_dim(value_state, index * NS, NS, 0)], axis=0).reshape(-1, HEADS, HD)
        query_pos = start + jnp.arange(W, dtype=jnp.int32)
        key_pos = start - W + jnp.arange(2 * W, dtype=jnp.int32)
        query_doc = lax.dynamic_slice_in_dim(documents, start, W, 0)
        key_doc = lax.dynamic_slice_in_dim(doc_pad, start, 2 * W, 0)
        nearby = (key_pos[None, :] >= 0) & (key_pos[None, :] <= query_pos[:, None]) & (key_doc[None, :] == query_doc[:, None])
        mask = jnp.concatenate([nearby, jnp.ones((W, NS), dtype=bool)], axis=1)
        out_tok = attend(query_win, key_win, value_win, mask).reshape(W, HEADS * HD)
        state_query = lax.dynamic_slice_in_dim(query_state, index * NS, NS, 0).reshape(NS, HEADS, HD)
        state_keys = lax.dynamic_slice_in_dim(key_tok, start, W, 0).reshape(W, HEADS, HD)
        state_values = lax.dynamic_slice_in_dim(value_tok, start, W, 0).reshape(W, HEADS, HD)
        out_state = attend(state_query, state_keys, state_values, jnp.ones((NS, W), dtype=bool)).reshape(NS, HEADS * HD)
        return (out_tok, out_state)
    out_tok, out_state = lax.map(jax.checkpoint(window), jnp.arange(window_count, dtype=jnp.int32))
    out_tok = out_tok.reshape(length, HEADS * HD)
    out_state = out_state.reshape(window_count * NS, HEADS * HD)
    mixed_tok = low_back(product(out_tok, output_w))
    mixed_state = low_back(product(out_state, output_w))
    resid = token_rows + mixed_tok
    forget = jax.nn.sigmoid(bias_forget)
    updated = flat_states * forget + mixed_state * (1.0 - forget)
    ff_in = low(normed(resid, gain_forward))
    gate = low_back(product(ff_in, gate_w))
    upval = low_back(product(ff_in, up_w))
    hidden = low(jax.nn.silu(gate) * upval)
    output = resid + low_back(product(hidden, down_w))
    return (output, updated.reshape(window_count, NS, D))

def reference(tokens, states, doc_lengths, w_query, w_key, w_value, w_output, w_gate, w_up, w_down, attention_gain, state_gain, forward_gain, forget_bias, d_output, d_new_states):
    weights = tuple((item.astype(jnp.float32) for item in (w_query, w_key, w_value, w_output, w_gate, w_up, w_down, attention_gain, state_gain, forward_gain, forget_bias)))

    def one_segment(totals, items):
        seg_tokens, seg_states, seg_lengths, seg_grad, seg_grad_states = items

        def forward(token_rows, state_rows, *params):
            return segment(token_rows, state_rows, seg_lengths, *params)
        outputs, pullback = jax.vjp(forward, seg_tokens.astype(jnp.float32), seg_states.astype(jnp.float32), *weights)
        grads = pullback((seg_grad.astype(jnp.float32), seg_grad_states.astype(jnp.float32)))
        totals = tuple((total + grad for total, grad in zip(totals, grads[2:])))
        return (totals, (outputs[0].astype(jnp.bfloat16), outputs[1].astype(jnp.bfloat16), grads[0], grads[1]))
    begin = tuple((jnp.zeros_like(item) for item in weights))
    totals, outs = lax.scan(one_segment, begin, (tokens, states, doc_lengths, d_output, d_new_states))
    return (outs[0], outs[1], outs[2], outs[3], totals[0], totals[1], totals[2], totals[3], totals[4], totals[5], totals[6], totals[7], totals[8], totals[9], totals[10])
```

```python
import jax
import jax.numpy as jnp
from jax import lax
from jax.sharding import PartitionSpec as P

D = 1024
HD = 128
W = 512
NS = 512
PARTS = 4
BLOCK = W // PARTS


EPS = 1e-05
NEG = -1e30


def passed_along(value, axis, steps):
    count = lax.axis_size(axis)
    leading, last = (max(0, -steps), min(count, count - steps))
    return lax.ppermute(value, axis, [(source, source + steps) for source in range(leading, last)])


def shifted(value, axis, steps):
    count = lax.axis_size(axis)
    return lax.ppermute(value, axis, [(i, (i + steps) % count) for i in range(count)])


def shifted_y(value, steps):
    return shifted(value, "dp", steps)


def shifted_z(value, steps):
    return shifted(value, "seq", 2 * steps)


def other_core(value):
    return lax.ppermute(value, "seq", [(i, i ^ 1) for i in range(lax.axis_size("seq"))])


def product(left, right):
    return jnp.dot(left, right, preferred_element_type=jnp.float32)


def product_t(left, right):
    return lax.dot_general(
        left, right, (((1,), (1,)), ((), ())), preferred_element_type=jnp.float32
    )


def outer_sum(left, right):
    return lax.dot_general(
        left, right, (((0,), (0,)), ((), ())), preferred_element_type=jnp.float32
    )


def inv_rms(values):
    return lax.rsqrt(jnp.mean(values * values, axis=-1, keepdims=True) + EPS)


def norm_back(values, scale, gain, grad):
    inner = grad * gain
    along = jnp.mean(inner * values, axis=-1, keepdims=True)
    d_values = scale * inner - values * (scale * scale * scale) * along
    d_gain = jnp.sum(grad * values * scale, axis=0)
    return (d_values, d_gain)


def split_heads(values):
    return values.reshape(values.shape[0], -1, HD)


def attend_fwd(queries, keys, values, mask):
    raw = jnp.einsum("qhd,khd->hqk", queries, keys, preferred_element_type=jnp.float32)
    scores = raw * HD ** (-0.5)
    if mask is not None:
        scores = jnp.where(mask[None], scores, NEG)
    peak = jnp.max(scores, axis=-1, keepdims=True)
    total = jnp.sum(jnp.exp(scores - peak), axis=-1, keepdims=True)
    logsum = peak + jnp.log(total)
    probs = jnp.exp(scores - logsum).astype(jnp.bfloat16)
    output = jnp.einsum("hqk,khd->qhd", probs, values, preferred_element_type=jnp.float32)
    return (output.astype(jnp.bfloat16).reshape(queries.shape[0], -1), logsum)


def attend_back(queries, keys, values, mask, logsum, d_out):
    scale = HD ** (-0.5)
    raw = jnp.einsum("qhd,khd->hqk", queries, keys, preferred_element_type=jnp.float32)
    scores = raw * scale
    if mask is not None:
        scores = jnp.where(mask[None], scores, NEG)
    probs = jnp.exp(scores - logsum)
    d_probs = jnp.einsum("qhd,khd->hqk", d_out, values, preferred_element_type=jnp.float32)
    center = jnp.sum(probs * d_probs, axis=-1, keepdims=True)
    d_scores = (probs * (d_probs - center)).astype(jnp.bfloat16)
    d_queries = (
        jnp.einsum("hqk,khd->qhd", d_scores, keys, preferred_element_type=jnp.float32) * scale
    )
    d_keys = (
        jnp.einsum("hqk,qhd->khd", d_scores, queries, preferred_element_type=jnp.float32) * scale
    )
    d_values = jnp.einsum(
        "hqk,qhd->khd", probs.astype(jnp.bfloat16), d_out, preferred_element_type=jnp.float32
    )
    return (
        d_queries.reshape(queries.shape[0], -1),
        d_keys.reshape(keys.shape[0], -1),
        d_values.reshape(keys.shape[0], -1),
    )


def in_order(pieces, place):
    turned = [pieces[0], pieces[3], pieces[2], pieces[1]]
    twice = jnp.stack(turned + turned[:3])
    return lax.dynamic_slice_in_dim(twice, (PARTS - place) % PARTS, PARTS, 0)


def gathered_from(value, shift, place):
    return in_order([value] + [shift(value, k) for k in (1, 2, 3)], place)


def gather_planes(first, second, y, z, core):
    first = gathered_from(first, shifted_y, y)
    second = gathered_from(second, shifted_z, z)
    first = jnp.swapaxes(gathered_from(first, shifted_z, z), 0, 1)
    second = gathered_from(second, shifted_y, y)
    out = []
    for mine in (first, second):
        theirs = other_core(mine)
        pair = jnp.where(
            core == 0, jnp.stack([mine, theirs], axis=2), jnp.stack([theirs, mine], axis=2)
        )
        out.append(pair.reshape(D, mine.shape[-1]))
    return out


def scattered_to(value, shift, place):
    pieces = [
        lax.dynamic_index_in_dim(value, (place + k) % PARTS, 0, keepdims=False) for k in range(4)
    ]
    total = pieces[0].astype(jnp.float32)
    for k in (1, 2, 3):
        total = total + shift(pieces[k], k).astype(jnp.float32)
    return total


def scatter_planes(value, y, z, core):
    columns = value.shape[1]
    split = value.reshape(4, 4, 2, 32, columns)
    keep = lax.dynamic_index_in_dim(split, core, 2, keepdims=False)
    give = lax.dynamic_index_in_dim(split, 1 - core, 2, keepdims=False)
    total = (keep.astype(jnp.float32) + other_core(give).astype(jnp.float32)).astype(jnp.bfloat16)
    half = columns // 2
    first, second = total[..., :half], total[..., half:]
    first = scattered_to(jnp.swapaxes(first, 0, 1), shifted_z, z).astype(jnp.bfloat16)
    second = scattered_to(second, shifted_y, y).astype(jnp.bfloat16)
    first = scattered_to(first, shifted_y, y)
    second = scattered_to(second, shifted_z, z)
    return jnp.concatenate([first, second], axis=1)


def sum_everywhere(value):
    for shift in (lambda v, k: shifted(v, "mp", k), shifted_z, shifted_y):
        value = value + shift(value, 1) + shift(value, 2) + shift(value, 3)
    return value + other_core(value)


def turned(value, place):
    return jnp.concatenate(
        [
            lax.dynamic_slice_in_dim(value, ((place + 4 - k) % PARTS) * BLOCK, BLOCK, 0)
            for k in range(PARTS)
        ],
        axis=0,
    )


def sent_back(blocks):
    return [blocks[0]] + [shifted(blocks[k], "mp", -k) for k in (1, 2, 3)]


def shared(value):
    return [value] + [shifted(value, "mp", k) for k in (1, 2, 3)]


def row_blocks(value):
    return [value[k * BLOCK : (k + 1) * BLOCK] for k in range(PARTS)]


def total_of(pieces):
    total = pieces[0].astype(jnp.float32)
    for piece in pieces[1:]:
        total = total + piece.astype(jnp.float32)
    return total


def whole_rows(pieces, place):
    stacked = in_order(pieces, place)
    return stacked.reshape(-1, stacked.shape[-1])


def local(
    tokens,
    states,
    doc_lengths,
    w_query,
    w_key,
    w_value,
    w_output,
    w_gate,
    w_up,
    w_down,
    attention_gain,
    state_gain,
    forward_gain,
    forget_bias,
    d_output,
    d_new_states,
):
    bf16, f32 = jnp.bfloat16, jnp.float32
    place = lax.axis_index("mp")
    y = lax.axis_index("dp")
    seq = lax.axis_index("seq")
    z, core = seq // 2, seq % 2

    gains = jnp.stack([attention_gain, state_gain, forward_gain, forget_bias], axis=1)
    gains = jnp.pad(gains, ((0, 0), (0, 124)))
    first = jnp.concatenate([w_query, w_key, gains], axis=1)
    second = jnp.concatenate([w_value, w_output.T], axis=1)
    first, second = gather_planes(first, second, y, z, core)
    qkv_w = jnp.concatenate([first[:, :512], second[:, :256]], axis=1)
    own_output_w = second[:, 256:]
    vectors = first[:, 512:516].astype(f32).T
    gain_attn, gain_state, gain_forward = vectors[0], vectors[1], vectors[2]
    forget = jax.nn.sigmoid(vectors[3])

    ff_shard = jnp.concatenate([w_gate, w_up, w_down.T], axis=1)
    ff_shard, own_output_w = lax.optimization_barrier((ff_shard, own_output_w))
    ff_w = lax.all_gather(ff_shard, ("dp", "seq"), axis=0, tiled=True)
    gate_up_w, down_w = ff_w[:, :2048], ff_w[:, 2048:]
    output_w = jnp.concatenate(sent_back([own_output_w] * 4), axis=1)

    token_rows = turned(tokens[0], place).astype(f32)
    state_rows = turned(states[0, 0], place).astype(f32)
    grad_out = turned(d_output[0], place)
    grad_new = turned(d_new_states[0, 0], place).astype(f32)

    tok_scale = inv_rms(token_rows)
    state_scale = inv_rms(state_rows)
    normed_rows = jnp.concatenate(
        [token_rows * tok_scale * gain_attn, state_rows * state_scale * gain_state], axis=0
    ).astype(bf16)
    qkv = product(normed_rows, qkv_w).astype(bf16)
    queries, keys, values = qkv[:, :256], qkv[:, 256:512], qkv[:, 512:]

    start = seq * W
    ends = jnp.cumsum(doc_lengths[0])
    offsets = jnp.concatenate(
        [((place + 4 - k) % PARTS) * BLOCK + jnp.arange(BLOCK, dtype=jnp.int32) for k in range(4)]
    )
    key_pos = jnp.concatenate([start - W + offsets, start + offsets])
    key_docs = jnp.sum(
        (key_pos[:, None] >= ends[None, :]).astype(jnp.int32), axis=1, dtype=jnp.int32
    )
    query_pos, query_doc = key_pos[W:], key_docs[W:]
    nearby = (
        (key_pos[None, :] >= 0)
        & (key_pos[None, :] <= query_pos[:, None])
        & (key_docs[None, :] == query_doc[:, None])
    )
    mask = jnp.concatenate([nearby, jnp.ones((W, NS), dtype=bool)], axis=1)

    pair_tok = qkv[:W, 256:]
    pair_prev = passed_along(pair_tok, "seq", 1)
    pair_all = jnp.concatenate([pair_prev, qkv[:, 256:]], axis=0)
    query_tok, query_state = split_heads(queries[:W]), split_heads(queries[W:])
    key_all, value_all = split_heads(pair_all[:, :256]), split_heads(pair_all[:, 256:])
    key_tok, value_tok = split_heads(pair_tok[:, :256]), split_heads(pair_tok[:, 256:])
    attn_state, sums_state = attend_fwd(query_state, key_tok, value_tok, None)
    attn_tok, sums_tok = attend_fwd(query_tok, key_all, value_all, mask)

    both = [
        jnp.concatenate([a, b], axis=0) for a, b in zip(row_blocks(attn_tok), row_blocks(attn_state))
    ]
    attn_own = jnp.concatenate(sent_back(both), axis=1)
    mixed = product_t(attn_own, output_w)
    mixed_tok, mixed_state = mixed[:BLOCK], mixed[BLOCK:]
    tok_own, state_own, grad_new_own = token_rows[:BLOCK], state_rows[:BLOCK], grad_new[:BLOCK]
    resid = tok_own + mixed_tok
    updated = (state_own * forget + mixed_state * (1.0 - forget)).astype(bf16)
    ff_scale = inv_rms(resid)
    ff_in_own = (resid * ff_scale * gain_forward).astype(bf16)
    ff_in = jnp.concatenate(shared(ff_in_own), axis=0)
    updated = whole_rows(shared(updated), place)

    d_hidden = product(grad_out, down_w)
    gate_up = product(ff_in, gate_up_w)
    gate_val, up_val = gate_up[:, :1024], gate_up[:, 1024:]
    sigma = jax.nn.sigmoid(gate_val)
    active = gate_val * sigma
    hidden = (active * up_val).astype(bf16)
    d_gate_val = (d_hidden * up_val * sigma * (1.0 + gate_val * (1.0 - sigma))).astype(bf16)
    d_up_val = (d_hidden * active).astype(bf16)
    d_gate_up = jnp.concatenate([d_gate_val, d_up_val], axis=1)
    d_ff_in = product_t(d_gate_up, gate_up_w).astype(bf16)
    d_ff_in = total_of(sent_back(row_blocks(d_ff_in)))
    ff_out = product_t(hidden, down_w).astype(bf16)
    ff_out = total_of(sent_back(row_blocks(ff_out)))
    result = whole_rows(shared((resid + ff_out).astype(bf16)), place)
    d_ff_w = jnp.concatenate(
        [outer_sum(ff_in, d_gate_up).astype(bf16), outer_sum(grad_out, hidden).astype(bf16)], axis=1
    )
    d_ff_w = lax.psum_scatter(d_ff_w, ("dp", "seq"), scatter_dimension=0, tiled=True).astype(f32)

    d_resid_norm, d_forward_gain = norm_back(resid, ff_scale, gain_forward, d_ff_in)
    d_resid = grad_out[:BLOCK].astype(f32) + d_resid_norm
    d_forget_bias = (
        jnp.sum(grad_new_own * (state_own - mixed_state), axis=0) * forget * (1.0 - forget)
    )
    d_mix_own = d_resid.astype(bf16)
    d_attn_own = product(d_mix_own, output_w).astype(bf16)
    d_attn_tok = jnp.concatenate(
        [d_attn_own[:, :256]]
        + [shifted(d_attn_own[:, 256 * k : 256 * (k + 1)], "mp", k) for k in (1, 2, 3)],
        axis=0,
    )
    d_mix_tok = jnp.concatenate(shared(d_mix_own), axis=0)
    d_mix_state = (grad_new * (1.0 - forget)).astype(bf16)
    d_attn_state = product(d_mix_state, own_output_w).astype(bf16)
    d_output_w = outer_sum(d_mix_tok, attn_tok) + outer_sum(d_mix_state, attn_state)

    d_query_state, d_key_more, d_value_more = attend_back(
        query_state, key_tok, value_tok, None, sums_state, split_heads(d_attn_state)
    )
    d_query_tok, d_key_all, d_value_all = attend_back(
        query_tok, key_all, value_all, mask, sums_tok, split_heads(d_attn_tok)
    )
    d_pair = jnp.concatenate([d_key_all, d_value_all], axis=1)
    back = passed_along(d_pair[:W].astype(bf16), "seq", -1).astype(f32)
    d_pair_tok = d_pair[W : 2 * W] + jnp.concatenate([d_key_more, d_value_more], axis=1) + back
    d_qkv = jnp.concatenate(
        [
            jnp.concatenate([d_query_tok, d_query_state], axis=0).astype(bf16),
            jnp.concatenate([d_pair_tok, d_pair[2 * W :]], axis=0).astype(bf16),
        ],
        axis=1,
    )
    d_rows = product_t(d_qkv, qkv_w).astype(bf16)
    d_rows = total_of(
        sent_back(
            [
                jnp.concatenate([a, b], axis=0)
                for a, b in zip(row_blocks(d_rows[:W]), row_blocks(d_rows[W:]))
            ]
        )
    )
    d_attn_w = jnp.concatenate(
        [outer_sum(normed_rows, d_qkv).astype(bf16), d_output_w.astype(bf16)], axis=1
    )
    d_attn_w = scatter_planes(d_attn_w, y, z, core)

    d_tok_norm, d_attention_gain = norm_back(tok_own, tok_scale[:BLOCK], gain_attn, d_rows[:BLOCK])
    d_state_norm, d_state_gain = norm_back(
        state_own, state_scale[:BLOCK], gain_state, d_rows[BLOCK:]
    )
    d_own = jnp.stack([d_resid + d_tok_norm, grad_new_own * forget + d_state_norm]).astype(bf16)
    d_vectors = sum_everywhere(
        jnp.stack([d_attention_gain, d_state_gain, d_forward_gain, d_forget_bias])
    )
    d_vectors = lax.dynamic_slice_in_dim(d_vectors, (y * 8 + seq) * 32, 32, 1)
    d_all = in_order(shared(d_own), place).astype(f32)
    d_tokens = d_all[:, 0].reshape(W, D)
    d_states = d_all[:, 1].reshape(NS, D)
    return (
        result[None],
        updated[None, None],
        d_tokens[None],
        d_states[None, None],
        d_attn_w[:, :256],
        d_attn_w[:, 256:512],
        d_attn_w[:, 512:768],
        d_attn_w[:, 768:].T,
        d_ff_w[:, :1024],
        d_ff_w[:, 1024:2048],
        d_ff_w[:, 2048:].T,
        d_vectors[0],
        d_vectors[1],
        d_vectors[2],
        d_vectors[3],
    )


def solution(mesh):
    plane = ("dp", "seq")
    placed = (
        P("dp", "seq", None),
        P("dp", "seq", None, None),
        P("dp", None),
        P(plane, "mp"),
        P(plane, "mp"),
        P(plane, "mp"),
        P("mp", plane),
        P(plane, "mp"),
        P(plane, "mp"),
        P("mp", plane),
        P(plane),
        P(plane),
        P(plane),
        P(plane),
        P("dp", "seq", None),
        P("dp", "seq", None, None),
    )
    return jax.shard_map(
        local,
        mesh=mesh,
        in_specs=placed,
        out_specs=(
            P("dp", "seq", None),
            P("dp", "seq", None, None),
            P("dp", "seq", None),
            P("dp", "seq", None, None),
            P(plane, "mp"),
            P(plane, "mp"),
            P(plane, "mp"),
            P("mp", plane),
            P(plane, "mp"),
            P(plane, "mp"),
            P("mp", plane),
            P(plane),
            P(plane),
            P(plane),
            P(plane),
        ),
        check_vma=False,
    )
```

```python
import functools

import jax
import jax.numpy as jnp
from jax import lax
from jax.experimental import pallas as pl
from jax.experimental.pallas import tpu as pltpu
from jax.sharding import PartitionSpec as P

D = 1024
HD = 128
W = 512
NS = 512
PARTS = 4
BLOCK = W // PARTS
QKV = 768
PACK = 1152
SHARD = 896
SCALE = HD ** (-0.5)


EPS = 1e-05
NEG = -1e30
BF16, F32 = jnp.bfloat16, jnp.float32


def passed_along(value, axis, steps):
    count = lax.axis_size(axis)
    leading, last = (max(0, -steps), min(count, count - steps))
    return lax.ppermute(value, axis, [(source, source + steps) for source in range(leading, last)])


def shifted(value, axis, steps):
    count = lax.axis_size(axis)
    return lax.ppermute(value, axis, [(i, (i + steps) % count) for i in range(count)])


def shifted_y(value, steps):
    return shifted(value, "dp", steps)


def shifted_z(value, steps):
    return shifted(value, "seq", 2 * steps)


def shifted_x(value, steps):
    return shifted(value, "mp", steps)


def other_core(value):
    return lax.ppermute(value, "seq", [(i, i ^ 1) for i in range(lax.axis_size("seq"))])


def sent_back(blocks):
    return [blocks[0]] + [shifted_x(blocks[k], -k) for k in (1, 2, 3)]


def sent_on(blocks):
    return [blocks[0]] + [shifted_x(blocks[k], k) for k in (1, 2, 3)]


def product(left, right):
    return jnp.dot(left, right, preferred_element_type=F32)


def product_t(left, right):
    return lax.dot_general(left, right, (((1,), (1,)), ((), ())), preferred_element_type=F32)


def outer_sum(left, right):
    return lax.dot_general(left, right, (((0,), (0,)), ((), ())), preferred_element_type=F32)


def inv_rms(values):
    return lax.rsqrt(jnp.mean(values * values, axis=-1, keepdims=True) + EPS)


def norm_back(values, scale, gain, grad):
    inner = grad * gain
    along = jnp.mean(inner * values, axis=-1, keepdims=True)
    return scale * inner - values * (scale * scale * scale) * along


def block_rows(place, k):
    return pl.ds(pl.multiple_of(((place + PARTS - k) & 3) * BLOCK, BLOCK), BLOCK)


def total_of(pieces):
    total = pieces[0][...].astype(F32)
    for piece in pieces[1:]:
        total = total + piece[...].astype(F32)
    return total


def after(value, *others):
    return lax.optimization_barrier((value, *others))[0]


class Part:
    def __init__(self, array, width, index):
        self.array, self.width, self.index = array, width, index

    def spec(self):
        return pl.BlockSpec((self.array.shape[0], self.width), lambda _: (0, self.index))


def whole(shape):
    return pl.BlockSpec(shape, lambda _: (0,) * len(shape))


def run(body, outs, args, scratch=(), limit=60):
    in_specs = [pl.BlockSpec(memory_space=pltpu.SMEM)]
    in_specs += [arg.spec() if isinstance(arg, Part) else whole(arg.shape) for arg in args[1:]]
    call = pl.pallas_call(
        body,
        out_shape=[jax.ShapeDtypeStruct(shape, kind) for shape, kind in outs],
        in_specs=in_specs,
        grid=(1,),
        out_specs=[whole(shape) for shape, _ in outs],
        scratch_shapes=[pltpu.VMEM(shape, kind) for shape, kind in scratch],
        compiler_params=pltpu.CompilerParams(vmem_limit_bytes=limit << 20),
        cost_estimate=pl.CostEstimate(flops=1, bytes_accessed=1, transcendentals=0),
        name=body.__name__.replace("_body", ""),
    )
    return list(call(*[arg.array if isinstance(arg, Part) else arg for arg in args]))


def project_body(info, tokens, states, *refs):
    mine, theirs, before = refs[:4], refs[4:8], refs[8:10]
    normed, query, pair_tok, pair_state, pair_prev, qkv_w, vectors, gains = refs[10:]
    y, z, core = info[1], info[2], info[3]
    for side, pieces in ((0, mine), (1, theirs)):
        for kz in range(4):
            for ky in range(4):
                shard = ((y + 4 - ky) & 3) * 8 + ((z + 4 - kz) & 3) * 2 + (core ^ side)
                rows = pl.ds(pl.multiple_of(shard * 32, 32), 32)
                qkv_w[rows, :] = pieces[kz][ky, :, :QKV]
                gains[rows, :] = pieces[kz][ky, :, QKV:]
    across = gains[...].astype(F32).T
    vectors[0:3, :] = across[0:3]
    vectors[3:4, :] = jax.nn.sigmoid(across[3:4])

    def normalized(values, lane):
        values = values.astype(F32)
        return (values * inv_rms(values) * vectors[lane : lane + 1, :]).astype(BF16)

    for part, (rows, pair) in enumerate(((tokens, pair_tok), (states, pair_state))):

        @pl.loop(0, 2)
        def _(b):
            here = pl.ds(pl.multiple_of(b * 256, 256), 256)
            there = pl.ds(pl.multiple_of(part * W + b * 256, 256), 256)
            normed[there, :] = normalized(rows[here, :], part)
            out = product(normed[there, :], qkv_w[...]).astype(BF16)
            query[there, :] = out[:, :256]
            pair[here, :] = out[:, 256:]

    for b, half in enumerate(before):
        here = pl.ds(pl.multiple_of(((info[0] + b) & 1) * 256, 256), 256)
        pair_prev[here, :] = product(normalized(half[...], 0), qkv_w[:, 256:]).astype(BF16)


def softmax_parts(scores):
    peak = functools.reduce(
        jnp.maximum, [jnp.max(part, axis=-1, keepdims=True) for part in scores]
    )
    grown = [jnp.exp(part - peak) for part in scores]
    total = functools.reduce(jnp.add, [jnp.sum(part, axis=-1, keepdims=True) for part in grown])
    inverse = 1.0 / total
    return [(part * inverse).astype(BF16) for part in grown], peak + jnp.log(total)


def state_fwd_body(info, query, pair_tok, attn, logsum):
    for head in range(2):
        lanes = pl.ds(head * HD, HD)
        key, value = pair_tok[:, lanes], pair_tok[:, pl.ds(256 + head * HD, HD)]

        @pl.loop(0, 2)
        def _(b):
            here = pl.ds(pl.multiple_of(b * 256, 256), 256)
            there = pl.ds(pl.multiple_of(W + b * 256, 256), 256)
            scores = product_t(query[there, lanes], key) * SCALE
            (probs,), total = softmax_parts([scores])
            attn[here, lanes] = product(probs, value).astype(BF16)
            logsum[here, lanes] = jnp.broadcast_to(total, (256, HD))


def documents(info, positions):
    count = jnp.zeros_like(positions)
    for index in range(4):
        count = count + (positions >= info[5 + index]).astype(jnp.int32)
    return count


def nearby_masks(info, first_row, rows):
    start = info[4] * W
    query_pos = start + first_row + lax.broadcasted_iota(jnp.int32, (rows, 1), 0)
    key_pos = start + lax.broadcasted_iota(jnp.int32, (1, W), 1)
    query_doc = documents(info, query_pos)
    prev = (key_pos >= W) & (documents(info, key_pos - W) == query_doc)
    own = (key_pos <= query_pos) & (documents(info, key_pos) == query_doc)
    return prev, own


def token_fwd_body(info, query, pair_prev, pair_tok, pair_state, attn, logsum):
    for head in range(2):
        lanes = pl.ds(head * HD, HD)
        far = pl.ds(256 + head * HD, HD)

        @pl.loop(0, 2)
        def _(b):
            here = pl.ds(pl.multiple_of(b * 256, 256), 256)
            prev, own = nearby_masks(info, b * 256, 256)
            rows = query[here, lanes]
            scores = [
                jnp.where(prev, product_t(rows, pair_prev[:, lanes]) * SCALE, NEG),
                jnp.where(own, product_t(rows, pair_tok[:, lanes]) * SCALE, NEG),
                product_t(rows, pair_state[:, lanes]) * SCALE,
            ]
            probs, total = softmax_parts(scores)
            out = (
                product(probs[0], pair_prev[:, far])
                + product(probs[1], pair_tok[:, far])
                + product(probs[2], pair_state[:, far])
            )
            attn[here, lanes] = out.astype(BF16)
            logsum[here, lanes] = jnp.broadcast_to(total, (256, HD))


def state_mix_body(info, states, grad_new, vectors, output_w, *refs):
    outs, updated, d_forget, attn = refs
    for k in range(4):
        attn[:, pl.ds(256 * k, 256)] = outs[(info[0] + 4 - k) & 3]
    forget = vectors[3:4, :]
    d_forget[...] = jnp.zeros_like(d_forget)

    @pl.loop(0, 4)
    def _(b):
        here = pl.ds(pl.multiple_of(b * 128, 128), 128)
        mixed = product_t(attn[here, :], output_w[...])
        given = states[here, :].astype(F32)
        updated[here, :] = (given * forget + mixed * (1.0 - forget)).astype(BF16)

        @pl.when(b == info[0])
        def _():
            along = jnp.sum(
                grad_new[here, :].astype(F32) * (given - mixed), axis=0, keepdims=True
            )
            d_forget[...] = along * forget * (1.0 - forget)


def forward_body(info, tokens, grad_out, vectors, late_w, *refs):
    outs = refs[:4]
    resid, ff_in, hidden, d_gate_up = refs[4:8]
    blocks = refs[8:12]
    d_ff_in, attn = refs[12:]
    for k in range(4):
        attn[:, pl.ds(256 * k, 256)] = outs[k][...]

    @pl.loop(0, 4)
    def _(b):
        here = pl.ds(pl.multiple_of(b * 128, 128), 128)
        values = tokens[here, :].astype(F32) + product_t(attn[here, :], late_w[:, 3 * D :])
        ff_in[here, :] = (values * inv_rms(values) * vectors[2:3, :]).astype(BF16)

        @pl.when(b == info[0])
        def _():
            resid[...] = values

    @pl.loop(0, 4, unroll=True)
    def _(c):
        at = [pl.ds(part * D + c * 256, 256) for part in range(3)]
        d_hidden = product(grad_out[...], late_w[:, at[2]])
        gate = product(ff_in[...], late_w[:, at[0]])
        up = product(ff_in[...], late_w[:, at[1]])
        sigma = jax.nn.sigmoid(gate)
        active = gate * sigma
        hidden[:, at[0]] = (active * up).astype(BF16)
        d_gate = d_hidden * up * sigma * (1.0 + gate * (1.0 - sigma))
        d_gate_up[:, at[0]] = d_gate.astype(BF16)
        d_gate_up[:, at[1]] = (d_hidden * active).astype(BF16)

    @pl.loop(0, 4, unroll=True)
    def _(c):
        at = pl.ds(pl.multiple_of(c * 256, 256), 256)
        d_ff_in[:, at] = product_t(d_gate_up[...], late_w[at, : 2 * D]).astype(BF16)

    for k in range(4):
        blocks[k][...] = d_ff_in[block_rows(info[0], k), :]


def forward_out_body(info, hidden, down_w, *blocks):
    for k in range(4):
        blocks[k][...] = product_t(hidden[block_rows(info[0], k), :], down_w[...]).astype(BF16)


def result_body(info, resid, d_mix, *refs):
    pieces, out = refs[:4], refs[4]
    out[:BLOCK, :] = d_mix[...]
    out[BLOCK:, :] = (resid[...] + total_of(pieces)).astype(BF16)


def collect_body(info, *refs):
    pieces, whole = refs[:4], refs[4]
    for k in range(4):
        whole[block_rows(info[0], k), :] = pieces[k][BLOCK:, :]


def resid_back_body(info, resid, grad_out, vectors, output_w, *refs):
    pieces = refs[:4]
    d_resid, d_mix, d_forward = refs[4:7]
    blocks = refs[7:]
    grad, values = total_of(pieces), resid[...]
    scale = inv_rms(values)
    d_forward[...] = jnp.sum(grad * values * scale, axis=0, keepdims=True)
    total = grad_out[block_rows(info[0], 0), :].astype(F32) + norm_back(
        values, scale, vectors[2:3, :], grad
    )
    d_resid[...] = total
    rounded = total.astype(BF16)
    d_mix[...] = rounded
    for k in range(4):
        at = pl.ds(256 * ((4 - k) % 4), 256)
        blocks[k][...] = product(rounded, output_w[:, at]).astype(BF16)


def part_back(query, turned_query, key, value, d_out, turned_d_out, logsum, center, mask):
    scores = product_t(query, key) * SCALE
    if mask is not None:
        scores = jnp.where(mask, scores, NEG)
    probs = jnp.exp(scores - logsum)
    d_probs = product_t(d_out, value)
    d_scores = (probs * (d_probs - center)).astype(BF16)
    d_query = product(d_scores, key) * SCALE
    d_key = product(turned_query, d_scores) * SCALE
    d_value = product(turned_d_out, probs.astype(BF16))
    return d_query, d_key.T, d_value.T


def turned(values):
    return values.astype(F32).T.astype(BF16)


def center_of(d_out, out):
    return jnp.sum(d_out.astype(F32) * out.astype(F32), axis=-1, keepdims=True)


def state_back_body(info, query, pair_tok, attn, logsum, grad_new, vectors, output_w, *refs):
    d_mix, d_query, d_pair, d_attn = refs
    keep = 1.0 - vectors[3:4, :]

    @pl.loop(0, 2)
    def _(b):
        here = pl.ds(pl.multiple_of(b * 256, 256), 256)
        rounded = (grad_new[here, :].astype(F32) * keep).astype(BF16)
        d_mix[here, :] = rounded
        d_attn[here, :] = product(rounded, output_w[...]).astype(BF16)

    for head in range(2):
        lanes = pl.ds(head * HD, HD)
        far = pl.ds(256 + head * HD, HD)
        rows, d_out = query[pl.ds(W, NS), lanes], d_attn[:, lanes]
        center = center_of(d_out, attn[:, lanes])
        total = logsum[:, pl.ds(head * HD, 1)]
        d_rows, d_key, d_value = part_back(
            rows, turned(rows), pair_tok[:, lanes], pair_tok[:, far], d_out, turned(d_out),
            total, center, None,
        )
        d_query[:, lanes] = d_rows.astype(BF16)
        d_pair[:, lanes] = d_key
        d_pair[:, far] = d_value


def prev_back_body(info, query, pair_prev, attn, logsum, *refs):
    pieces = refs[:4]
    d_pair, d_query, d_attn, centers = refs[4:]
    for k in range(4):
        d_attn[block_rows(info[0], k), :] = pieces[k][...]
    prev, _ = nearby_masks(info, 0, W)
    for head in range(2):
        lanes = pl.ds(head * HD, HD)
        far = pl.ds(256 + head * HD, HD)
        rows, d_out = query[pl.ds(0, W), lanes], d_attn[:, lanes]
        center = center_of(d_out, attn[:, lanes])
        centers[:, lanes] = jnp.broadcast_to(center, (W, HD))
        total = logsum[:, pl.ds(head * HD, 1)]
        d_rows, d_key, d_value = part_back(
            rows, turned(rows), pair_prev[:, lanes], pair_prev[:, far], d_out, turned(d_out),
            total, center, prev,
        )
        d_query[:, lanes] = d_rows
        d_pair[:, lanes] = d_key.astype(BF16)
        d_pair[:, far] = d_value.astype(BF16)


def token_back_body(
    info, query, pair_tok, pair_state, logsum, d_attn, centers, d_query_part, d_pair_more, *refs
):
    d_query, d_pair_tok, d_pair_state = refs
    _, own = nearby_masks(info, 0, W)
    for head in range(2):
        lanes = pl.ds(head * HD, HD)
        far = pl.ds(256 + head * HD, HD)
        rows, d_out = query[pl.ds(0, W), lanes], d_attn[:, lanes]
        rows_t, d_out_t = turned(rows), turned(d_out)
        total, center = logsum[:, pl.ds(head * HD, 1)], centers[:, pl.ds(head * HD, 1)]
        d_rows, d_key, d_value = part_back(
            rows, rows_t, pair_tok[:, lanes], pair_tok[:, far], d_out, d_out_t, total, center, own
        )
        d_pair_tok[:, lanes] = d_key + d_pair_more[:, lanes]
        d_pair_tok[:, far] = d_value + d_pair_more[:, far]
        more, d_key, d_value = part_back(
            rows, rows_t, pair_state[:, lanes], pair_state[:, far], d_out, d_out_t, total, center,
            None,
        )
        d_query[:, lanes] = (d_query_part[:, lanes] + d_rows + more).astype(BF16)
        d_pair_state[:, lanes] = d_key.astype(BF16)
        d_pair_state[:, far] = d_value.astype(BF16)


def rows_back(info, given, qkv_w, d_qkv, d_gain, blocks):
    d_gain[...] = jnp.zeros_like(d_gain)
    for k in range(4):
        rows = block_rows(info[0], k)
        grad = product_t(d_qkv[rows, :], qkv_w[...])
        values = given[rows, :].astype(F32)
        d_gain[...] += jnp.sum(grad * values * inv_rms(values), axis=0, keepdims=True)
        blocks[k][...] = grad.astype(BF16)


def state_rows_body(info, states, qkv_w, d_query, d_pair, d_qkv, d_gain, *blocks):
    d_qkv[:, :256] = d_query[...]
    d_qkv[:, 256:] = d_pair[...]
    rows_back(info, states, qkv_w, d_qkv, d_gain, blocks)


def token_rows_body(
    info, tokens, qkv_w, d_query, d_pair, d_pair_back, d_state, d_forward, d_forget, d_qkv, *refs
):
    blocks, d_gain = refs[:4], refs[4]
    d_qkv[:, :256] = d_query[...]
    d_qkv[:, 256:] = (d_pair[...] + d_pair_back[...].astype(F32)).astype(BF16)
    rows_back(info, tokens, qkv_w, d_qkv, d_gain, [block.at[pl.ds(0, BLOCK), :] for block in blocks])
    gains = jnp.concatenate(
        [d_gain[...], d_state[...], d_forward[...], d_forget[...], jnp.zeros((12, D), F32)], axis=0
    ).astype(BF16)
    for block in blocks:
        block[BLOCK:, :] = gains


def attn_grads_body(
    info, normed, d_qkv_tok, d_qkv_state, d_mix_state, attn_tok, attn_state, *refs
):
    d_mix_tok, keep, give, whole = refs[:4], refs[4], refs[5], refs[6]
    for k in range(4):
        whole[block_rows(info[0], k), :] = d_mix_tok[k][:BLOCK, :]
    first = info[3] == 0

    @pl.loop(0, 4)
    def _(c):
        at = pl.ds(pl.multiple_of(c * 256, 256), 256)
        groups = pl.ds(pl.multiple_of(c * 4, 4), 4)
        sums = (
            outer_sum(normed[:W, at], d_qkv_tok[...]) + outer_sum(normed[W:, at], d_qkv_state[...]),
            outer_sum(whole[:, at], attn_tok[...]) + outer_sum(d_mix_state[:, at], attn_state[...]),
        )
        for part, lanes in zip(sums, (pl.ds(0, QKV), pl.ds(QKV, 256))):
            split = part.astype(BF16).reshape(4, 2, 32, part.shape[1])
            even, odd = split[:, 0], split[:, 1]
            keep[groups, :, lanes] = jnp.where(first, even, odd)
            give[groups, :, lanes] = jnp.where(first, odd, even)


def scatter_z_body(info, keep, came, gains, *refs):
    pieces, rows, across = refs[:4], refs[4], refs[5]
    rows[...] = jnp.zeros_like(rows)
    rows[0:8, :] = gains[...]
    rows[8:16, :] = gains[...]
    across[...] = rows[...].T
    near = lax.broadcasted_iota(jnp.int32, (32, 128), 1) < 8
    for k in range(4):
        z = (info[2] + k) & 3
        for y in range(4):
            group = y * 4 + z
            pieces[k][y, :, :D] = (keep[group].astype(F32) + came[group].astype(F32)).astype(BF16)
            own = across[pl.ds(pl.multiple_of((group * 2 + info[3]) * 32, 32), 32), :]
            other = across[pl.ds(pl.multiple_of((group * 2 + 1 - info[3]) * 32, 32), 32), :]
            pieces[k][y, :, D:] = jnp.where(near, own, other).astype(BF16)


def scatter_y_body(info, *refs):
    pieces, outs = refs[:4], refs[4:]
    for k in range(4):
        y = (info[1] + k) & 3
        total = pieces[0][y].astype(F32)
        for piece in pieces[1:]:
            total = total + piece[y].astype(F32)
        outs[k][...] = total.astype(BF16)


def scatter_end_body(info, *refs):
    total = total_of(refs[:4])
    d_query, d_key, d_value, d_output, d_vectors = refs[4:]
    d_query[...] = total[:, :256]
    d_key[...] = total[:, 256:512]
    d_value[...] = total[:, 512:768]
    d_output[...] = total[:, 768:1024].T
    d_vectors[...] = total[:, 1024:]


def ends_body(info, tokens, states, grad_new, vectors, d_resid, *refs):
    from_states, from_tokens, d_own, gains = refs[:4], refs[4:8], refs[8], refs[9]
    rows = block_rows(info[0], 0)
    values = states[rows, :].astype(F32)
    d_own[BLOCK:, :] = (
        grad_new[rows, :].astype(F32) * vectors[3:4, :]
        + norm_back(values, inv_rms(values), vectors[1:2, :], total_of(from_states))
    ).astype(BF16)
    values = tokens[rows, :].astype(F32)
    grad = total_of([piece.at[pl.ds(0, BLOCK), :] for piece in from_tokens])
    d_own[:BLOCK, :] = (
        d_resid[...] + norm_back(values, inv_rms(values), vectors[0:1, :], grad)
    ).astype(BF16)
    gains[...] = total_of([piece.at[pl.ds(BLOCK, 16), :] for piece in from_tokens])[:8]


def widen_body(given, d_tokens, d_states):
    d_tokens[...] = given[:BLOCK, :].astype(F32)
    d_states[...] = given[BLOCK:, :].astype(F32)


def widened(given):
    return pl.pallas_call(
        widen_body,
        out_shape=[jax.ShapeDtypeStruct((W, D), F32)] * 2,
        grid=(PARTS,),
        in_specs=[pl.BlockSpec((2 * BLOCK, D), lambda b: (b, 0))],
        out_specs=[pl.BlockSpec((BLOCK, D), lambda b: (b, 0))] * 2,
        compiler_params=pltpu.CompilerParams(vmem_limit_bytes=60 << 20),
        name="widened",
    )(given)


def local(
    tokens,
    states,
    doc_lengths,
    w_query,
    w_key,
    w_value,
    w_output,
    w_gate,
    w_up,
    w_down,
    attention_gain,
    state_gain,
    forward_gain,
    forget_bias,
    d_output,
    d_new_states,
):
    place = lax.axis_index("mp")
    y = lax.axis_index("dp")
    seq = lax.axis_index("seq")
    info = jnp.concatenate(
        [jnp.stack([place, y, seq // 2, seq % 2, seq]), jnp.cumsum(doc_lengths[0])]
    ).astype(jnp.int32)
    tokens, states = tokens[0], states[0, 0]
    grad_out, grad_new = d_output[0], d_new_states[0, 0]

    gains = jnp.stack([attention_gain, state_gain, forward_gain, forget_bias], axis=1)
    gains = jnp.pad(gains, ((0, 0), (0, 124)))
    packed = jnp.concatenate([w_query, w_key, w_value, gains], axis=1)
    output_shard = after(w_output, packed).T
    packed = jnp.stack([packed] + [shifted_y(packed, k) for k in (1, 2, 3)])
    mine = [packed] + [shifted_z(packed, k) for k in (1, 2, 3)]
    theirs = [other_core(piece) for piece in mine]
    half = lax.dynamic_slice_in_dim(tokens, (place % 2) * 256, 256, 0)
    half = passed_along(half, "seq", 1)
    before = [half, lax.ppermute(half, "mp", [(0, 1), (1, 0), (2, 3), (3, 2)])]
    late_shard = jnp.concatenate(
        [w_gate, w_up, w_down.T] + sent_on([output_shard] * 4), axis=1
    )
    late_w = lax.all_gather(after(late_shard, half), ("dp", "seq"), axis=0, tiled=True)

    normed, query, pair_tok, pair_state, pair_prev, qkv_w, vectors = run(
        project_body,
        [
            ((2 * W, D), BF16), ((2 * W, 256), BF16), ((W, 512), BF16), ((W, 512), BF16),
            ((W, 512), BF16), ((D, QKV), BF16), ((8, D), F32),
        ],
        [info, tokens, states] + mine + theirs + before,
        [((D, 128), BF16)],
    )
    attn_tok, sums_tok = run(
        token_fwd_body, [((W, 256), BF16), ((W, 256), F32)],
        [info, query, pair_prev, pair_tok, pair_state],
    )
    attn_state, sums_state = run(
        state_fwd_body, [((NS, 256), BF16), ((NS, 256), F32)], [info, after(query, sums_tok), pair_tok],
    )
    outs_tok = sent_on([attn_tok] * 4)
    outs_state = lax.all_gather(after(attn_state, late_w[0]), "mp", axis=0)
    output_w, own_output_w = Part(late_w, D, 3), Part(late_w, 256, 12)
    d_mix_state, d_query_state, d_pair_more = run(
        state_back_body,
        [((NS, D), BF16), ((NS, 256), BF16), ((NS, 512), F32)],
        [info, query, pair_tok, attn_state, sums_state, grad_new, vectors, own_output_w],
        [((NS, 256), BF16)],
    )
    outs_tok[0] = after(outs_tok[0], d_query_state)
    resid, ff_in, hidden, d_gate_up, *blocks = run(
        forward_body,
        [((BLOCK, D), F32), ((W, D), BF16), ((W, D), BF16), ((W, 2 * D), BF16)]
        + [((BLOCK, D), BF16)] * 4,
        [info, tokens, grad_out, vectors, late_w] + outs_tok,
        [((W, D), BF16), ((W, D), BF16)],
    )
    pieces = sent_back(blocks)

    d_ff_w = jnp.concatenate(
        [outer_sum(ff_in, d_gate_up).astype(BF16), outer_sum(grad_out, hidden).astype(BF16)], axis=1
    )
    ff_outs = run(
        forward_out_body, [((BLOCK, D), BF16)] * 4, [info, hidden, Part(late_w, D, 2)],
    )
    pieces[0] = after(pieces[0], d_ff_w, ff_outs[0])
    d_ff_w = after(d_ff_w, ff_outs[0], *pieces[1:])
    ff_outs = sent_back([after(block, *pieces[1:]) for block in ff_outs])
    d_ff_w = lax.psum_scatter(d_ff_w, ("dp", "seq"), scatter_dimension=0, tiled=True).astype(F32)

    d_resid, d_mix_own, d_forward, *blocks = run(
        resid_back_body,
        [((BLOCK, D), F32), ((BLOCK, D), BF16), ((1, D), F32)] + [((BLOCK, 256), BF16)] * 4,
        [info, resid, grad_out, vectors, output_w] + pieces,
    )
    pieces = sent_on(blocks)
    (shared_rows,) = run(
        result_body, [((2 * BLOCK, D), BF16)], [info, resid, d_mix_own] + ff_outs
    )
    pieces[0] = after(pieces[0], shared_rows)
    shared_rows = sent_on([shared_rows] * 4)
    d_pair_prev, d_query_part, d_attn_tok, centers = run(
        prev_back_body,
        [((W, 512), BF16), ((W, 256), F32), ((W, 256), BF16), ((W, 256), F32)],
        [info, query, pair_prev, attn_tok, sums_tok] + pieces,
    )
    d_pair_back = passed_along(d_pair_prev, "seq", -1)
    d_query_tok, d_pair_tok, d_pair_state = run(
        token_back_body,
        [((W, 256), BF16), ((W, 512), F32), ((W, 512), BF16)],
        [
            info, query, pair_tok, pair_state, sums_tok, d_attn_tok, centers, d_query_part,
            d_pair_more,
        ],
    )
    d_qkv_state, d_state_gain, *blocks = run(
        state_rows_body,
        [((NS, QKV), BF16), ((1, D), F32)] + [((BLOCK, D), BF16)] * 4,
        [info, states, qkv_w, d_query_state, d_pair_state],
    )
    pieces_state = sent_back(blocks)
    updated, d_forget = run(
        state_mix_body,
        [((NS, D), BF16), ((1, D), F32)],
        [info, states, grad_new, vectors, Part(after(late_w, d_state_gain), D, 3), outs_state],
        [((NS, D), BF16)],
    )
    d_qkv_tok, *blocks = run(
        token_rows_body,
        [((W, QKV), BF16)] + [((BLOCK + 16, D), BF16)] * 4,
        [
            info, tokens, qkv_w, d_query_tok, d_pair_tok, after(d_pair_back, d_state_gain),
            d_state_gain, d_forward, d_forget,
        ],
        [((1, D), F32)],
    )
    pieces_tok = sent_back(blocks)

    keep, give = run(
        attn_grads_body,
        [((16, 32, D), BF16)] * 2,
        [info, normed, d_qkv_tok, d_qkv_state, d_mix_state, attn_tok, attn_state]
        + shared_rows,
        [((W, D), BF16)],
    )
    came = other_core(give)
    d_own, d_gains = run(
        ends_body,
        [((2 * BLOCK, D), BF16), ((8, D), F32)],
        [info, tokens, states, grad_new, vectors, d_resid, after(pieces_state[0], give)]
        + pieces_state[1:] + pieces_tok,
    )
    d_all = lax.all_gather(d_own, "mp", axis=0, tiled=True)
    shards = run(
        scatter_z_body, [((4, 32, PACK), BF16)] * 4, [info, keep, came, d_gains],
        [((128, D), F32), ((D, 128), F32)],
    )
    shards = [shards[0]] + [shifted_z(shards[k], k) for k in (1, 2, 3)]
    shards = run(scatter_y_body, [((32, PACK), BF16)] * 4, [info] + shards)
    shards = [shards[0]] + [shifted_y(shards[k], k) for k in (1, 2, 3)]
    d_query_w, d_key_w, d_value_w, d_output_w, d_vectors = run(
        scatter_end_body,
        [((32, 256), F32)] * 3 + [((256, 32), F32), ((32, 128), F32)],
        [info] + shards,
    )
    d_vectors = d_vectors[:, :4] + other_core(d_vectors)[:, 8:12]
    (result,) = run(
        collect_body, [((W, D), BF16)], [info, after(shared_rows[0], shards[0])] + shared_rows[1:]
    )
    d_all = after(d_all, d_ff_w, result, d_query_w)
    d_tokens, d_states = widened(d_all)
    return (
        result[None],
        updated[None, None],
        d_tokens[None],
        d_states[None, None],
        d_query_w,
        d_key_w,
        d_value_w,
        d_output_w,
        d_ff_w[:, :1024],
        d_ff_w[:, 1024:2048],
        d_ff_w[:, 2048:].T,
        d_vectors[:, 0],
        d_vectors[:, 1],
        d_vectors[:, 2],
        d_vectors[:, 3],
    )


def solution(mesh):
    plane = ("dp", "seq")
    placed = (
        P("dp", "seq", None),
        P("dp", "seq", None, None),
        P("dp", None),
        P(plane, "mp"),
        P(plane, "mp"),
        P(plane, "mp"),
        P("mp", plane),
        P(plane, "mp"),
        P(plane, "mp"),
        P("mp", plane),
        P(plane),
        P(plane),
        P(plane),
        P(plane),
        P("dp", "seq", None),
        P("dp", "seq", None, None),
    )
    return jax.shard_map(
        local,
        mesh=mesh,
        in_specs=placed,
        out_specs=(
            P("dp", "seq", None),
            P("dp", "seq", None, None),
            P("dp", "seq", None),
            P("dp", "seq", None, None),
            P(plane, "mp"),
            P(plane, "mp"),
            P(plane, "mp"),
            P("mp", plane),
            P(plane, "mp"),
            P(plane, "mp"),
            P("mp", plane),
            P(plane),
            P(plane),
            P(plane),
            P(plane),
        ),
        check_vma=False,
    )
```

```python
import functools

import jax
import jax.numpy as jnp
from jax import lax
from jax.experimental import pallas as pl
from jax.experimental.pallas import tpu as pltpu
from jax.sharding import Mesh
from jax.sharding import PartitionSpec as P

D = 1024
HD = 128
W = 512
NS = 512
PARTS = 4
BLOCK = W // PARTS
QKV = 768
PACK = 1152
SHARD = 896
SCALE = HD ** (-0.5)


EPS = 1e-05
NEG = -1e30
BF16, F32 = jnp.bfloat16, jnp.float32


SEQ = ("z", "core")
CHIPS = ("dp", "z")
PLANE = ("dp", "z", "core")


def passed_along(value, steps):
    count = lax.axis_size(SEQ)
    leading, last = (max(0, -steps), min(count, count - steps))
    return lax.ppermute(value, SEQ, [(source, source + steps) for source in range(leading, last)])


def shifted_x(value, steps):
    return lax.ppermute(value, "mp", [(i, (i + steps) % PARTS) for i in range(PARTS)])


def shifted(value, axis, steps):
    return lax.ppermute(value, axis, [(i, (i + steps) % 4) for i in range(4)])


def other_core(value):
    return lax.ppermute(value, "core", [(0, 1), (1, 0)])


def sent_back(blocks):
    return [blocks[0]] + [shifted_x(blocks[k], -k) for k in (1, 2, 3)]


def sent_on(blocks):
    return [blocks[0]] + [shifted_x(blocks[k], k) for k in (1, 2, 3)]


def product(left, right):
    return jnp.dot(left, right, preferred_element_type=F32)


def product_t(left, right):
    return lax.dot_general(left, right, (((1,), (1,)), ((), ())), preferred_element_type=F32)


def outer_sum(left, right):
    return lax.dot_general(left, right, (((0,), (0,)), ((), ())), preferred_element_type=F32)


def inv_rms(values):
    return lax.rsqrt(jnp.mean(values * values, axis=-1, keepdims=True) + EPS)


def norm_back(values, scale, gain, grad):
    inner = grad * gain
    along = jnp.mean(inner * values, axis=-1, keepdims=True)
    return scale * inner - values * (scale * scale * scale) * along


def block_rows(place, k):
    return pl.ds(pl.multiple_of(((place + PARTS - k) & 3) * BLOCK, BLOCK), BLOCK)


def total_of(pieces):
    total = pieces[0][...].astype(F32)
    for piece in pieces[1:]:
        total = total + piece[...].astype(F32)
    return total


def after(value, *others):
    return lax.optimization_barrier((value, *others))[0]


class Part:
    def __init__(self, array, width, index):
        self.array, self.shape = array, (array.shape[0], width)
        self.where = lambda ref, info: ref.at[:, pl.ds(index * width, width)]
        self.block = lambda _: (0, index)


class Rows:
    def __init__(self, array, start, size):
        self.array, self.shape = array, (size, array.shape[1])
        self.where = lambda ref, info: ref.at[pl.ds(start, size), :]
        self.block = lambda _: (start // size, 0)


class Source:
    def __init__(self, copy, ref):
        self.copy, self.ref = copy, ref
        copy.start()

    def ready(self):
        if self.copy is not None:
            self.copy.wait()
            self.copy = None
        return self.ref

    def __getitem__(self, index):
        return self.ready()[index]


class Target:
    def __init__(self, copy, ref):
        self.copy, self.ref, self.sent = copy, ref, False
        self.shape, self.dtype = ref.shape, ref.dtype

    def send(self):
        if not self.sent:
            self.copy.start()
            self.sent = True

    def __getitem__(self, index):
        return self.ref[index]

    def __setitem__(self, index, value):
        self.ref[index] = value


class Held:
    def __init__(self, ref):
        self.ref, self.shape, self.dtype = ref, ref.shape, ref.dtype

    def ready(self):
        return self.ref

    def send(self):
        pass

    def __getitem__(self, index):
        return self.ref[index]

    def __setitem__(self, index, value):
        self.ref[index] = value


def ready(*sources):
    for source in sources:
        source.ready()


def send(*targets):
    for target in targets:
        target.send()


def run(body, outs, args, scratch=(), limit=60):
    n_refs = len(args) - 1 + len(outs)

    def kernel(info, *refs):
        body(info, *[Held(ref) for ref in refs[:n_refs]], *refs[n_refs:])

    def spec(arg):
        if hasattr(arg, "block"):
            return pl.BlockSpec(arg.shape, arg.block)
        return pl.BlockSpec(arg.shape, lambda _: (0,) * len(arg.shape))

    call = pl.pallas_call(
        kernel,
        out_shape=[jax.ShapeDtypeStruct(shape, kind) for shape, kind in outs],
        grid=(1,),
        in_specs=[pl.BlockSpec(memory_space=pltpu.SMEM)] + [spec(arg) for arg in args[1:]],
        out_specs=[spec(jax.ShapeDtypeStruct(shape, kind)) for shape, kind in outs],
        scratch_shapes=[pltpu.VMEM(shape, kind) for shape, kind in scratch],
        compiler_params=pltpu.CompilerParams(vmem_limit_bytes=limit << 20),
        cost_estimate=pl.CostEstimate(flops=1, bytes_accessed=1, transcendentals=0),
        name=body.__name__.replace("_body", ""),
    )
    return list(call(*[arg.array if hasattr(arg, "block") else arg for arg in args]))


def run_early(body, outs, args, scratch=(), limit=60):
    n_in, n_out = len(args) - 1, len(outs)

    def kernel(info, *refs):
        given, results = refs[:n_in], refs[n_in : n_in + n_out]
        held = refs[n_in + n_out : 2 * (n_in + n_out)]
        extra, (in_sems, out_sems) = refs[2 * (n_in + n_out) : -2], refs[-2:]
        sources = []
        for index, (arg, ref) in enumerate(zip(args[1:], given)):
            where = arg.where(ref, info) if hasattr(arg, "where") else ref
            copy = pltpu.make_async_copy(where, held[index], in_sems.at[index])
            sources.append(Source(copy, held[index]))
        targets = []
        for index, ref in enumerate(results):
            copy = pltpu.make_async_copy(held[n_in + index], ref, out_sems.at[index])
            targets.append(Target(copy, held[n_in + index]))
        body(info, *sources, *targets, *extra)
        ready(*sources)
        send(*targets)
        for target in targets:
            target.copy.wait()

    arrays = [arg.array if hasattr(arg, "where") else arg for arg in args]
    buffers = [pltpu.VMEM(arg.shape, array.dtype) for arg, array in zip(args[1:], arrays[1:])]
    buffers += [pltpu.VMEM(shape, kind) for shape, kind in outs]
    call = pl.pallas_call(
        kernel,
        out_shape=[jax.ShapeDtypeStruct(shape, kind) for shape, kind in outs],
        in_specs=[pl.BlockSpec(memory_space=pltpu.SMEM)] + [pl.BlockSpec(memory_space=pl.ANY)] * n_in,
        out_specs=[pl.BlockSpec(memory_space=pl.ANY)] * n_out,
        scratch_shapes=buffers
        + [pltpu.VMEM(shape, kind) for shape, kind in scratch]
        + [pltpu.SemaphoreType.DMA((n_in,)), pltpu.SemaphoreType.DMA((n_out,))],
        compiler_params=pltpu.CompilerParams(vmem_limit_bytes=limit << 20),
        cost_estimate=pl.CostEstimate(flops=1, bytes_accessed=1, transcendentals=0),
        name=body.__name__.replace("_body", ""),
    )
    return list(call(*arrays))


def softmax_parts(scores):
    peak = functools.reduce(
        jnp.maximum, [jnp.max(part, axis=-1, keepdims=True) for part in scores]
    )
    grown = [jnp.exp(part - peak) for part in scores]
    total = functools.reduce(jnp.add, [jnp.sum(part, axis=-1, keepdims=True) for part in grown])
    inverse = 1.0 / total
    return [(part * inverse).astype(BF16) for part in grown], peak + jnp.log(total)


def state_fwd_body(info, query, pair_tok, attn, logsum):
    ready(query, pair_tok)
    for head in range(2):
        lanes = pl.ds(head * HD, HD)
        key, value = pair_tok[:, lanes], pair_tok[:, pl.ds(256 + head * HD, HD)]

        @pl.loop(0, 2)
        def _(b):
            here = pl.ds(pl.multiple_of(b * 256, 256), 256)
            scores = product_t(query[here, lanes], key) * SCALE
            (probs,), total = softmax_parts([scores])
            attn[here, lanes] = product(probs, value).astype(BF16)
            logsum[here, lanes] = jnp.broadcast_to(total, (256, HD))


def documents(info, positions):
    count, end = jnp.zeros_like(positions), 0
    for index in range(4):
        end = end + info[5 + index]
        count = count + (positions >= end).astype(jnp.int32)
    return count


def nearby_masks(info, first_row, rows):
    start = info[4] * W
    query_pos = start + first_row + lax.broadcasted_iota(jnp.int32, (rows, 1), 0)
    key_pos = start + lax.broadcasted_iota(jnp.int32, (1, W), 1)
    query_doc = documents(info, query_pos)
    prev = (key_pos >= W) & (documents(info, key_pos - W) == query_doc)
    own = (key_pos <= query_pos) & (documents(info, key_pos) == query_doc)
    return prev, own


def attend_body(info, *refs):
    mine, theirs, before, tokens, states = refs[:4], refs[4:8], refs[8:10], refs[10], refs[11]
    normed, query, pair_tok, pair_state, pair_prev, qkv_w, vectors = refs[12:19]
    attn, logsum, gains = refs[19:]
    y, z, core = info[1], info[2], info[3]
    for kz in range(4):
        for side, pieces in ((0, mine), (1, theirs)):
            for ky in range(4):
                shard = ((y + 4 - ky) & 3) * 8 + ((z + 4 - kz) & 3) * 2 + (core ^ side)
                rows = pl.ds(pl.multiple_of(shard * 32, 32), 32)
                qkv_w[rows, :] = pieces[kz][ky, :, :QKV]
                gains[rows, :] = pieces[kz][ky, :, QKV:]
    qkv_w.send()
    across = gains[...].astype(F32).T
    vectors[0:3, :] = across[0:3]
    vectors[3:4, :] = jax.nn.sigmoid(across[3:4])
    vectors[4:8, :] = jnp.zeros((4, D), F32)
    vectors.send()

    def normalized(values, lane):
        values = values.astype(F32)
        return (values * inv_rms(values) * vectors[lane : lane + 1, :]).astype(BF16)

    for part, (rows, pair) in enumerate(((tokens, pair_tok), (states, pair_state))):
        ready(rows)

        @pl.loop(0, 2)
        def _(b):
            here = pl.ds(pl.multiple_of(b * 256, 256), 256)
            there = pl.ds(pl.multiple_of(part * W + b * 256, 256), 256)
            normed[there, :] = normalized(rows[here, :], part)
            out = product(normed[there, :], qkv_w[...]).astype(BF16)
            query[there, :] = out[:, :256]
            pair[here, :] = out[:, 256:]

        pair.send()
    send(normed, query)
    for b, half in enumerate(before):
        here = pl.ds(pl.multiple_of(((info[0] + b) & 1) * 256, 256), 256)
        pair_prev[here, :] = product(normalized(half[...], 0), qkv_w[:, 256:]).astype(BF16)
    pair_prev.send()

    for head in range(2):
        lanes = pl.ds(head * HD, HD)
        far = pl.ds(256 + head * HD, HD)

        @pl.loop(0, 2)
        def _(b):
            here = pl.ds(pl.multiple_of(b * 256, 256), 256)
            prev, own = nearby_masks(info, b * 256, 256)
            rows = query[here, lanes]
            scores = [
                jnp.where(prev, product_t(rows, pair_prev[:, lanes]) * SCALE, NEG),
                jnp.where(own, product_t(rows, pair_tok[:, lanes]) * SCALE, NEG),
                product_t(rows, pair_state[:, lanes]) * SCALE,
            ]
            probs, total = softmax_parts(scores)
            out = (
                product(probs[0], pair_prev[:, far])
                + product(probs[1], pair_tok[:, far])
                + product(probs[2], pair_state[:, far])
            )
            attn[here, lanes] = out.astype(BF16)
            logsum[here, lanes] = jnp.broadcast_to(total, (256, HD))


def state_mix_body(info, outs, output_w, states, vectors, updated, attn):
    ready(outs, output_w, states, vectors)
    for k in range(4):
        attn[:, pl.ds(256 * k, 256)] = outs[(info[0] + 4 - k) & 3]
    forget = vectors[3:4, :]

    @pl.loop(0, 2)
    def _(b):
        here = pl.ds(pl.multiple_of(b * 256, 256), 256)
        mixed = product_t(attn[here, :], output_w[...])
        given = states[here, :].astype(F32)
        updated[here, :] = (given * forget + mixed * (1.0 - forget)).astype(BF16)


def forward_body(info, *refs):
    outs = refs[:4]
    tokens, vectors, output_w, down_w, grad_out, gate_w, up_w = refs[4:11]
    resid, ff_in, hidden, d_gate_up = refs[11:15]
    blocks = refs[15:19]
    d_ff_in, attn, values = refs[19:]
    for k in range(4):
        attn[:, pl.ds(256 * k, 256)] = outs[k][...]
    ready(tokens, vectors, output_w)
    for c in range(4):
        at = pl.ds(c * 256, 256)
        values[:, at] = tokens[:, at].astype(F32) + product_t(attn[...], output_w[at, :])

    @pl.loop(0, 4)
    def _(b):
        here = pl.ds(pl.multiple_of(b * 128, 128), 128)
        rows = values[here, :]
        ff_in[here, :] = (rows * inv_rms(rows) * vectors[2:3, :]).astype(BF16)

    ff_in.send()
    resid[...] = values[block_rows(info[0], 0), :]
    resid.send()
    for c in range(4):
        at, beyond = pl.ds(c * 256, 256), pl.ds(D + c * 256, 256)
        d_hidden = product(grad_out[...], down_w[:, at])
        gate = product(ff_in[...], gate_w[:, at])
        up = product(ff_in[...], up_w[:, at])
        sigma = jax.nn.sigmoid(gate)
        active = gate * sigma
        hidden[:, at] = (active * up).astype(BF16)
        d_gate = d_hidden * up * sigma * (1.0 + gate * (1.0 - sigma))
        d_gate_up[:, at] = d_gate.astype(BF16)
        d_gate_up[:, beyond] = (d_hidden * active).astype(BF16)
    send(hidden, d_gate_up)
    for c in range(4):
        at = pl.ds(c * 256, 256)
        d_ff_in[:, at] = (
            product_t(d_gate_up[:, :D], gate_w[at, :]) + product_t(d_gate_up[:, D:], up_w[at, :])
        ).astype(BF16)
    for k in range(4):
        blocks[k][...] = d_ff_in[block_rows(info[0], k), :]
        blocks[k].send()


def forward_out_body(info, hidden, down_w, d_mix, *refs):
    shared, out = refs[:4], refs[4]
    ready(hidden, down_w)
    for c in range(4):
        at = pl.ds(c * 256, 256)
        out[:, at] = product_t(hidden[...], down_w[at, :]).astype(BF16)
    for k in range(4):
        shared[k][:BLOCK, :] = out[block_rows(info[0], k), :]
        shared[k][BLOCK:, :] = d_mix[...]


def resid_back_body(info, *refs):
    pieces, resid, vectors, grad_out, output_w = refs[:4], refs[4], refs[5], refs[6], refs[7]
    d_resid, d_forward, d_mix = refs[8:11]
    blocks = refs[11:]
    grad, values = total_of(pieces), resid[...]
    scale = inv_rms(values)
    total = grad_out[block_rows(info[0], 0), :].astype(F32) + norm_back(values, scale, vectors[2:3, :], grad)
    rounded = total.astype(BF16)
    for k in range(4):
        at = pl.ds(256 * ((4 - k) % 4), 256)
        blocks[k][...] = product(rounded, output_w[:, at]).astype(BF16)
    d_mix[...] = rounded
    d_resid[...] = total
    d_forward[...] = jnp.sum(grad * values * scale, axis=0, keepdims=True)


def part_back(query, turned_query, key, value, d_out, turned_d_out, logsum, center, mask):
    scores = product_t(query, key) * SCALE
    if mask is not None:
        scores = jnp.where(mask, scores, NEG)
    probs = jnp.exp(scores - logsum)
    d_probs = product_t(d_out, value)
    d_scores = (probs * (d_probs - center)).astype(BF16)
    d_query = product(d_scores, key) * SCALE
    d_key = product(turned_query, d_scores) * SCALE
    d_value = product(turned_d_out, probs.astype(BF16))
    return d_query, d_key.T, d_value.T


def turned(values):
    return values.astype(F32).T.astype(BF16)


def center_of(d_out, out):
    return jnp.sum(d_out.astype(F32) * out.astype(F32), axis=-1, keepdims=True)


def state_back_body(
    info, output_w, vectors, grad_new, states, attn, query, pair_tok, logsum, *refs
):
    d_mix, d_query, d_pair, d_forget, d_attn = refs
    ready(output_w, vectors, grad_new, attn)
    forget = vectors[3:4, :]
    own = block_rows(info[0], 0)
    d_forget[...] = jnp.sum(
        grad_new[own, :].astype(F32) * states[own, :].astype(F32), axis=0, keepdims=True
    )

    @pl.loop(0, 2)
    def _(b):
        here = pl.ds(pl.multiple_of(b * 256, 256), 256)
        grad = grad_new[here, :].astype(F32)
        rounded = (grad * (1.0 - forget)).astype(BF16)
        d_mix[here, :] = rounded
        d_attn[here, :] = product(rounded, output_w[...]).astype(BF16)
        mixed = product_t(attn[here, :], output_w[...])
        d_forget[...] -= jnp.sum(grad * mixed, axis=0, keepdims=True)

    d_mix.send()
    d_forget[...] *= forget * (1.0 - forget)
    for head in range(2):
        lanes = pl.ds(head * HD, HD)
        far = pl.ds(256 + head * HD, HD)
        rows, d_out = query[:, lanes], d_attn[:, lanes]
        center = center_of(d_out, attn[:, lanes])
        total = logsum[:, pl.ds(head * HD, 1)]
        d_rows, d_key, d_value = part_back(
            rows, turned(rows), pair_tok[:, lanes], pair_tok[:, far], d_out, turned(d_out),
            total, center, None,
        )
        d_query[:, lanes] = d_rows.astype(BF16)
        d_pair[:, lanes] = d_key
        d_pair[:, far] = d_value


def prev_back_body(info, *refs):
    pieces, query, pair_prev, attn, logsum = refs[:4], refs[4], refs[5], refs[6], refs[7]
    d_pair, d_query, d_attn = refs[8:]
    for k in range(4):
        d_attn[block_rows(info[0], k), :] = pieces[k][...]
    d_attn.send()
    prev, _ = nearby_masks(info, 0, W)
    for head in range(2):
        lanes = pl.ds(head * HD, HD)
        far = pl.ds(256 + head * HD, HD)
        rows, d_out = query[:, lanes], d_attn[:, lanes]
        center = center_of(d_out, attn[:, lanes])
        total = logsum[:, pl.ds(head * HD, 1)]
        d_rows, d_key, d_value = part_back(
            rows, turned(rows), pair_prev[:, lanes], pair_prev[:, far], d_out, turned(d_out),
            total, center, prev,
        )
        d_query[:, lanes] = d_rows
        d_pair[:, lanes] = d_key.astype(BF16)
        d_pair[:, far] = d_value.astype(BF16)


def rows_back(info, given, qkv_w, d_qkv, d_gain, blocks):
    d_gain[...] = jnp.zeros(d_gain.shape, F32)
    for k in range(4):
        rows = block_rows(info[0], k)
        grad = product_t(d_qkv[rows, :], qkv_w[...])
        values = given[rows, :].astype(F32)
        d_gain[...] += jnp.sum(grad * values * inv_rms(values), axis=0, keepdims=True)
        blocks[k][...] = grad.astype(BF16)
        blocks[k].send()


def own_back_body(
    info, query, pair_state, d_attn, attn, logsum, pair_tok, d_query_part, d_pair_more,
    d_query_state, qkv_w, states, *refs,
):
    d_query, d_pair_tok, d_qkv, d_gain = refs[:4]
    blocks = refs[4:]
    _, own = nearby_masks(info, 0, W)
    for head in range(2):
        lanes = pl.ds(head * HD, HD)
        far = pl.ds(256 + head * HD, HD)
        rows, d_out = query[:, lanes], d_attn[:, lanes]
        rows_t, d_out_t = turned(rows), turned(d_out)
        center = center_of(d_out, attn[:, lanes])
        total = logsum[:, pl.ds(head * HD, 1)]
        more, d_key, d_value = part_back(
            rows, rows_t, pair_state[:, lanes], pair_state[:, far], d_out, d_out_t, total, center,
            None,
        )
        d_qkv[:, pl.ds(256 + head * HD, HD)] = d_key.astype(BF16)
        d_qkv[:, pl.ds(512 + head * HD, HD)] = d_value.astype(BF16)
        d_rows, d_key, d_value = part_back(
            rows, rows_t, pair_tok[:, lanes], pair_tok[:, far], d_out, d_out_t, total, center, own
        )
        d_pair_tok[:, lanes] = d_key + d_pair_more[:, lanes]
        d_pair_tok[:, far] = d_value + d_pair_more[:, far]
        d_query[:, lanes] = (d_query_part[:, lanes] + d_rows + more).astype(BF16)
    send(d_pair_tok, d_query)
    d_qkv[:, :256] = d_query_state[...]
    d_qkv.send()

    rows_back(info, states, qkv_w, d_qkv, d_gain, blocks)


def token_rows_body(
    info, d_query, d_pair, d_pair_back, qkv_w, tokens, d_state, d_forward, d_forget, d_qkv, *refs
):
    blocks, d_gain = refs[:4], refs[4]
    d_qkv[:, :256] = d_query[...]
    d_qkv[:, 256:] = (d_pair[...] + d_pair_back[...].astype(F32)).astype(BF16)
    tops = [Held(block.ref.at[pl.ds(0, BLOCK), :]) for block in blocks]
    rows_back(info, tokens, qkv_w, d_qkv, d_gain, tops)
    gains = jnp.concatenate(
        [d_gain[...], d_state[...], d_forward[...], d_forget[...], jnp.zeros((12, D), F32)], axis=0
    ).astype(BF16)
    for block in blocks:
        block[BLOCK:, :] = gains


def attn_grads_body(
    info, normed, d_qkv_tok, d_qkv_state, d_mix_state, attn_tok, attn_state, *refs
):
    shared, keep, give, whole = refs[:4], refs[4], refs[5], refs[6]
    for k in range(4):
        whole[block_rows(info[0], 4 - k), :] = shared[k][BLOCK:, :]
    first = info[3] == 0
    ready(normed, d_qkv_tok, d_qkv_state, d_mix_state, attn_tok, attn_state)

    @pl.loop(0, 4)
    def _(c):
        at = pl.ds(pl.multiple_of(c * 256, 256), 256)
        groups = pl.ds(pl.multiple_of(c * 4, 4), 4)
        sums = (
            outer_sum(normed[:W, at], d_qkv_tok[...]) + outer_sum(normed[W:, at], d_qkv_state[...]),
            outer_sum(whole[:, at], attn_tok[...]) + outer_sum(d_mix_state[:, at], attn_state[...]),
        )
        for part, lanes in zip(sums, (pl.ds(0, QKV), pl.ds(QKV, 256))):
            split = part.astype(BF16).reshape(4, 2, 32, part.shape[1])
            even, odd = split[:, 0], split[:, 1]
            keep[groups, :, lanes] = jnp.where(first, even, odd)
            give[groups, :, lanes] = jnp.where(first, odd, even)


def scatter_z_body(info, keep, came, gains, *refs):
    pieces, rows, across = refs[:4], refs[4], refs[5]
    rows[...] = jnp.zeros_like(rows)
    rows[0:8, :] = gains[...]
    rows[8:16, :] = gains[...]
    across[...] = rows[...].T
    near = lax.broadcasted_iota(jnp.int32, (32, 128), 1) < 8
    for k in range(4):
        z = (info[2] + k) & 3
        for y in range(4):
            group = y * 4 + z
            pieces[k][y, :, :D] = (keep[group].astype(F32) + came[group].astype(F32)).astype(BF16)
            own = across[pl.ds(pl.multiple_of((group * 2 + info[3]) * 32, 32), 32), :]
            other = across[pl.ds(pl.multiple_of((group * 2 + 1 - info[3]) * 32, 32), 32), :]
            pieces[k][y, :, D:] = jnp.where(near, own, other).astype(BF16)
        pieces[k].send()


def scatter_y_body(info, *refs):
    pieces, outs = refs[:4], refs[4:]
    for k in range(4):
        y = (info[1] + k) & 3
        total = pieces[0][y].astype(F32)
        for piece in pieces[1:]:
            total = total + piece[y].astype(F32)
        outs[k][...] = total.astype(BF16)


def scatter_end_body(info, *refs):
    total = total_of(refs[:4])
    d_query, d_key, d_value, d_output, d_vectors = refs[4:]
    d_query[...] = total[:, :256]
    d_key[...] = total[:, 256:512]
    d_value[...] = total[:, 512:768]
    d_output[...] = total[:, 768:1024]
    d_vectors[...] = total[:, 1024:].T[:16]


def ends_body(info, *refs):
    from_states, shared, resid, states, grad_new, vectors, tokens, d_resid, from_tokens = (
        refs[:4], refs[4:8], refs[8], refs[9], refs[10], refs[11], refs[12], refs[13], refs[14:18],
    )
    d_own, result, gains = refs[18:]
    values = states[...].astype(F32)
    d_own[BLOCK:, :] = (
        grad_new[...].astype(F32) * vectors[3:4, :]
        + norm_back(values, inv_rms(values), vectors[1:2, :], total_of(from_states))
    ).astype(BF16)
    values = tokens[...].astype(F32)
    total = total_of(from_tokens)
    d_own[:BLOCK, :] = (
        d_resid[...] + norm_back(values, inv_rms(values), vectors[0:1, :], total[:BLOCK])
    ).astype(BF16)
    gains[...] = total[BLOCK : BLOCK + 8]
    result[...] = (resid[...] + total_of(shared)).astype(BF16)


def collect_body(info, own, left, right, far_tok, far_state, d_tokens, d_states):
    for k, piece in ((0, own), (1, left), (3, right)):
        rows = block_rows(info[0], k)
        d_tokens[rows, :] = piece[:BLOCK, :].astype(F32)
        d_states[rows, :] = piece[BLOCK:, :].astype(F32)
    rows = block_rows(info[0], 2)
    d_tokens[rows, :] = far_tok[...].astype(F32)
    d_states[rows, :] = far_state[...].astype(F32)


def local(
    tokens,
    states,
    doc_lengths,
    w_query,
    w_key,
    w_value,
    w_output,
    w_gate,
    w_up,
    w_down,
    attention_gain,
    state_gain,
    forward_gain,
    forget_bias,
    d_output,
    d_new_states,
):
    place = lax.axis_index("mp")
    y = lax.axis_index("dp")
    z, core = lax.axis_index("z"), lax.axis_index("core")
    info = jnp.concatenate(
        [jnp.stack([place, y, z, core, 2 * z + core]), doc_lengths[0]]
    ).astype(jnp.int32)
    tokens, states = tokens[0], states[0, 0]
    grad_out, grad_new = d_output[0], d_new_states[0, 0]
    gains = jnp.stack([attention_gain, state_gain, forward_gain, forget_bias], axis=1)
    gains = jnp.pad(gains, ((0, 0), (0, 124)))
    packed = jnp.concatenate([w_query, w_key, w_value, gains], axis=1)
    output_shard = w_output.T
    late_shard = jnp.concatenate(
        [w_gate, w_up, w_down.T] + sent_on([output_shard] * 4), axis=1
    )
    late_w = lax.all_gather(late_shard, PLANE, axis=0, tiled=True)
    half = lax.dynamic_slice_in_dim(tokens, (place % 2) * 256, 256, 0)
    half = passed_along(half, 1)
    before = [half, lax.ppermute(half, "mp", [(0, 1), (1, 0), (2, 3), (3, 2)])]
    packed = jnp.stack([after(packed, half)] + [shifted(packed, "dp", k) for k in (1, 2, 3)])
    mine = [packed] + [shifted(packed, "z", k) for k in (1, 2, 3)]
    theirs = [other_core(piece) for piece in mine]

    normed, query, pair_tok, pair_state, pair_prev, qkv_w, vectors, attn_tok, sums_tok = run_early(
        attend_body,
        [
            ((2 * W, D), BF16), ((2 * W, 256), BF16), ((W, 512), BF16), ((W, 512), BF16),
            ((W, 512), BF16), ((D, QKV), BF16), ((8, D), F32), ((W, 256), BF16), ((W, 256), F32),
        ],
        [info] + mine + theirs + before + [tokens, states],
        [((D, 128), BF16)],
    )
    query_tok, query_state = Rows(query, 0, W), Rows(query, W, NS)
    attn_state, sums_state = run(
        state_fwd_body, [((NS, 256), BF16), ((NS, 256), F32)],
        [info, query_state, pair_tok],
    )
    outs_tok = sent_on([attn_tok] * 4)
    outs_state = lax.all_gather(after(attn_state, late_w[0]), "mp", axis=0)
    output_w, own_output_w = Part(late_w, D, 3), Part(late_w, 256, 12)
    down_w = Part(late_w, D, 2)
    d_mix_state, d_query_state, d_pair_more, d_forget = run(
        state_back_body,
        [((NS, D), BF16), ((NS, 256), BF16), ((NS, 512), F32), ((1, D), F32)],
        [
            info, own_output_w, vectors, grad_new, states, attn_state, query_state, pair_tok,
            sums_state,
        ],
        [((NS, 256), BF16)],
    )
    outs_tok[0] = after(outs_tok[0], d_query_state)
    resid, ff_in, hidden, d_gate_up, *blocks = run_early(
        forward_body,
        [((BLOCK, D), F32), ((W, D), BF16), ((W, D), BF16), ((W, 2 * D), BF16)]
        + [((BLOCK, D), BF16)] * 4,
        [info] + outs_tok
        + [tokens, vectors, output_w, down_w, grad_out, Part(late_w, D, 0), Part(late_w, D, 1)],
        [((W, D), BF16), ((W, D), BF16), ((W, D), F32)],
    )
    pieces = sent_back(blocks)

    d_ff_w = jnp.concatenate(
        [outer_sum(ff_in, d_gate_up).astype(BF16), outer_sum(grad_out, hidden).astype(BF16)], axis=1
    )
    pieces[0] = after(pieces[0], d_ff_w)
    d_ff_w = after(d_ff_w, *pieces[1:])
    d_ff_w = lax.psum_scatter(d_ff_w, PLANE, scatter_dimension=0, tiled=True).astype(F32)

    d_resid, d_forward, d_mix_own, *blocks = run(
        resid_back_body,
        [((BLOCK, D), F32), ((1, D), F32), ((BLOCK, D), BF16)] + [((BLOCK, 256), BF16)] * 4,
        [info] + pieces + [resid, vectors, grad_out, output_w],
    )
    pieces = sent_on(blocks)
    blocks = run(
        forward_out_body, [((2 * BLOCK, D), BF16)] * 4, [info, hidden, down_w, d_mix_own],
        [((W, D), BF16)],
    )
    pieces[0] = after(pieces[0], blocks[0])
    shared = sent_back([after(block, *pieces[1:]) for block in blocks])

    d_pair_prev, d_query_part, d_attn_tok = run(
        prev_back_body,
        [((W, 512), BF16), ((W, 256), F32), ((W, 256), BF16)],
        [info] + pieces + [query_tok, pair_prev, attn_tok, sums_tok],
    )
    d_pair_back = passed_along(d_pair_prev, -1)
    d_query_tok, d_pair_tok, d_qkv_state, d_state_gain, *blocks = run_early(
        own_back_body,
        [((W, 256), BF16), ((W, 512), F32), ((NS, QKV), BF16), ((1, D), F32)]
        + [((BLOCK, D), BF16)] * 4,
        [
            info, query_tok, pair_state, d_attn_tok, attn_tok, sums_tok, pair_tok, d_query_part,
            d_pair_more, d_query_state, qkv_w, states,
        ],
    )
    pieces_state = sent_back(blocks)
    d_pair_back = after(d_pair_back, d_state_gain, *shared[1:])
    d_qkv_tok, *blocks = run(
        token_rows_body,
        [((W, QKV), BF16)] + [((BLOCK + 16, D), BF16)] * 4,
        [
            info, d_query_tok, d_pair_tok, d_pair_back, qkv_w, tokens, d_state_gain, d_forward,
            d_forget,
        ],
        [((1, D), F32)],
    )
    pieces_tok = sent_back([after(block, *pieces_state[1:]) for block in blocks])

    keep, give = run(
        attn_grads_body,
        [((16, 32, D), BF16)] * 2,
        [
            info, normed, d_qkv_tok, d_qkv_state, d_mix_state, attn_tok,
            attn_state,
        ]
        + shared,
        [((W, D), BF16)],
    )
    own_tokens, own_states, own_grad_new = [
        lax.dynamic_slice_in_dim(rows, place * BLOCK, BLOCK, 0)
        for rows in (after(tokens, give), states, grad_new)
    ]
    d_own, result, d_gains = run(
        ends_body,
        [((2 * BLOCK, D), BF16), ((BLOCK, D), BF16), ((8, D), F32)],
        [info, after(pieces_state[0], give)] + pieces_state[1:]
        + [Rows(piece, 0, BLOCK) for piece in shared]
        + [resid, own_states, own_grad_new, vectors, own_tokens, d_resid] + pieces_tok,
    )
    came = other_core(after(give, d_own))
    result = lax.all_gather(result, "mp", axis=0, tiled=True)
    left, right = shifted_x(d_own, 1), shifted_x(d_own, -1)
    shards = run(
        scatter_z_body, [((4, 32, PACK), BF16)] * 4, [info, keep, came, d_gains],
        [((128, D), F32), ((D, 128), F32)],
    )
    sent = shards[0]
    shards = [shards[0]] + [shifted(shards[k], "z", k) for k in (1, 2, 3)]
    far_tok, far_state = shifted_x(left[:BLOCK], 1), shifted_x(right[BLOCK:], -1)
    (updated,) = run(
        state_mix_body, [((NS, D), BF16)],
        [info, outs_state, Part(after(late_w, sent), D, 3), states, vectors],
        [((NS, D), BF16)],
    )
    d_gate_w, d_up_w, d_down_w = d_ff_w[:, :D], d_ff_w[:, D : 2 * D], d_ff_w[:, 2 * D :].T
    shards[0] = after(shards[0], updated, d_gate_w, d_up_w, d_down_w, far_tok, far_state)
    shards = run(scatter_y_body, [((32, PACK), BF16)] * 4, [info] + shards)
    shards = [shards[0]] + [shifted(shards[k], "dp", k) for k in (1, 2, 3)]
    d_tokens, d_states = run(
        collect_body, [((W, D), F32)] * 2,
        [info, after(d_own, shards[0]), left, right, far_tok, far_state],
    )
    shards[0] = after(shards[0], d_states)
    d_query_w, d_key_w, d_value_w, d_output_w, d_vectors = run(
        scatter_end_body, [((32, 256), F32)] * 4 + [((16, 32), F32)], [info] + shards
    )
    d_vectors = d_vectors[:4] + other_core(d_vectors[8:12])
    return (
        result[None],
        updated[None, None],
        d_tokens[None],
        d_states[None, None],
        d_query_w,
        d_key_w,
        d_value_w,
        d_output_w.T,
        d_gate_w,
        d_up_w,
        d_down_w,
        d_vectors[0],
        d_vectors[1],
        d_vectors[2],
        d_vectors[3],
    )


def solution(mesh):
    plane = PLANE
    mesh = Mesh(mesh.devices.reshape(4, 4, 2, 4), PLANE + ("mp",))
    placed = (
        P("dp", SEQ, None),
        P("dp", SEQ, None, None),
        P("dp", None),
        P(plane, "mp"),
        P(plane, "mp"),
        P(plane, "mp"),
        P("mp", plane),
        P(plane, "mp"),
        P(plane, "mp"),
        P("mp", plane),
        P(plane),
        P(plane),
        P(plane),
        P(plane),
        P("dp", SEQ, None),
        P("dp", SEQ, None, None),
    )
    return jax.shard_map(
        local,
        mesh=mesh,
        in_specs=placed,
        out_specs=(
            P("dp", SEQ, None),
            P("dp", SEQ, None, None),
            P("dp", SEQ, None),
            P("dp", SEQ, None, None),
            P(plane, "mp"),
            P(plane, "mp"),
            P(plane, "mp"),
            P("mp", plane),
            P(plane, "mp"),
            P(plane, "mp"),
            P("mp", plane),
            P(plane),
            P(plane),
            P(plane),
            P(plane),
        ),
        check_vma=False,
    )
```

```python
import functools

import jax
import jax.numpy as jnp
from jax import lax
from jax.experimental import pallas as pl
from jax.experimental.pallas import tpu as pltpu
from jax.sharding import Mesh
from jax.sharding import PartitionSpec as P

D = 1024
HD = 128
W = 512
NS = 512
PARTS = 4
BLOCK = W // PARTS
QKV = 768
PACK = 1152
SHARD = 896
SCALE = HD ** (-0.5)


EPS = 1e-05
NEG = -1e30
BF16, F32 = jnp.bfloat16, jnp.float32


SEQ = ("z", "core")
CHIPS = ("dp", "z")
PLANE = ("dp", "z", "core")


def passed_along(value, steps):
    count = lax.axis_size(SEQ)
    leading, last = (max(0, -steps), min(count, count - steps))
    return lax.ppermute(value, SEQ, [(source, source + steps) for source in range(leading, last)])


def shifted_x(value, steps):
    return lax.ppermute(value, "mp", [(i, (i + steps) % PARTS) for i in range(PARTS)])


def shifted(value, axis, steps):
    return lax.ppermute(value, axis, [(i, (i + steps) % 4) for i in range(4)])


def other_core(value):
    return lax.ppermute(value, "core", [(0, 1), (1, 0)])


def sent_back(blocks):
    return [blocks[0]] + [shifted_x(blocks[k], -k) for k in (1, 2, 3)]


def sent_on(blocks):
    return [blocks[0]] + [shifted_x(blocks[k], k) for k in (1, 2, 3)]


def product(left, right):
    return jnp.dot(left, right, preferred_element_type=F32)


def product_t(left, right):
    return lax.dot_general(left, right, (((1,), (1,)), ((), ())), preferred_element_type=F32)


def outer_sum(left, right):
    return lax.dot_general(left, right, (((0,), (0,)), ((), ())), preferred_element_type=F32)


def inv_rms(values):
    return lax.rsqrt(jnp.mean(values * values, axis=-1, keepdims=True) + EPS)


def norm_back(values, scale, gain, grad):
    inner = grad * gain
    along = jnp.mean(inner * values, axis=-1, keepdims=True)
    return scale * inner - values * (scale * scale * scale) * along


def block_rows(place, k):
    return pl.ds(pl.multiple_of(((place + PARTS - k) & 3) * BLOCK, BLOCK), BLOCK)


def total_of(pieces):
    total = pieces[0][...].astype(F32)
    for piece in pieces[1:]:
        total = total + piece[...].astype(F32)
    return total


def after(value, *others):
    return lax.optimization_barrier((value, *others))[0]


class Part:
    def __init__(self, array, width, index):
        self.array, self.shape = array, (array.shape[0], width)
        self.where = lambda ref, info: ref.at[:, pl.ds(index * width, width)]
        self.block = lambda _: (0, index)


class Rows:
    def __init__(self, array, start, size):
        self.array, self.shape = array, (size, array.shape[1])
        self.where = lambda ref, info: ref.at[pl.ds(start, size), :]
        self.block = lambda _: (start // size, 0)


class Source:
    def __init__(self, copy, ref):
        self.copy, self.ref = copy, ref
        copy.start()

    def ready(self):
        if self.copy is not None:
            self.copy.wait()
            self.copy = None
        return self.ref

    def __getitem__(self, index):
        return self.ready()[index]


class Target:
    def __init__(self, copy, ref):
        self.copy, self.ref, self.sent = copy, ref, False
        self.shape, self.dtype = ref.shape, ref.dtype

    def send(self):
        if not self.sent:
            self.copy.start()
            self.sent = True

    def __getitem__(self, index):
        return self.ref[index]

    def __setitem__(self, index, value):
        self.ref[index] = value


class Held:
    def __init__(self, ref):
        self.ref, self.shape, self.dtype = ref, ref.shape, ref.dtype

    def ready(self):
        return self.ref

    def send(self):
        pass

    def __getitem__(self, index):
        return self.ref[index]

    def __setitem__(self, index, value):
        self.ref[index] = value


def ready(*sources):
    for source in sources:
        source.ready()


def send(*targets):
    for target in targets:
        target.send()


def run(body, outs, args, scratch=(), limit=60):
    n_refs = len(args) - 1 + len(outs)

    def kernel(info, *refs):
        body(info, *[Held(ref) for ref in refs[:n_refs]], *refs[n_refs:])

    def spec(arg):
        if hasattr(arg, "block"):
            return pl.BlockSpec(arg.shape, arg.block)
        return pl.BlockSpec(arg.shape, lambda _: (0,) * len(arg.shape))

    call = pl.pallas_call(
        kernel,
        out_shape=[jax.ShapeDtypeStruct(shape, kind) for shape, kind in outs],
        grid=(1,),
        in_specs=[pl.BlockSpec(memory_space=pltpu.SMEM)] + [spec(arg) for arg in args[1:]],
        out_specs=[spec(jax.ShapeDtypeStruct(shape, kind)) for shape, kind in outs],
        scratch_shapes=[pltpu.VMEM(shape, kind) for shape, kind in scratch],
        compiler_params=pltpu.CompilerParams(vmem_limit_bytes=limit << 20),
        cost_estimate=pl.CostEstimate(flops=1, bytes_accessed=1, transcendentals=0),
        name=body.__name__.replace("_body", ""),
    )
    return list(call(*[arg.array if hasattr(arg, "block") else arg for arg in args]))


def run_early(body, outs, args, scratch=(), limit=60):
    n_in, n_out = len(args) - 1, len(outs)

    def kernel(info, *refs):
        given, results = refs[:n_in], refs[n_in : n_in + n_out]
        held = refs[n_in + n_out : 2 * (n_in + n_out)]
        extra, (in_sems, out_sems) = refs[2 * (n_in + n_out) : -2], refs[-2:]
        sources = []
        for index, (arg, ref) in enumerate(zip(args[1:], given)):
            where = arg.where(ref, info) if hasattr(arg, "where") else ref
            copy = pltpu.make_async_copy(where, held[index], in_sems.at[index])
            sources.append(Source(copy, held[index]))
        targets = []
        for index, ref in enumerate(results):
            copy = pltpu.make_async_copy(held[n_in + index], ref, out_sems.at[index])
            targets.append(Target(copy, held[n_in + index]))
        body(info, *sources, *targets, *extra)
        ready(*sources)
        send(*targets)
        for target in targets:
            target.copy.wait()

    arrays = [arg.array if hasattr(arg, "where") else arg for arg in args]
    buffers = [pltpu.VMEM(arg.shape, array.dtype) for arg, array in zip(args[1:], arrays[1:])]
    buffers += [pltpu.VMEM(shape, kind) for shape, kind in outs]
    call = pl.pallas_call(
        kernel,
        out_shape=[jax.ShapeDtypeStruct(shape, kind) for shape, kind in outs],
        in_specs=[pl.BlockSpec(memory_space=pltpu.SMEM)] + [pl.BlockSpec(memory_space=pl.ANY)] * n_in,
        out_specs=[pl.BlockSpec(memory_space=pl.ANY)] * n_out,
        scratch_shapes=buffers
        + [pltpu.VMEM(shape, kind) for shape, kind in scratch]
        + [pltpu.SemaphoreType.DMA((n_in,)), pltpu.SemaphoreType.DMA((n_out,))],
        compiler_params=pltpu.CompilerParams(vmem_limit_bytes=limit << 20),
        cost_estimate=pl.CostEstimate(flops=1, bytes_accessed=1, transcendentals=0),
        name=body.__name__.replace("_body", ""),
    )
    return list(call(*arrays))


def softmax_parts(scores):
    peak = functools.reduce(
        jnp.maximum, [jnp.max(part, axis=-1, keepdims=True) for part in scores]
    )
    grown = [jnp.exp(part - peak) for part in scores]
    total = functools.reduce(jnp.add, [jnp.sum(part, axis=-1, keepdims=True) for part in grown])
    inverse = 1.0 / total
    return [(part * inverse).astype(BF16) for part in grown], peak + jnp.log(total)


def state_fwd_body(info, query, pair_tok, attn, logsum):
    ready(query, pair_tok)
    for head in range(2):
        lanes = pl.ds(head * HD, HD)
        key, value = pair_tok[:, lanes], pair_tok[:, pl.ds(256 + head * HD, HD)]

        @pl.loop(0, 2)
        def _(b):
            here = pl.ds(pl.multiple_of(b * 256, 256), 256)
            scores = product_t(query[here, lanes], key) * SCALE
            (probs,), total = softmax_parts([scores])
            attn[here, lanes] = product(probs, value).astype(BF16)
            logsum[here, lanes] = jnp.broadcast_to(total, (256, HD))


def documents(info, positions):
    count, end = jnp.zeros_like(positions), 0
    for index in range(4):
        end = end + info[5 + index]
        count = count + (positions >= end).astype(jnp.int32)
    return count


def nearby_masks(info, first_row, rows):
    start = info[4] * W
    query_pos = start + first_row + lax.broadcasted_iota(jnp.int32, (rows, 1), 0)
    key_pos = start + lax.broadcasted_iota(jnp.int32, (1, W), 1)
    query_doc = documents(info, query_pos)
    prev = (key_pos >= W) & (documents(info, key_pos - W) == query_doc)
    own = (key_pos <= query_pos) & (documents(info, key_pos) == query_doc)
    return prev, own


def attend_body(info, *refs):
    mine, theirs, before, tokens, states = refs[:4], refs[4:8], refs[8:10], refs[10], refs[11]
    normed, query, pair_tok, pair_state, pair_prev, qkv_w, vectors = refs[12:19]
    attn, logsum, gains = refs[19:]
    y, z, core = info[1], info[2], info[3]
    for kz in range(4):
        for side, pieces in ((0, mine), (1, theirs)):
            for ky in range(4):
                shard = ((y + 4 - ky) & 3) * 8 + ((z + 4 - kz) & 3) * 2 + (core ^ side)
                rows = pl.ds(pl.multiple_of(shard * 32, 32), 32)
                qkv_w[rows, :] = pieces[kz][ky, :, :QKV]
                gains[rows, :] = pieces[kz][ky, :, QKV:]
    qkv_w.send()
    across = gains[...].astype(F32).T
    vectors[0:3, :] = across[0:3]
    vectors[3:4, :] = jax.nn.sigmoid(across[3:4])
    vectors[4:8, :] = jnp.zeros((4, D), F32)
    vectors.send()

    def normalized(values, lane):
        values = values.astype(F32)
        return (values * inv_rms(values) * vectors[lane : lane + 1, :]).astype(BF16)

    for part, (rows, pair) in enumerate(((tokens, pair_tok), (states, pair_state))):
        ready(rows)

        @pl.loop(0, 2)
        def _(b):
            here = pl.ds(pl.multiple_of(b * 256, 256), 256)
            there = pl.ds(pl.multiple_of(part * W + b * 256, 256), 256)
            normed[there, :] = normalized(rows[here, :], part)
            out = product(normed[there, :], qkv_w[...]).astype(BF16)
            query[there, :] = out[:, :256]
            pair[here, :] = out[:, 256:]

        pair.send()
    send(normed, query)
    for b, half in enumerate(before):
        here = pl.ds(pl.multiple_of(((info[0] + b) & 1) * 256, 256), 256)
        pair_prev[here, :] = product(normalized(half[...], 0), qkv_w[:, 256:]).astype(BF16)
    pair_prev.send()

    for head in range(2):
        lanes = pl.ds(head * HD, HD)
        far = pl.ds(256 + head * HD, HD)

        @pl.loop(0, 2)
        def _(b):
            here = pl.ds(pl.multiple_of(b * 256, 256), 256)
            prev, own = nearby_masks(info, b * 256, 256)
            rows = query[here, lanes]
            scores = [
                jnp.where(prev, product_t(rows, pair_prev[:, lanes]) * SCALE, NEG),
                jnp.where(own, product_t(rows, pair_tok[:, lanes]) * SCALE, NEG),
                product_t(rows, pair_state[:, lanes]) * SCALE,
            ]
            probs, total = softmax_parts(scores)
            out = (
                product(probs[0], pair_prev[:, far])
                + product(probs[1], pair_tok[:, far])
                + product(probs[2], pair_state[:, far])
            )
            attn[here, lanes] = out.astype(BF16)
            logsum[here, lanes] = jnp.broadcast_to(total, (256, HD))


def state_mix_body(info, outs, output_w, states, vectors, updated, attn):
    ready(outs, output_w, states, vectors)
    for k in range(4):
        attn[:, pl.ds(256 * k, 256)] = outs[(info[0] + 4 - k) & 3]
    forget = vectors[3:4, :]

    @pl.loop(0, 2)
    def _(b):
        here = pl.ds(pl.multiple_of(b * 256, 256), 256)
        mixed = product_t(attn[here, :], output_w[...])
        given = states[here, :].astype(F32)
        updated[here, :] = (given * forget + mixed * (1.0 - forget)).astype(BF16)


def forward_body(info, *refs):
    outs = refs[:4]
    tokens, vectors, output_w, down_w, grad_out, gate_w, up_w = refs[4:11]
    resid, ff_in, hidden, d_gate_up = refs[11:15]
    blocks = refs[15:19]
    d_ff_in, attn, values = refs[19:]
    for k in range(4):
        attn[:, pl.ds(256 * k, 256)] = outs[k][...]
    ready(tokens, vectors, output_w)
    for c in range(4):
        at = pl.ds(c * 256, 256)
        values[:, at] = tokens[:, at].astype(F32) + product_t(attn[...], output_w[at, :])

    @pl.loop(0, 4)
    def _(b):
        here = pl.ds(pl.multiple_of(b * 128, 128), 128)
        rows = values[here, :]
        ff_in[here, :] = (rows * inv_rms(rows) * vectors[2:3, :]).astype(BF16)

    ff_in.send()
    resid[...] = values[block_rows(info[0], 0), :]
    resid.send()
    for c in range(4):
        at, beyond = pl.ds(c * 256, 256), pl.ds(D + c * 256, 256)
        d_hidden = product(grad_out[...], down_w[:, at])
        gate = product(ff_in[...], gate_w[:, at])
        up = product(ff_in[...], up_w[:, at])
        sigma = jax.nn.sigmoid(gate)
        active = gate * sigma
        hidden[:, at] = (active * up).astype(BF16)
        d_gate = d_hidden * up * sigma * (1.0 + gate * (1.0 - sigma))
        d_gate_up[:, at] = d_gate.astype(BF16)
        d_gate_up[:, beyond] = (d_hidden * active).astype(BF16)
    send(hidden, d_gate_up)
    for c in range(4):
        at = pl.ds(c * 256, 256)
        d_ff_in[:, at] = (
            product_t(d_gate_up[:, :D], gate_w[at, :]) + product_t(d_gate_up[:, D:], up_w[at, :])
        ).astype(BF16)
    for k in range(4):
        blocks[k][...] = d_ff_in[block_rows(info[0], k), :]
        blocks[k].send()


def forward_out_body(info, hidden, down_w, d_mix, *refs):
    shared, out = refs[:4], refs[4]
    ready(hidden, down_w)
    for c in range(4):
        at = pl.ds(c * 256, 256)
        out[:, at] = product_t(hidden[...], down_w[at, :]).astype(BF16)
    for k in range(4):
        shared[k][:BLOCK, :] = out[block_rows(info[0], k), :]
        shared[k][BLOCK:, :] = d_mix[...]


def resid_back_body(info, *refs):
    pieces, resid, vectors, grad_out, output_w = refs[:4], refs[4], refs[5], refs[6], refs[7]
    d_resid, d_forward, d_mix = refs[8:11]
    blocks = refs[11:]
    grad, values = total_of(pieces), resid[...]
    scale = inv_rms(values)
    total = grad_out[block_rows(info[0], 0), :].astype(F32) + norm_back(values, scale, vectors[2:3, :], grad)
    rounded = total.astype(BF16)
    for k in range(4):
        at = pl.ds(256 * ((4 - k) % 4), 256)
        blocks[k][...] = product(rounded, output_w[:, at]).astype(BF16)
    d_mix[...] = rounded
    d_resid[...] = total
    d_forward[...] = jnp.sum(grad * values * scale, axis=0, keepdims=True)


def part_back(query, turned_query, key, value, d_out, turned_d_out, logsum, center, mask):
    scores = product_t(query, key) * SCALE
    if mask is not None:
        scores = jnp.where(mask, scores, NEG)
    probs = jnp.exp(scores - logsum)
    d_probs = product_t(d_out, value)
    d_scores = (probs * (d_probs - center)).astype(BF16)
    d_query = product(d_scores, key) * SCALE
    d_key = product(turned_query, d_scores) * SCALE
    d_value = product(turned_d_out, probs.astype(BF16))
    return d_query, d_key.T, d_value.T


def turned(values):
    return values.astype(F32).T.astype(BF16)


def center_of(d_out, out):
    return jnp.sum(d_out.astype(F32) * out.astype(F32), axis=-1, keepdims=True)


def state_back_body(
    info, output_w, vectors, grad_new, states, attn, query, pair_tok, logsum, *refs
):
    d_mix, d_query, d_pair, d_forget, d_attn = refs
    ready(output_w, vectors, grad_new, attn)
    forget = vectors[3:4, :]
    own = block_rows(info[0], 0)
    d_forget[...] = jnp.sum(
        grad_new[own, :].astype(F32) * states[own, :].astype(F32), axis=0, keepdims=True
    )

    @pl.loop(0, 2)
    def _(b):
        here = pl.ds(pl.multiple_of(b * 256, 256), 256)
        grad = grad_new[here, :].astype(F32)
        rounded = (grad * (1.0 - forget)).astype(BF16)
        d_mix[here, :] = rounded
        d_attn[here, :] = product(rounded, output_w[...]).astype(BF16)
        mixed = product_t(attn[here, :], output_w[...])
        d_forget[...] -= jnp.sum(grad * mixed, axis=0, keepdims=True)

    d_mix.send()
    d_forget[...] *= forget * (1.0 - forget)
    for head in range(2):
        lanes = pl.ds(head * HD, HD)
        far = pl.ds(256 + head * HD, HD)
        rows, d_out = query[:, lanes], d_attn[:, lanes]
        center = center_of(d_out, attn[:, lanes])
        total = logsum[:, pl.ds(head * HD, 1)]
        d_rows, d_key, d_value = part_back(
            rows, turned(rows), pair_tok[:, lanes], pair_tok[:, far], d_out, turned(d_out),
            total, center, None,
        )
        d_query[:, lanes] = d_rows.astype(BF16)
        d_pair[:, lanes] = d_key
        d_pair[:, far] = d_value


def prev_back_body(info, *refs):
    pieces, query, pair_prev, attn, logsum = refs[:4], refs[4], refs[5], refs[6], refs[7]
    d_pair, d_query, d_attn = refs[8:]
    for k in range(4):
        d_attn[block_rows(info[0], k), :] = pieces[k][...]
    d_attn.send()
    prev, _ = nearby_masks(info, 0, W)
    for head in range(2):
        lanes = pl.ds(head * HD, HD)
        far = pl.ds(256 + head * HD, HD)
        rows, d_out = query[:, lanes], d_attn[:, lanes]
        center = center_of(d_out, attn[:, lanes])
        total = logsum[:, pl.ds(head * HD, 1)]
        d_rows, d_key, d_value = part_back(
            rows, turned(rows), pair_prev[:, lanes], pair_prev[:, far], d_out, turned(d_out),
            total, center, prev,
        )
        d_query[:, lanes] = d_rows
        d_pair[:, lanes] = d_key.astype(BF16)
        d_pair[:, far] = d_value.astype(BF16)


def rows_back(info, given, qkv_w, d_qkv, d_gain, blocks):
    d_gain[...] = jnp.zeros(d_gain.shape, F32)
    for k in range(4):
        rows = block_rows(info[0], k)
        grad = product_t(d_qkv[rows, :], qkv_w[...])
        values = given[rows, :].astype(F32)
        d_gain[...] += jnp.sum(grad * values * inv_rms(values), axis=0, keepdims=True)
        blocks[k][...] = grad.astype(BF16)
        blocks[k].send()


def own_back_body(
    info, query, pair_state, d_attn, attn, logsum, pair_tok, d_query_part, d_pair_more,
    d_query_state, qkv_w, states, *refs,
):
    d_query, d_pair_tok, d_qkv, d_gain = refs[:4]
    blocks = refs[4:]
    _, own = nearby_masks(info, 0, W)
    for head in range(2):
        lanes = pl.ds(head * HD, HD)
        far = pl.ds(256 + head * HD, HD)
        rows, d_out = query[:, lanes], d_attn[:, lanes]
        rows_t, d_out_t = turned(rows), turned(d_out)
        center = center_of(d_out, attn[:, lanes])
        total = logsum[:, pl.ds(head * HD, 1)]
        more, d_key, d_value = part_back(
            rows, rows_t, pair_state[:, lanes], pair_state[:, far], d_out, d_out_t, total, center,
            None,
        )
        d_qkv[:, pl.ds(256 + head * HD, HD)] = d_key.astype(BF16)
        d_qkv[:, pl.ds(512 + head * HD, HD)] = d_value.astype(BF16)
        d_rows, d_key, d_value = part_back(
            rows, rows_t, pair_tok[:, lanes], pair_tok[:, far], d_out, d_out_t, total, center, own
        )
        d_pair_tok[:, lanes] = d_key + d_pair_more[:, lanes]
        d_pair_tok[:, far] = d_value + d_pair_more[:, far]
        d_query[:, lanes] = (d_query_part[:, lanes] + d_rows + more).astype(BF16)
    send(d_pair_tok, d_query)
    d_qkv[:, :256] = d_query_state[...]
    d_qkv.send()

    rows_back(info, states, qkv_w, d_qkv, d_gain, blocks)


def token_rows_body(
    info, d_query, d_pair, d_pair_back, qkv_w, tokens, d_state, d_forward, d_forget, d_qkv, *refs
):
    blocks, d_gain = refs[:4], refs[4]
    d_qkv[:, :256] = d_query[...]
    d_qkv[:, 256:] = (d_pair[...] + d_pair_back[...].astype(F32)).astype(BF16)
    tops = [Held(block.ref.at[pl.ds(0, BLOCK), :]) for block in blocks]
    rows_back(info, tokens, qkv_w, d_qkv, d_gain, tops)
    gains = jnp.concatenate(
        [d_gain[...], d_state[...], d_forward[...], d_forget[...], jnp.zeros((12, D), F32)], axis=0
    ).astype(BF16)
    for block in blocks:
        block[BLOCK:, :] = gains


def attn_grads_body(
    info, normed, d_qkv_tok, d_qkv_state, d_mix_state, attn_tok, attn_state, *refs
):
    shared, keep, give, whole = refs[:4], refs[4], refs[5], refs[6]
    for k in range(4):
        whole[block_rows(info[0], 4 - k), :] = shared[k][BLOCK:, :]
    first = info[3] == 0
    ready(normed, d_qkv_tok, d_qkv_state, d_mix_state, attn_tok, attn_state)

    @pl.loop(0, 4)
    def _(c):
        at = pl.ds(pl.multiple_of(c * 256, 256), 256)
        groups = pl.ds(pl.multiple_of(c * 4, 4), 4)
        sums = (
            outer_sum(normed[:W, at], d_qkv_tok[...]) + outer_sum(normed[W:, at], d_qkv_state[...]),
            outer_sum(whole[:, at], attn_tok[...]) + outer_sum(d_mix_state[:, at], attn_state[...]),
        )
        for part, lanes in zip(sums, (pl.ds(0, QKV), pl.ds(QKV, 256))):
            split = part.astype(BF16).reshape(4, 2, 32, part.shape[1])
            even, odd = split[:, 0], split[:, 1]
            keep[groups, :, lanes] = jnp.where(first, even, odd)
            give[groups, :, lanes] = jnp.where(first, odd, even)


def scatter_z_body(info, keep, came, gains, *refs):
    pieces, rows, across = refs[:4], refs[4], refs[5]
    rows[...] = jnp.zeros_like(rows)
    rows[0:8, :] = gains[...]
    rows[8:16, :] = gains[...]
    across[...] = rows[...].T
    near = lax.broadcasted_iota(jnp.int32, (32, 128), 1) < 8
    for k in range(4):
        z = (info[2] + k) & 3
        for y in range(4):
            group = y * 4 + z
            pieces[k][y, :, :D] = (keep[group].astype(F32) + came[group].astype(F32)).astype(BF16)
            own = across[pl.ds(pl.multiple_of((group * 2 + info[3]) * 32, 32), 32), :]
            other = across[pl.ds(pl.multiple_of((group * 2 + 1 - info[3]) * 32, 32), 32), :]
            pieces[k][y, :, D:] = jnp.where(near, own, other).astype(BF16)
        pieces[k].send()


def scatter_y_body(info, *refs):
    pieces, outs = refs[:4], refs[4:]
    for k in range(4):
        y = (info[1] + k) & 3
        total = pieces[0][y].astype(F32)
        for piece in pieces[1:]:
            total = total + piece[y].astype(F32)
        outs[k][...] = total.astype(BF16)


def scatter_end_body(info, *refs):
    total = total_of(refs[:4])
    d_query, d_key, d_value, d_output, d_vectors = refs[4:]
    d_query[...] = total[:, :256]
    d_key[...] = total[:, 256:512]
    d_value[...] = total[:, 512:768]
    d_output[...] = total[:, 768:1024]
    d_vectors[...] = total[:, 1024:].T[:16]


def ends_body(info, *refs):
    from_states, shared, resid, states, grad_new, vectors, tokens, d_resid, from_tokens = (
        refs[:4], refs[4:8], refs[8], refs[9], refs[10], refs[11], refs[12], refs[13], refs[14:18],
    )
    d_own, result, gains = refs[18:]
    values = states[...].astype(F32)
    d_own[BLOCK:, :] = (
        grad_new[...].astype(F32) * vectors[3:4, :]
        + norm_back(values, inv_rms(values), vectors[1:2, :], total_of(from_states))
    ).astype(BF16)
    values = tokens[...].astype(F32)
    total = total_of(from_tokens)
    d_own[:BLOCK, :] = (
        d_resid[...] + norm_back(values, inv_rms(values), vectors[0:1, :], total[:BLOCK])
    ).astype(BF16)
    gains[...] = total[BLOCK : BLOCK + 8]
    result[...] = (resid[...] + total_of(shared)).astype(BF16)


def collect_body(info, own, left, right, far_tok, far_state, d_tokens, d_states):
    for k, piece in ((0, own), (1, left), (3, right)):
        rows = block_rows(info[0], k)
        d_tokens[rows, :] = piece[:BLOCK, :].astype(F32)
        d_states[rows, :] = piece[BLOCK:, :].astype(F32)
    rows = block_rows(info[0], 2)
    d_tokens[rows, :] = far_tok[...].astype(F32)
    d_states[rows, :] = far_state[...].astype(F32)


def local(
    tokens,
    states,
    doc_lengths,
    w_query,
    w_key,
    w_value,
    w_output,
    w_gate,
    w_up,
    w_down,
    attention_gain,
    state_gain,
    forward_gain,
    forget_bias,
    d_output,
    d_new_states,
):
    place = lax.axis_index("mp")
    y = lax.axis_index("dp")
    z, core = lax.axis_index("z"), lax.axis_index("core")
    info = jnp.concatenate(
        [jnp.stack([place, y, z, core, 2 * z + core]), doc_lengths[0]]
    ).astype(jnp.int32)
    tokens, states = tokens[0], states[0, 0]
    grad_out, grad_new = d_output[0], d_new_states[0, 0]
    gains = jnp.stack([attention_gain, state_gain, forward_gain, forget_bias], axis=1)
    gains = jnp.pad(gains, ((0, 0), (0, 124)))
    packed = jnp.concatenate([w_query, w_key, w_value, gains], axis=1)
    output_shard = w_output.T
    late_shard = jnp.concatenate(
        [w_gate, w_up, w_down.T] + sent_on([output_shard] * 4), axis=1
    )
    late_w = lax.all_gather(late_shard, PLANE, axis=0, tiled=True)
    half = lax.dynamic_slice_in_dim(tokens, (place % 2) * 256, 256, 0)
    half = passed_along(half, 1)
    before = [half, lax.ppermute(half, "mp", [(0, 1), (1, 0), (2, 3), (3, 2)])]
    packed = jnp.stack([after(packed, half)] + [shifted(packed, "dp", k) for k in (1, 2, 3)])
    mine = [packed] + [shifted(packed, "z", k) for k in (1, 2, 3)]
    theirs = [other_core(piece) for piece in mine]

    normed, query, pair_tok, pair_state, pair_prev, qkv_w, vectors, attn_tok, sums_tok = run_early(
        attend_body,
        [
            ((2 * W, D), BF16), ((2 * W, 256), BF16), ((W, 512), BF16), ((W, 512), BF16),
            ((W, 512), BF16), ((D, QKV), BF16), ((8, D), F32), ((W, 256), BF16), ((W, 256), F32),
        ],
        [info] + mine + theirs + before + [tokens, states],
        [((D, 128), BF16)],
    )
    query_tok, query_state = Rows(query, 0, W), Rows(query, W, NS)
    attn_state, sums_state = run(
        state_fwd_body, [((NS, 256), BF16), ((NS, 256), F32)],
        [info, query_state, pair_tok],
    )
    outs_tok = sent_on([attn_tok] * 4)
    outs_state = lax.all_gather(after(attn_state, late_w[0]), "mp", axis=0)
    output_w, own_output_w = Part(late_w, D, 3), Part(late_w, 256, 12)
    down_w = Part(late_w, D, 2)
    d_mix_state, d_query_state, d_pair_more, d_forget = run(
        state_back_body,
        [((NS, D), BF16), ((NS, 256), BF16), ((NS, 512), F32), ((1, D), F32)],
        [
            info, own_output_w, vectors, grad_new, states, attn_state, query_state, pair_tok,
            sums_state,
        ],
        [((NS, 256), BF16)],
    )
    outs_tok[0] = after(outs_tok[0], d_query_state)
    resid, ff_in, hidden, d_gate_up, *blocks = run_early(
        forward_body,
        [((BLOCK, D), F32), ((W, D), BF16), ((W, D), BF16), ((W, 2 * D), BF16)]
        + [((BLOCK, D), BF16)] * 4,
        [info] + outs_tok
        + [tokens, vectors, output_w, down_w, grad_out, Part(late_w, D, 0), Part(late_w, D, 1)],
        [((W, D), BF16), ((W, D), BF16), ((W, D), F32)],
    )
    pieces = sent_back(blocks)

    d_ff_w = jnp.concatenate(
        [outer_sum(ff_in, d_gate_up).astype(BF16), outer_sum(grad_out, hidden).astype(BF16)], axis=1
    )
    pieces[0] = after(pieces[0], d_ff_w)
    d_ff_w = after(d_ff_w, *pieces[1:])
    d_ff_w = lax.psum_scatter(d_ff_w, PLANE, scatter_dimension=0, tiled=True).astype(F32)

    d_resid, d_forward, d_mix_own, *blocks = run(
        resid_back_body,
        [((BLOCK, D), F32), ((1, D), F32), ((BLOCK, D), BF16)] + [((BLOCK, 256), BF16)] * 4,
        [info] + pieces + [resid, vectors, grad_out, output_w],
    )
    pieces = sent_on(blocks)
    blocks = run(
        forward_out_body, [((2 * BLOCK, D), BF16)] * 4, [info, hidden, down_w, d_mix_own],
        [((W, D), BF16)],
    )
    pieces[0] = after(pieces[0], blocks[0])
    shared = sent_back([after(block, *pieces[1:]) for block in blocks])

    d_pair_prev, d_query_part, d_attn_tok = run(
        prev_back_body,
        [((W, 512), BF16), ((W, 256), F32), ((W, 256), BF16)],
        [info] + pieces + [query_tok, pair_prev, attn_tok, sums_tok],
    )
    d_pair_back = passed_along(d_pair_prev, -1)
    d_query_tok, d_pair_tok, d_qkv_state, d_state_gain, *blocks = run_early(
        own_back_body,
        [((W, 256), BF16), ((W, 512), F32), ((NS, QKV), BF16), ((1, D), F32)]
        + [((BLOCK, D), BF16)] * 4,
        [
            info, query_tok, pair_state, d_attn_tok, attn_tok, sums_tok, pair_tok, d_query_part,
            d_pair_more, d_query_state, qkv_w, states,
        ],
    )
    pieces_state = sent_back(blocks)
    d_pair_back = after(d_pair_back, d_state_gain, *shared[1:])
    d_qkv_tok, *blocks = run(
        token_rows_body,
        [((W, QKV), BF16)] + [((BLOCK + 16, D), BF16)] * 4,
        [
            info, d_query_tok, d_pair_tok, d_pair_back, qkv_w, tokens, d_state_gain, d_forward,
            d_forget,
        ],
        [((1, D), F32)],
    )
    pieces_tok = sent_back([after(block, *pieces_state[1:]) for block in blocks])

    keep, give = run(
        attn_grads_body,
        [((16, 32, D), BF16)] * 2,
        [
            info, normed, d_qkv_tok, d_qkv_state, d_mix_state, attn_tok,
            attn_state,
        ]
        + shared,
        [((W, D), BF16)],
    )
    own_tokens, own_states, own_grad_new = [
        lax.dynamic_slice_in_dim(rows, place * BLOCK, BLOCK, 0)
        for rows in (after(tokens, give), states, grad_new)
    ]
    d_own, result, d_gains = run(
        ends_body,
        [((2 * BLOCK, D), BF16), ((BLOCK, D), BF16), ((8, D), F32)],
        [info, after(pieces_state[0], give)] + pieces_state[1:]
        + [Rows(piece, 0, BLOCK) for piece in shared]
        + [resid, own_states, own_grad_new, vectors, own_tokens, d_resid] + pieces_tok,
    )
    came = other_core(after(give, d_own))
    result = lax.all_gather(result, "mp", axis=0, tiled=True)
    left, right = shifted_x(d_own, 1), shifted_x(d_own, -1)
    shards = run(
        scatter_z_body, [((4, 32, PACK), BF16)] * 4, [info, keep, came, d_gains],
        [((128, D), F32), ((D, 128), F32)], limit=12,
    )
    sent = shards[0]
    shards = [shards[0]] + [shifted(shards[k], "z", k) for k in (1, 2, 3)]
    far_tok, far_state = shifted_x(left[:BLOCK], 1), shifted_x(right[BLOCK:], -1)
    (updated,) = run(
        state_mix_body, [((NS, D), BF16)],
        [info, outs_state, Part(after(late_w, sent), D, 3), states, vectors],
        [((NS, D), BF16)],
    )
    d_gate_w, d_up_w, d_down_w = d_ff_w[:, :D], d_ff_w[:, D : 2 * D], d_ff_w[:, 2 * D :].T
    shards[0] = after(shards[0], updated, d_gate_w, d_up_w, d_down_w, far_tok, far_state)
    shards = run(scatter_y_body, [((32, PACK), BF16)] * 4, [info] + shards, limit=6)
    shards = [shards[0]] + [shifted(shards[k], "dp", k) for k in (1, 2, 3)]
    d_tokens, d_states = run(
        collect_body, [((W, D), F32)] * 2,
        [info, after(d_own, shards[0]), left, right, far_tok, far_state],
    )
    shards[0] = after(shards[0], d_states)
    d_query_w, d_key_w, d_value_w, d_output_w, d_vectors = run(
        scatter_end_body, [((32, 256), F32)] * 4 + [((16, 32), F32)], [info] + shards, limit=6)
    d_vectors = d_vectors[:4] + other_core(d_vectors[8:12])
    return (
        result[None],
        updated[None, None],
        d_tokens[None],
        d_states[None, None],
        d_query_w,
        d_key_w,
        d_value_w,
        d_output_w.T,
        d_gate_w,
        d_up_w,
        d_down_w,
        d_vectors[0],
        d_vectors[1],
        d_vectors[2],
        d_vectors[3],
    )


def solution(mesh):
    plane = PLANE
    mesh = Mesh(mesh.devices.reshape(4, 4, 2, 4), PLANE + ("mp",))
    placed = (
        P("dp", SEQ, None),
        P("dp", SEQ, None, None),
        P("dp", None),
        P(plane, "mp"),
        P(plane, "mp"),
        P(plane, "mp"),
        P("mp", plane),
        P(plane, "mp"),
        P(plane, "mp"),
        P("mp", plane),
        P(plane),
        P(plane),
        P(plane),
        P(plane),
        P("dp", SEQ, None),
        P("dp", SEQ, None, None),
    )
    return jax.shard_map(
        local,
        mesh=mesh,
        in_specs=placed,
        out_specs=(
            P("dp", SEQ, None),
            P("dp", SEQ, None, None),
            P("dp", SEQ, None),
            P("dp", SEQ, None, None),
            P(plane, "mp"),
            P(plane, "mp"),
            P(plane, "mp"),
            P("mp", plane),
            P(plane, "mp"),
            P(plane, "mp"),
            P("mp", plane),
            P(plane),
            P(plane),
            P(plane),
            P(plane),
        ),
        check_vma=False,
    )
```

```python
import functools

import jax
import jax.numpy as jnp
from jax import lax
from jax.experimental import pallas as pl
from jax.experimental.pallas import tpu as pltpu
from jax.sharding import Mesh
from jax.sharding import PartitionSpec as P

D = 1024
HD = 128
W = 512
NS = 512
PARTS = 4
BLOCK = W // PARTS
QKV = 768
PACK = 1152
SHARD = 896
SCALE = HD ** (-0.5)


EPS = 1e-05
NEG = -1e30
BF16, F32 = jnp.bfloat16, jnp.float32


SEQ = ("z", "core")
CHIPS = ("dp", "z")
PLANE = ("dp", "z", "core")


def passed_along(value, steps):
    count = lax.axis_size(SEQ)
    leading, last = (max(0, -steps), min(count, count - steps))
    return lax.ppermute(value, SEQ, [(source, source + steps) for source in range(leading, last)])


def shifted_x(value, steps):
    return lax.ppermute(value, "mp", [(i, (i + steps) % PARTS) for i in range(PARTS)])


def shifted(value, axis, steps):
    return lax.ppermute(value, axis, [(i, (i + steps) % 4) for i in range(4)])


def other_core(value):
    return lax.ppermute(value, "core", [(0, 1), (1, 0)])


def sent_back(blocks):
    return [blocks[0]] + [shifted_x(blocks[k], -k) for k in (1, 2, 3)]


def sent_on(blocks):
    return [blocks[0]] + [shifted_x(blocks[k], k) for k in (1, 2, 3)]


def product(left, right):
    return jnp.dot(left, right, preferred_element_type=F32)


def product_t(left, right):
    return lax.dot_general(left, right, (((1,), (1,)), ((), ())), preferred_element_type=F32)


def outer_sum(left, right):
    return lax.dot_general(left, right, (((0,), (0,)), ((), ())), preferred_element_type=F32)


def inv_rms(values):
    return lax.rsqrt(jnp.mean(values * values, axis=-1, keepdims=True) + EPS)


def norm_back(values, scale, gain, grad):
    inner = grad * gain
    along = jnp.mean(inner * values, axis=-1, keepdims=True)
    return scale * inner - values * (scale * scale * scale) * along


def block_rows(place, k):
    return pl.ds(pl.multiple_of(((place + PARTS - k) & 3) * BLOCK, BLOCK), BLOCK)


def total_of(pieces):
    total = pieces[0][...].astype(F32)
    for piece in pieces[1:]:
        total = total + piece[...].astype(F32)
    return total


def after(value, *others):
    return lax.optimization_barrier((value, *others))[0]


class Part:
    def __init__(self, array, width, index):
        self.array, self.shape = array, (array.shape[0], width)
        self.where = lambda ref, info: ref.at[:, pl.ds(index * width, width)]
        self.block = lambda _: (0, index)


class Rows:
    def __init__(self, array, start, size):
        self.array, self.shape = array, (size, array.shape[1])
        self.where = lambda ref, info: ref.at[pl.ds(start, size), :]
        self.block = lambda _: (start // size, 0)


class Source:
    def __init__(self, copy, ref):
        self.copy, self.ref = copy, ref
        copy.start()

    def ready(self):
        if self.copy is not None:
            self.copy.wait()
            self.copy = None
        return self.ref

    def __getitem__(self, index):
        return self.ready()[index]


class Target:
    def __init__(self, copy, ref):
        self.copy, self.ref, self.sent = copy, ref, False
        self.shape, self.dtype = ref.shape, ref.dtype

    def send(self):
        if not self.sent:
            self.copy.start()
            self.sent = True

    def __getitem__(self, index):
        return self.ref[index]

    def __setitem__(self, index, value):
        self.ref[index] = value


class Held:
    def __init__(self, ref):
        self.ref, self.shape, self.dtype = ref, ref.shape, ref.dtype

    def ready(self):
        return self.ref

    def send(self):
        pass

    def __getitem__(self, index):
        return self.ref[index]

    def __setitem__(self, index, value):
        self.ref[index] = value


def ready(*sources):
    for source in sources:
        source.ready()


def send(*targets):
    for target in targets:
        target.send()


def run(body, outs, args, scratch=(), limit=60):
    n_refs = len(args) - 1 + len(outs)

    def kernel(info, *refs):
        body(info, *[Held(ref) for ref in refs[:n_refs]], *refs[n_refs:])

    def spec(arg):
        if hasattr(arg, "block"):
            return pl.BlockSpec(arg.shape, arg.block)
        return pl.BlockSpec(arg.shape, lambda _: (0,) * len(arg.shape))

    call = pl.pallas_call(
        kernel,
        out_shape=[jax.ShapeDtypeStruct(shape, kind) for shape, kind in outs],
        grid=(1,),
        in_specs=[pl.BlockSpec(memory_space=pltpu.SMEM)] + [spec(arg) for arg in args[1:]],
        out_specs=[spec(jax.ShapeDtypeStruct(shape, kind)) for shape, kind in outs],
        scratch_shapes=[pltpu.VMEM(shape, kind) for shape, kind in scratch],
        compiler_params=pltpu.CompilerParams(vmem_limit_bytes=limit << 20),
        cost_estimate=pl.CostEstimate(flops=1, bytes_accessed=1, transcendentals=0),
        name=body.__name__.replace("_body", ""),
    )
    return list(call(*[arg.array if hasattr(arg, "block") else arg for arg in args]))


def run_early(body, outs, args, scratch=(), limit=60):
    n_in, n_out = len(args) - 1, len(outs)

    def kernel(info, *refs):
        given, results = refs[:n_in], refs[n_in : n_in + n_out]
        held = refs[n_in + n_out : 2 * (n_in + n_out)]
        extra, (in_sems, out_sems) = refs[2 * (n_in + n_out) : -2], refs[-2:]
        sources = []
        for index, (arg, ref) in enumerate(zip(args[1:], given)):
            where = arg.where(ref, info) if hasattr(arg, "where") else ref
            copy = pltpu.make_async_copy(where, held[index], in_sems.at[index])
            sources.append(Source(copy, held[index]))
        targets = []
        for index, ref in enumerate(results):
            copy = pltpu.make_async_copy(held[n_in + index], ref, out_sems.at[index])
            targets.append(Target(copy, held[n_in + index]))
        body(info, *sources, *targets, *extra)
        ready(*sources)
        send(*targets)
        for target in targets:
            target.copy.wait()

    arrays = [arg.array if hasattr(arg, "where") else arg for arg in args]
    buffers = [pltpu.VMEM(arg.shape, array.dtype) for arg, array in zip(args[1:], arrays[1:])]
    buffers += [pltpu.VMEM(shape, kind) for shape, kind in outs]
    call = pl.pallas_call(
        kernel,
        out_shape=[jax.ShapeDtypeStruct(shape, kind) for shape, kind in outs],
        in_specs=[pl.BlockSpec(memory_space=pltpu.SMEM)] + [pl.BlockSpec(memory_space=pl.ANY)] * n_in,
        out_specs=[pl.BlockSpec(memory_space=pl.ANY)] * n_out,
        scratch_shapes=buffers
        + [pltpu.VMEM(shape, kind) for shape, kind in scratch]
        + [pltpu.SemaphoreType.DMA((n_in,)), pltpu.SemaphoreType.DMA((n_out,))],
        compiler_params=pltpu.CompilerParams(vmem_limit_bytes=limit << 20),
        cost_estimate=pl.CostEstimate(flops=1, bytes_accessed=1, transcendentals=0),
        name=body.__name__.replace("_body", ""),
    )
    return list(call(*arrays))


def softmax_parts(scores):
    peak = functools.reduce(
        jnp.maximum, [jnp.max(part, axis=-1, keepdims=True) for part in scores]
    )
    grown = [jnp.exp(part - peak) for part in scores]
    total = functools.reduce(jnp.add, [jnp.sum(part, axis=-1, keepdims=True) for part in grown])
    inverse = 1.0 / total
    return [(part * inverse).astype(BF16) for part in grown], peak + jnp.log(total)


def state_fwd_body(info, query, pair_tok, attn, logsum):
    ready(query, pair_tok)
    for head in range(2):
        lanes = pl.ds(head * HD, HD)
        key, value = pair_tok[:, lanes], pair_tok[:, pl.ds(256 + head * HD, HD)]

        @pl.loop(0, 2)
        def _(b):
            here = pl.ds(pl.multiple_of(b * 256, 256), 256)
            scores = product_t(query[here, lanes], key) * SCALE
            (probs,), total = softmax_parts([scores])
            attn[here, lanes] = product(probs, value).astype(BF16)
            logsum[here, lanes] = jnp.broadcast_to(total, (256, HD))


def documents(info, positions):
    count, end = jnp.zeros_like(positions), 0
    for index in range(4):
        end = end + info[5 + index]
        count = count + (positions >= end).astype(jnp.int32)
    return count


def nearby_masks(info, first_row, rows):
    start = info[4] * W
    query_pos = start + first_row + lax.broadcasted_iota(jnp.int32, (rows, 1), 0)
    key_pos = start + lax.broadcasted_iota(jnp.int32, (1, W), 1)
    query_doc = documents(info, query_pos)
    prev = (key_pos >= W) & (documents(info, key_pos - W) == query_doc)
    own = (key_pos <= query_pos) & (documents(info, key_pos) == query_doc)
    return prev, own


def attend_body(info, *refs):
    mine, theirs, before, tokens, states = refs[:4], refs[4:8], refs[8:10], refs[10], refs[11]
    normed, query, pair_tok, pair_state, pair_prev, qkv_w, vectors = refs[12:19]
    attn, logsum, gains = refs[19:]
    y, z, core = info[1], info[2], info[3]
    for kz in range(4):
        for side, pieces in ((0, mine), (1, theirs)):
            for ky in range(4):
                shard = ((y + 4 - ky) & 3) * 8 + ((z + 4 - kz) & 3) * 2 + (core ^ side)
                rows = pl.ds(pl.multiple_of(shard * 32, 32), 32)
                qkv_w[rows, :] = pieces[kz][ky, :, :QKV]
                gains[rows, :] = pieces[kz][ky, :, QKV:]
    qkv_w.send()
    across = gains[...].astype(F32).T
    vectors[0:3, :] = across[0:3]
    vectors[3:4, :] = jax.nn.sigmoid(across[3:4])
    vectors[4:8, :] = jnp.zeros((4, D), F32)
    vectors.send()

    def normalized(values, lane):
        values = values.astype(F32)
        return (values * inv_rms(values) * vectors[lane : lane + 1, :]).astype(BF16)

    for part, (rows, pair) in enumerate(((tokens, pair_tok), (states, pair_state))):
        ready(rows)

        @pl.loop(0, 2)
        def _(b):
            here = pl.ds(pl.multiple_of(b * 256, 256), 256)
            there = pl.ds(pl.multiple_of(part * W + b * 256, 256), 256)
            normed[there, :] = normalized(rows[here, :], part)
            out = product(normed[there, :], qkv_w[...]).astype(BF16)
            query[there, :] = out[:, :256]
            pair[here, :] = out[:, 256:]

        pair.send()
    send(normed, query)
    for b, half in enumerate(before):
        here = pl.ds(pl.multiple_of(((info[0] + b) & 1) * 256, 256), 256)
        pair_prev[here, :] = product(normalized(half[...], 0), qkv_w[:, 256:]).astype(BF16)
    pair_prev.send()

    for head in range(2):
        lanes = pl.ds(head * HD, HD)
        far = pl.ds(256 + head * HD, HD)

        @pl.loop(0, 2)
        def _(b):
            here = pl.ds(pl.multiple_of(b * 256, 256), 256)
            prev, own = nearby_masks(info, b * 256, 256)
            rows = query[here, lanes]
            scores = [
                jnp.where(prev, product_t(rows, pair_prev[:, lanes]) * SCALE, NEG),
                jnp.where(own, product_t(rows, pair_tok[:, lanes]) * SCALE, NEG),
                product_t(rows, pair_state[:, lanes]) * SCALE,
            ]
            probs, total = softmax_parts(scores)
            out = (
                product(probs[0], pair_prev[:, far])
                + product(probs[1], pair_tok[:, far])
                + product(probs[2], pair_state[:, far])
            )
            attn[here, lanes] = out.astype(BF16)
            logsum[here, lanes] = jnp.broadcast_to(total, (256, HD))


def state_mix_body(info, outs, output_w, states, vectors, updated, attn):
    ready(outs, output_w, states, vectors)
    for k in range(4):
        attn[:, pl.ds(256 * k, 256)] = outs[(info[0] + 4 - k) & 3]
    forget = vectors[3:4, :]

    @pl.loop(0, 2)
    def _(b):
        here = pl.ds(pl.multiple_of(b * 256, 256), 256)
        mixed = product_t(attn[here, :], output_w[...])
        given = states[here, :].astype(F32)
        updated[here, :] = (given * forget + mixed * (1.0 - forget)).astype(BF16)


def forward_body(info, *refs):
    outs = refs[:4]
    tokens, vectors, output_w, down_w, grad_out, gate_w, up_w = refs[4:11]
    resid, ff_in, hidden, d_gate_up = refs[11:15]
    blocks = refs[15:19]
    d_ff_in, attn, values = refs[19:]
    for k in range(4):
        attn[:, pl.ds(256 * k, 256)] = outs[k][...]
    ready(tokens, vectors, output_w)
    for c in range(2):
        at = pl.ds(c * 512, 512)
        values[:, at] = tokens[:, at].astype(F32) + product_t(attn[...], output_w[at, :])

    @pl.loop(0, 4)
    def _(b):
        here = pl.ds(pl.multiple_of(b * 128, 128), 128)
        rows = values[here, :]
        ff_in[here, :] = (rows * inv_rms(rows) * vectors[2:3, :]).astype(BF16)

    ff_in.send()
    resid[...] = values[block_rows(info[0], 0), :]
    resid.send()
    for c in range(2):
        at, beyond = pl.ds(c * 512, 512), pl.ds(D + c * 512, 512)
        d_hidden = product(grad_out[...], down_w[:, at])
        gate = product(ff_in[...], gate_w[:, at])
        up = product(ff_in[...], up_w[:, at])
        sigma = jax.nn.sigmoid(gate)
        active = gate * sigma
        hidden[:, at] = (active * up).astype(BF16)
        d_gate = d_hidden * up * sigma * (1.0 + gate * (1.0 - sigma))
        d_gate_up[:, at] = d_gate.astype(BF16)
        d_gate_up[:, beyond] = (d_hidden * active).astype(BF16)
    send(hidden, d_gate_up)
    for c in range(2):
        at = pl.ds(c * 512, 512)
        d_ff_in[:, at] = (
            product_t(d_gate_up[:, :D], gate_w[at, :]) + product_t(d_gate_up[:, D:], up_w[at, :])
        ).astype(BF16)
    for k in range(4):
        blocks[k][...] = d_ff_in[block_rows(info[0], k), :]
        blocks[k].send()


def forward_out_body(info, hidden, down_w, d_mix, *refs):
    shared, out = refs[:4], refs[4]
    ready(hidden, down_w)
    for c in range(4):
        at = pl.ds(c * 256, 256)
        out[:, at] = product_t(hidden[...], down_w[at, :]).astype(BF16)
    for k in range(4):
        shared[k][:BLOCK, :] = out[block_rows(info[0], k), :]
        shared[k][BLOCK:, :] = d_mix[...]


def resid_back_body(info, *refs):
    pieces, resid, vectors, grad_out, output_w = refs[:4], refs[4], refs[5], refs[6], refs[7]
    d_resid, d_forward, d_mix = refs[8:11]
    blocks = refs[11:]
    grad, values = total_of(pieces), resid[...]
    scale = inv_rms(values)
    total = grad_out[block_rows(info[0], 0), :].astype(F32) + norm_back(values, scale, vectors[2:3, :], grad)
    rounded = total.astype(BF16)
    for k in range(4):
        at = pl.ds(256 * ((4 - k) % 4), 256)
        blocks[k][...] = product(rounded, output_w[:, at]).astype(BF16)
    d_mix[...] = rounded
    d_resid[...] = total
    d_forward[...] = jnp.sum(grad * values * scale, axis=0, keepdims=True)


def part_back(query, turned_query, key, value, d_out, turned_d_out, logsum, center, mask):
    scores = product_t(query, key) * SCALE
    if mask is not None:
        scores = jnp.where(mask, scores, NEG)
    probs = jnp.exp(scores - logsum)
    d_probs = product_t(d_out, value)
    d_scores = (probs * (d_probs - center)).astype(BF16)
    d_query = product(d_scores, key) * SCALE
    d_key = product(turned_query, d_scores) * SCALE
    d_value = product(turned_d_out, probs.astype(BF16))
    return d_query, d_key.T, d_value.T


def turned(values):
    return values.astype(F32).T.astype(BF16)


def center_of(d_out, out):
    return jnp.sum(d_out.astype(F32) * out.astype(F32), axis=-1, keepdims=True)


def state_back_body(
    info, output_w, vectors, grad_new, states, attn, query, pair_tok, logsum, *refs
):
    d_mix, d_query, d_pair, d_forget, d_attn = refs
    ready(output_w, vectors, grad_new, attn)
    forget = vectors[3:4, :]
    own = block_rows(info[0], 0)
    d_forget[...] = jnp.sum(
        grad_new[own, :].astype(F32) * states[own, :].astype(F32), axis=0, keepdims=True
    )

    @pl.loop(0, 2)
    def _(b):
        here = pl.ds(pl.multiple_of(b * 256, 256), 256)
        grad = grad_new[here, :].astype(F32)
        rounded = (grad * (1.0 - forget)).astype(BF16)
        d_mix[here, :] = rounded
        d_attn[here, :] = product(rounded, output_w[...]).astype(BF16)
        mixed = product_t(attn[here, :], output_w[...])
        d_forget[...] -= jnp.sum(grad * mixed, axis=0, keepdims=True)

    d_mix.send()
    d_forget[...] *= forget * (1.0 - forget)
    for head in range(2):
        lanes = pl.ds(head * HD, HD)
        far = pl.ds(256 + head * HD, HD)
        rows, d_out = query[:, lanes], d_attn[:, lanes]
        center = center_of(d_out, attn[:, lanes])
        total = logsum[:, pl.ds(head * HD, 1)]
        d_rows, d_key, d_value = part_back(
            rows, turned(rows), pair_tok[:, lanes], pair_tok[:, far], d_out, turned(d_out),
            total, center, None,
        )
        d_query[:, lanes] = d_rows.astype(BF16)
        d_pair[:, lanes] = d_key
        d_pair[:, far] = d_value


def prev_back_body(info, *refs):
    pieces, query, pair_prev, attn, logsum = refs[:4], refs[4], refs[5], refs[6], refs[7]
    d_pair, d_query, d_attn = refs[8:]
    for k in range(4):
        d_attn[block_rows(info[0], k), :] = pieces[k][...]
    d_attn.send()
    prev, _ = nearby_masks(info, 0, W)
    for head in range(2):
        lanes = pl.ds(head * HD, HD)
        far = pl.ds(256 + head * HD, HD)
        rows, d_out = query[:, lanes], d_attn[:, lanes]
        center = center_of(d_out, attn[:, lanes])
        total = logsum[:, pl.ds(head * HD, 1)]
        d_rows, d_key, d_value = part_back(
            rows, turned(rows), pair_prev[:, lanes], pair_prev[:, far], d_out, turned(d_out),
            total, center, prev,
        )
        d_query[:, lanes] = d_rows
        d_pair[:, lanes] = d_key.astype(BF16)
        d_pair[:, far] = d_value.astype(BF16)


def rows_back(info, given, qkv_w, d_qkv, d_gain, blocks):
    d_gain[...] = jnp.zeros(d_gain.shape, F32)
    for k in range(4):
        rows = block_rows(info[0], k)
        grad = product_t(d_qkv[rows, :], qkv_w[...])
        values = given[rows, :].astype(F32)
        d_gain[...] += jnp.sum(grad * values * inv_rms(values), axis=0, keepdims=True)
        blocks[k][...] = grad.astype(BF16)
        blocks[k].send()


def own_back_body(
    info, query, pair_state, d_attn, attn, logsum, pair_tok, d_query_part, d_pair_more,
    d_query_state, qkv_w, states, *refs,
):
    d_query, d_pair_tok, d_qkv, d_gain = refs[:4]
    blocks = refs[4:]
    _, own = nearby_masks(info, 0, W)
    for head in range(2):
        lanes = pl.ds(head * HD, HD)
        far = pl.ds(256 + head * HD, HD)
        rows, d_out = query[:, lanes], d_attn[:, lanes]
        rows_t, d_out_t = turned(rows), turned(d_out)
        center = center_of(d_out, attn[:, lanes])
        total = logsum[:, pl.ds(head * HD, 1)]
        more, d_key, d_value = part_back(
            rows, rows_t, pair_state[:, lanes], pair_state[:, far], d_out, d_out_t, total, center,
            None,
        )
        d_qkv[:, pl.ds(256 + head * HD, HD)] = d_key.astype(BF16)
        d_qkv[:, pl.ds(512 + head * HD, HD)] = d_value.astype(BF16)
        d_rows, d_key, d_value = part_back(
            rows, rows_t, pair_tok[:, lanes], pair_tok[:, far], d_out, d_out_t, total, center, own
        )
        d_pair_tok[:, lanes] = d_key + d_pair_more[:, lanes]
        d_pair_tok[:, far] = d_value + d_pair_more[:, far]
        d_query[:, lanes] = (d_query_part[:, lanes] + d_rows + more).astype(BF16)
    send(d_pair_tok, d_query)
    d_qkv[:, :256] = d_query_state[...]
    d_qkv.send()

    rows_back(info, states, qkv_w, d_qkv, d_gain, blocks)


def token_rows_body(
    info, d_query, d_pair, d_pair_back, qkv_w, tokens, d_state, d_forward, d_forget, d_qkv, *refs
):
    blocks, d_gain = refs[:4], refs[4]
    d_qkv[:, :256] = d_query[...]
    d_qkv[:, 256:] = (d_pair[...] + d_pair_back[...].astype(F32)).astype(BF16)
    tops = [Held(block.ref.at[pl.ds(0, BLOCK), :]) for block in blocks]
    rows_back(info, tokens, qkv_w, d_qkv, d_gain, tops)
    gains = jnp.concatenate(
        [d_gain[...], d_state[...], d_forward[...], d_forget[...], jnp.zeros((12, D), F32)], axis=0
    ).astype(BF16)
    for block in blocks:
        block[BLOCK:, :] = gains


def attn_grads_body(
    info, normed, d_qkv_tok, d_qkv_state, d_mix_state, attn_tok, attn_state, *refs
):
    shared, keep, give, whole = refs[:4], refs[4], refs[5], refs[6]
    for k in range(4):
        whole[block_rows(info[0], 4 - k), :] = shared[k][BLOCK:, :]
    first = info[3] == 0
    ready(normed, d_qkv_tok, d_qkv_state, d_mix_state, attn_tok, attn_state)

    @pl.loop(0, 4)
    def _(c):
        at = pl.ds(pl.multiple_of(c * 256, 256), 256)
        groups = pl.ds(pl.multiple_of(c * 4, 4), 4)
        sums = (
            outer_sum(normed[:W, at], d_qkv_tok[...]) + outer_sum(normed[W:, at], d_qkv_state[...]),
            outer_sum(whole[:, at], attn_tok[...]) + outer_sum(d_mix_state[:, at], attn_state[...]),
        )
        for part, lanes in zip(sums, (pl.ds(0, QKV), pl.ds(QKV, 256))):
            split = part.astype(BF16).reshape(4, 2, 32, part.shape[1])
            even, odd = split[:, 0], split[:, 1]
            keep[groups, :, lanes] = jnp.where(first, even, odd)
            give[groups, :, lanes] = jnp.where(first, odd, even)


def scatter_z_body(info, keep, came, gains, *refs):
    pieces, rows, across = refs[:4], refs[4], refs[5]
    rows[...] = jnp.zeros_like(rows)
    rows[0:8, :] = gains[...]
    rows[8:16, :] = gains[...]
    across[...] = rows[...].T
    near = lax.broadcasted_iota(jnp.int32, (32, 128), 1) < 8
    for k in range(4):
        z = (info[2] + k) & 3
        for y in range(4):
            group = y * 4 + z
            pieces[k][y, :, :D] = (keep[group].astype(F32) + came[group].astype(F32)).astype(BF16)
            own = across[pl.ds(pl.multiple_of((group * 2 + info[3]) * 32, 32), 32), :]
            other = across[pl.ds(pl.multiple_of((group * 2 + 1 - info[3]) * 32, 32), 32), :]
            pieces[k][y, :, D:] = jnp.where(near, own, other).astype(BF16)
        pieces[k].send()


def scatter_y_body(info, *refs):
    pieces, outs = refs[:4], refs[4:]
    for k in range(4):
        y = (info[1] + k) & 3
        total = pieces[0][y].astype(F32)
        for piece in pieces[1:]:
            total = total + piece[y].astype(F32)
        outs[k][...] = total.astype(BF16)


def scatter_end_body(info, *refs):
    total = total_of(refs[:4])
    d_query, d_key, d_value, d_output, d_vectors = refs[4:]
    d_query[...] = total[:, :256]
    d_key[...] = total[:, 256:512]
    d_value[...] = total[:, 512:768]
    d_output[...] = total[:, 768:1024]
    d_vectors[...] = total[:, 1024:].T[:16]


def ends_body(info, *refs):
    from_states, shared, resid, states, grad_new, vectors, tokens, d_resid, from_tokens = (
        refs[:4], refs[4:8], refs[8], refs[9], refs[10], refs[11], refs[12], refs[13], refs[14:18],
    )
    d_own, result, gains = refs[18:]
    values = states[...].astype(F32)
    d_own[BLOCK:, :] = (
        grad_new[...].astype(F32) * vectors[3:4, :]
        + norm_back(values, inv_rms(values), vectors[1:2, :], total_of(from_states))
    ).astype(BF16)
    values = tokens[...].astype(F32)
    total = total_of(from_tokens)
    d_own[:BLOCK, :] = (
        d_resid[...] + norm_back(values, inv_rms(values), vectors[0:1, :], total[:BLOCK])
    ).astype(BF16)
    gains[...] = total[BLOCK : BLOCK + 8]
    result[...] = (resid[...] + total_of(shared)).astype(BF16)


def collect_body(info, own, left, right, far_tok, far_state, d_tokens, d_states):
    for k, piece in ((0, own), (1, left), (3, right)):
        rows = block_rows(info[0], k)
        d_tokens[rows, :] = piece[:BLOCK, :].astype(F32)
        d_states[rows, :] = piece[BLOCK:, :].astype(F32)
    rows = block_rows(info[0], 2)
    d_tokens[rows, :] = far_tok[...].astype(F32)
    d_states[rows, :] = far_state[...].astype(F32)


def local(
    tokens,
    states,
    doc_lengths,
    w_query,
    w_key,
    w_value,
    w_output,
    w_gate,
    w_up,
    w_down,
    attention_gain,
    state_gain,
    forward_gain,
    forget_bias,
    d_output,
    d_new_states,
):
    place = lax.axis_index("mp")
    y = lax.axis_index("dp")
    z, core = lax.axis_index("z"), lax.axis_index("core")
    info = jnp.concatenate(
        [jnp.stack([place, y, z, core, 2 * z + core]), doc_lengths[0]]
    ).astype(jnp.int32)
    tokens, states = tokens[0], states[0, 0]
    grad_out, grad_new = d_output[0], d_new_states[0, 0]
    gains = jnp.stack([attention_gain, state_gain, forward_gain, forget_bias], axis=1)
    gains = jnp.pad(gains, ((0, 0), (0, 124)))
    packed = jnp.concatenate([w_query, w_key, w_value, gains], axis=1)
    output_shard = w_output.T
    late_shard = jnp.concatenate(
        [w_gate, w_up, w_down.T] + sent_on([output_shard] * 4), axis=1
    )
    late_w = lax.all_gather(late_shard, PLANE, axis=0, tiled=True)
    half = lax.dynamic_slice_in_dim(tokens, (place % 2) * 256, 256, 0)
    half = passed_along(half, 1)
    before = [half, lax.ppermute(half, "mp", [(0, 1), (1, 0), (2, 3), (3, 2)])]
    packed = jnp.stack([after(packed, half)] + [shifted(packed, "dp", k) for k in (1, 2, 3)])
    mine = [packed] + [shifted(packed, "z", k) for k in (1, 2, 3)]
    theirs = [other_core(piece) for piece in mine]

    normed, query, pair_tok, pair_state, pair_prev, qkv_w, vectors, attn_tok, sums_tok = run_early(
        attend_body,
        [
            ((2 * W, D), BF16), ((2 * W, 256), BF16), ((W, 512), BF16), ((W, 512), BF16),
            ((W, 512), BF16), ((D, QKV), BF16), ((8, D), F32), ((W, 256), BF16), ((W, 256), F32),
        ],
        [info] + mine + theirs + before + [tokens, states],
        [((D, 128), BF16)],
    )
    query_tok, query_state = Rows(query, 0, W), Rows(query, W, NS)
    attn_state, sums_state = run(
        state_fwd_body, [((NS, 256), BF16), ((NS, 256), F32)],
        [info, query_state, pair_tok],
    )
    outs_tok = sent_on([attn_tok] * 4)
    outs_state = lax.all_gather(after(attn_state, late_w[0]), "mp", axis=0)
    output_w, own_output_w = Part(late_w, D, 3), Part(late_w, 256, 12)
    down_w = Part(late_w, D, 2)
    d_mix_state, d_query_state, d_pair_more, d_forget = run(
        state_back_body,
        [((NS, D), BF16), ((NS, 256), BF16), ((NS, 512), F32), ((1, D), F32)],
        [
            info, own_output_w, vectors, grad_new, states, attn_state, query_state, pair_tok,
            sums_state,
        ],
        [((NS, 256), BF16)],
    )
    outs_tok[0] = after(outs_tok[0], d_query_state)
    resid, ff_in, hidden, d_gate_up, *blocks = run_early(
        forward_body,
        [((BLOCK, D), F32), ((W, D), BF16), ((W, D), BF16), ((W, 2 * D), BF16)]
        + [((BLOCK, D), BF16)] * 4,
        [info] + outs_tok
        + [tokens, vectors, output_w, down_w, grad_out, Part(late_w, D, 0), Part(late_w, D, 1)],
        [((W, D), BF16), ((W, D), BF16), ((W, D), F32)],
    )
    pieces = sent_back(blocks)

    d_ff_w = jnp.concatenate(
        [outer_sum(ff_in, d_gate_up).astype(BF16), outer_sum(grad_out, hidden).astype(BF16)], axis=1
    )
    pieces[0] = after(pieces[0], d_ff_w)
    d_ff_w = after(d_ff_w, *pieces[1:])
    d_ff_w = lax.psum_scatter(d_ff_w, PLANE, scatter_dimension=0, tiled=True).astype(F32)

    d_resid, d_forward, d_mix_own, *blocks = run(
        resid_back_body,
        [((BLOCK, D), F32), ((1, D), F32), ((BLOCK, D), BF16)] + [((BLOCK, 256), BF16)] * 4,
        [info] + pieces + [resid, vectors, grad_out, output_w],
    )
    pieces = sent_on(blocks)
    blocks = run(
        forward_out_body, [((2 * BLOCK, D), BF16)] * 4, [info, hidden, down_w, d_mix_own],
        [((W, D), BF16)],
    )
    pieces[0] = after(pieces[0], blocks[0])
    shared = sent_back([after(block, *pieces[1:]) for block in blocks])

    d_pair_prev, d_query_part, d_attn_tok = run(
        prev_back_body,
        [((W, 512), BF16), ((W, 256), F32), ((W, 256), BF16)],
        [info] + pieces + [query_tok, pair_prev, attn_tok, sums_tok],
    )
    d_pair_back = passed_along(d_pair_prev, -1)
    d_query_tok, d_pair_tok, d_qkv_state, d_state_gain, *blocks = run_early(
        own_back_body,
        [((W, 256), BF16), ((W, 512), F32), ((NS, QKV), BF16), ((1, D), F32)]
        + [((BLOCK, D), BF16)] * 4,
        [
            info, query_tok, pair_state, d_attn_tok, attn_tok, sums_tok, pair_tok, d_query_part,
            d_pair_more, d_query_state, qkv_w, states,
        ],
    )
    pieces_state = sent_back(blocks)
    d_pair_back = after(d_pair_back, d_state_gain, *shared[1:])
    d_qkv_tok, *blocks = run(
        token_rows_body,
        [((W, QKV), BF16)] + [((BLOCK + 16, D), BF16)] * 4,
        [
            info, d_query_tok, d_pair_tok, d_pair_back, qkv_w, tokens, d_state_gain, d_forward,
            d_forget,
        ],
        [((1, D), F32)],
    )
    pieces_tok = sent_back([after(block, *pieces_state[1:]) for block in blocks])

    keep, give = run(
        attn_grads_body,
        [((16, 32, D), BF16)] * 2,
        [
            info, normed, d_qkv_tok, d_qkv_state, d_mix_state, attn_tok,
            attn_state,
        ]
        + shared,
        [((W, D), BF16)],
    )
    own_tokens, own_states, own_grad_new = [
        lax.dynamic_slice_in_dim(rows, place * BLOCK, BLOCK, 0)
        for rows in (after(tokens, give), states, grad_new)
    ]
    d_own, result, d_gains = run(
        ends_body,
        [((2 * BLOCK, D), BF16), ((BLOCK, D), BF16), ((8, D), F32)],
        [info, after(pieces_state[0], give)] + pieces_state[1:]
        + [Rows(piece, 0, BLOCK) for piece in shared]
        + [resid, own_states, own_grad_new, vectors, own_tokens, d_resid] + pieces_tok,
    )
    came = other_core(after(give, d_own))
    result = lax.all_gather(result, "mp", axis=0, tiled=True)
    left, right = shifted_x(d_own, 1), shifted_x(d_own, -1)
    shards = run(
        scatter_z_body, [((4, 32, PACK), BF16)] * 4, [info, keep, came, d_gains],
        [((128, D), F32), ((D, 128), F32)], limit=12,
    )
    sent = shards[0]
    (updated,) = run(
        state_mix_body, [((NS, D), BF16)],
        [info, outs_state, Part(after(late_w, sent), D, 3), states, vectors],
        [((NS, D), BF16)],
    )
    shards = [shards[0]] + [shifted(after(shards[k], updated), "z", k) for k in (1, 2, 3)]
    far_tok, far_state = shifted_x(left[:BLOCK], 1), shifted_x(right[BLOCK:], -1)
    d_gate_w, d_up_w, d_down_w = d_ff_w[:, :D], d_ff_w[:, D : 2 * D], d_ff_w[:, 2 * D :].T
    shards[0] = after(shards[0], d_gate_w, d_up_w, d_down_w)
    shards = run(scatter_y_body, [((32, PACK), BF16)] * 4, [info] + shards, limit=6)
    shards = [shards[0]] + [shifted(shards[k], "dp", k) for k in (1, 2, 3)]
    d_tokens, d_states = run(
        collect_body, [((W, D), F32)] * 2,
        [info, after(d_own, shards[0]), left, right, far_tok, far_state],
    )
    shards[0] = after(shards[0], d_states)
    d_query_w, d_key_w, d_value_w, d_output_w, d_vectors = run(
        scatter_end_body, [((32, 256), F32)] * 4 + [((16, 32), F32)], [info] + shards, limit=6)
    d_vectors = d_vectors[:4] + other_core(d_vectors[8:12])
    return (
        result[None],
        updated[None, None],
        d_tokens[None],
        d_states[None, None],
        d_query_w,
        d_key_w,
        d_value_w,
        d_output_w.T,
        d_gate_w,
        d_up_w,
        d_down_w,
        d_vectors[0],
        d_vectors[1],
        d_vectors[2],
        d_vectors[3],
    )


def solution(mesh):
    plane = PLANE
    mesh = Mesh(mesh.devices.reshape(4, 4, 2, 4), PLANE + ("mp",))
    placed = (
        P("dp", SEQ, None),
        P("dp", SEQ, None, None),
        P("dp", None),
        P(plane, "mp"),
        P(plane, "mp"),
        P(plane, "mp"),
        P("mp", plane),
        P(plane, "mp"),
        P(plane, "mp"),
        P("mp", plane),
        P(plane),
        P(plane),
        P(plane),
        P(plane),
        P("dp", SEQ, None),
        P("dp", SEQ, None, None),
    )
    return jax.shard_map(
        local,
        mesh=mesh,
        in_specs=placed,
        out_specs=(
            P("dp", SEQ, None),
            P("dp", SEQ, None, None),
            P("dp", SEQ, None),
            P("dp", SEQ, None, None),
            P(plane, "mp"),
            P(plane, "mp"),
            P(plane, "mp"),
            P("mp", plane),
            P(plane, "mp"),
            P(plane, "mp"),
            P("mp", plane),
            P(plane),
            P(plane),
            P(plane),
            P(plane),
        ),
        check_vma=False,
    )
```

```python
import functools

import jax
import jax.numpy as jnp
from jax import lax
from jax.experimental import pallas as pl
from jax.experimental.pallas import tpu as pltpu
from jax.sharding import Mesh
from jax.sharding import PartitionSpec as P

D = 1024
HD = 128
W = 512
NS = 512
PARTS = 4
BLOCK = W // PARTS
QKV = 768
PACK = 1152
SHARD = 896
SCALE = HD ** (-0.5)


EPS = 1e-05
NEG = -1e30
BF16, F32 = jnp.bfloat16, jnp.float32


SEQ = ("z", "core")
CHIPS = ("dp", "z")
PLANE = ("dp", "z", "core")


def passed_along(value, steps):
    count = lax.axis_size(SEQ)
    leading, last = (max(0, -steps), min(count, count - steps))
    return lax.ppermute(value, SEQ, [(source, source + steps) for source in range(leading, last)])


def shifted_x(value, steps):
    return lax.ppermute(value, "mp", [(i, (i + steps) % PARTS) for i in range(PARTS)])


def shifted(value, axis, steps):
    return lax.ppermute(value, axis, [(i, (i + steps) % 4) for i in range(4)])


def other_core(value):
    return lax.ppermute(value, "core", [(0, 1), (1, 0)])


def sent_back(blocks):
    return [blocks[0]] + [shifted_x(blocks[k], -k) for k in (1, 2, 3)]


def sent_on(blocks):
    return [blocks[0]] + [shifted_x(blocks[k], k) for k in (1, 2, 3)]


def product(left, right):
    return jnp.dot(left, right, preferred_element_type=F32)


def product_t(left, right):
    return lax.dot_general(left, right, (((1,), (1,)), ((), ())), preferred_element_type=F32)


def outer_sum(left, right):
    return lax.dot_general(left, right, (((0,), (0,)), ((), ())), preferred_element_type=F32)


def inv_rms(values):
    return lax.rsqrt(jnp.mean(values * values, axis=-1, keepdims=True) + EPS)


def norm_back(values, scale, gain, grad):
    inner = grad * gain
    along = jnp.mean(inner * values, axis=-1, keepdims=True)
    return scale * inner - values * (scale * scale * scale) * along


def block_rows(place, k):
    return pl.ds(pl.multiple_of(((place + PARTS - k) & 3) * BLOCK, BLOCK), BLOCK)


def total_of(pieces):
    total = pieces[0][...].astype(F32)
    for piece in pieces[1:]:
        total = total + piece[...].astype(F32)
    return total


def after(value, *others):
    return lax.optimization_barrier((value, *others))[0]


class Part:
    def __init__(self, array, width, index):
        self.array, self.shape = array, (array.shape[0], width)
        self.where = lambda ref, info: ref.at[:, pl.ds(index * width, width)]
        self.block = lambda _: (0, index)


class Rows:
    def __init__(self, array, start, size):
        self.array, self.shape = array, (size, array.shape[1])
        self.where = lambda ref, info: ref.at[pl.ds(start, size), :]
        self.block = lambda _: (start // size, 0)


class Source:
    def __init__(self, copy, ref):
        self.copy, self.ref = copy, ref
        copy.start()

    def ready(self):
        if self.copy is not None:
            self.copy.wait()
            self.copy = None
        return self.ref

    def __getitem__(self, index):
        return self.ready()[index]


class Target:
    def __init__(self, copy, ref):
        self.copy, self.ref, self.sent = copy, ref, False
        self.shape, self.dtype = ref.shape, ref.dtype

    def send(self):
        if not self.sent:
            self.copy.start()
            self.sent = True

    def __getitem__(self, index):
        return self.ref[index]

    def __setitem__(self, index, value):
        self.ref[index] = value


class Held:
    def __init__(self, ref):
        self.ref, self.shape, self.dtype = ref, ref.shape, ref.dtype

    def ready(self):
        return self.ref

    def send(self):
        pass

    def __getitem__(self, index):
        return self.ref[index]

    def __setitem__(self, index, value):
        self.ref[index] = value


def ready(*sources):
    for source in sources:
        source.ready()


def send(*targets):
    for target in targets:
        target.send()


def run(body, outs, args, scratch=(), limit=60):
    n_refs = len(args) - 1 + len(outs)

    def kernel(info, *refs):
        body(info, *[Held(ref) for ref in refs[:n_refs]], *refs[n_refs:])

    def spec(arg):
        if hasattr(arg, "block"):
            return pl.BlockSpec(arg.shape, arg.block)
        return pl.BlockSpec(arg.shape, lambda _: (0,) * len(arg.shape))

    call = pl.pallas_call(
        kernel,
        out_shape=[jax.ShapeDtypeStruct(shape, kind) for shape, kind in outs],
        grid=(1,),
        in_specs=[pl.BlockSpec(memory_space=pltpu.SMEM)] + [spec(arg) for arg in args[1:]],
        out_specs=[spec(jax.ShapeDtypeStruct(shape, kind)) for shape, kind in outs],
        scratch_shapes=[pltpu.VMEM(shape, kind) for shape, kind in scratch],
        compiler_params=pltpu.CompilerParams(vmem_limit_bytes=limit << 20),
        cost_estimate=pl.CostEstimate(flops=1, bytes_accessed=1, transcendentals=0),
        name=body.__name__.replace("_body", ""),
    )
    return list(call(*[arg.array if hasattr(arg, "block") else arg for arg in args]))


def run_early(body, outs, args, scratch=(), limit=60):
    n_in, n_out = len(args) - 1, len(outs)

    def kernel(info, *refs):
        given, results = refs[:n_in], refs[n_in : n_in + n_out]
        held = refs[n_in + n_out : 2 * (n_in + n_out)]
        extra, (in_sems, out_sems) = refs[2 * (n_in + n_out) : -2], refs[-2:]
        sources = []
        for index, (arg, ref) in enumerate(zip(args[1:], given)):
            where = arg.where(ref, info) if hasattr(arg, "where") else ref
            copy = pltpu.make_async_copy(where, held[index], in_sems.at[index])
            sources.append(Source(copy, held[index]))
        targets = []
        for index, ref in enumerate(results):
            copy = pltpu.make_async_copy(held[n_in + index], ref, out_sems.at[index])
            targets.append(Target(copy, held[n_in + index]))
        body(info, *sources, *targets, *extra)
        ready(*sources)
        send(*targets)
        for target in targets:
            target.copy.wait()

    arrays = [arg.array if hasattr(arg, "where") else arg for arg in args]
    buffers = [pltpu.VMEM(arg.shape, array.dtype) for arg, array in zip(args[1:], arrays[1:])]
    buffers += [pltpu.VMEM(shape, kind) for shape, kind in outs]
    call = pl.pallas_call(
        kernel,
        out_shape=[jax.ShapeDtypeStruct(shape, kind) for shape, kind in outs],
        in_specs=[pl.BlockSpec(memory_space=pltpu.SMEM)] + [pl.BlockSpec(memory_space=pl.ANY)] * n_in,
        out_specs=[pl.BlockSpec(memory_space=pl.ANY)] * n_out,
        scratch_shapes=buffers
        + [pltpu.VMEM(shape, kind) for shape, kind in scratch]
        + [pltpu.SemaphoreType.DMA((n_in,)), pltpu.SemaphoreType.DMA((n_out,))],
        compiler_params=pltpu.CompilerParams(vmem_limit_bytes=limit << 20),
        cost_estimate=pl.CostEstimate(flops=1, bytes_accessed=1, transcendentals=0),
        name=body.__name__.replace("_body", ""),
    )
    return list(call(*arrays))


def softmax_parts(scores):
    peak = functools.reduce(
        jnp.maximum, [jnp.max(part, axis=-1, keepdims=True) for part in scores]
    )
    grown = [jnp.exp(part - peak) for part in scores]
    total = functools.reduce(jnp.add, [jnp.sum(part, axis=-1, keepdims=True) for part in grown])
    inverse = 1.0 / total
    return [(part * inverse).astype(BF16) for part in grown], peak + jnp.log(total)


def state_fwd_body(info, query, pair_tok, attn, logsum):
    ready(query, pair_tok)
    for head in range(2):
        lanes = pl.ds(head * HD, HD)
        key, value = pair_tok[:, lanes], pair_tok[:, pl.ds(256 + head * HD, HD)]

        @pl.loop(0, 2)
        def _(b):
            here = pl.ds(pl.multiple_of(b * 256, 256), 256)
            scores = product_t(query[here, lanes], key) * SCALE
            (probs,), total = softmax_parts([scores])
            attn[here, lanes] = product(probs, value).astype(BF16)
            logsum[here, lanes] = jnp.broadcast_to(total, (256, HD))


def documents(info, positions):
    count, end = jnp.zeros_like(positions), 0
    for index in range(4):
        end = end + info[5 + index]
        count = count + (positions >= end).astype(jnp.int32)
    return count


def nearby_masks(info, first_row, rows):
    start = info[4] * W
    query_pos = start + first_row + lax.broadcasted_iota(jnp.int32, (rows, 1), 0)
    key_pos = start + lax.broadcasted_iota(jnp.int32, (1, W), 1)
    query_doc = documents(info, query_pos)
    prev = (key_pos >= W) & (documents(info, key_pos - W) == query_doc)
    own = (key_pos <= query_pos) & (documents(info, key_pos) == query_doc)
    return prev, own


def attend_body(info, *refs):
    mine, theirs, before, tokens, states = refs[:4], refs[4:8], refs[8:10], refs[10], refs[11]
    normed, query, pair_tok, pair_state, pair_prev, qkv_w, vectors = refs[12:19]
    attn, logsum, gains = refs[19:]
    y, z, core = info[1], info[2], info[3]
    for kz in range(4):
        for side, pieces in ((0, mine), (1, theirs)):
            for ky in range(4):
                shard = ((y + 4 - ky) & 3) * 8 + ((z + 4 - kz) & 3) * 2 + (core ^ side)
                rows = pl.ds(pl.multiple_of(shard * 32, 32), 32)
                qkv_w[rows, :] = pieces[kz][ky, :, :QKV]
                gains[rows, :] = pieces[kz][ky, :, QKV:]
    qkv_w.send()
    across = gains[...].astype(F32).T
    vectors[0:3, :] = across[0:3]
    vectors[3:4, :] = jax.nn.sigmoid(across[3:4])
    vectors[4:8, :] = jnp.zeros((4, D), F32)
    vectors.send()

    def normalized(values, lane):
        values = values.astype(F32)
        return (values * inv_rms(values) * vectors[lane : lane + 1, :]).astype(BF16)

    for part, (rows, pair) in enumerate(((tokens, pair_tok), (states, pair_state))):
        ready(rows)

        @pl.loop(0, 2)
        def _(b):
            here = pl.ds(pl.multiple_of(b * 256, 256), 256)
            there = pl.ds(pl.multiple_of(part * W + b * 256, 256), 256)
            normed[there, :] = normalized(rows[here, :], part)
            out = product(normed[there, :], qkv_w[...]).astype(BF16)
            query[there, :] = out[:, :256]
            pair[here, :] = out[:, 256:]

        pair.send()
    send(normed, query)
    for b, half in enumerate(before):
        here = pl.ds(pl.multiple_of(((info[0] + b) & 1) * 256, 256), 256)
        pair_prev[here, :] = product(normalized(half[...], 0), qkv_w[:, 256:]).astype(BF16)
    pair_prev.send()

    for head in range(2):
        lanes = pl.ds(head * HD, HD)
        far = pl.ds(256 + head * HD, HD)

        @pl.loop(0, 2)
        def _(b):
            here = pl.ds(pl.multiple_of(b * 256, 256), 256)
            prev, own = nearby_masks(info, b * 256, 256)
            rows = query[here, lanes]
            scores = [
                jnp.where(prev, product_t(rows, pair_prev[:, lanes]) * SCALE, NEG),
                jnp.where(own, product_t(rows, pair_tok[:, lanes]) * SCALE, NEG),
                product_t(rows, pair_state[:, lanes]) * SCALE,
            ]
            probs, total = softmax_parts(scores)
            out = (
                product(probs[0], pair_prev[:, far])
                + product(probs[1], pair_tok[:, far])
                + product(probs[2], pair_state[:, far])
            )
            attn[here, lanes] = out.astype(BF16)
            logsum[here, lanes] = jnp.broadcast_to(total, (256, HD))


def state_mix_body(info, outs, output_w, states, vectors, updated, attn):
    ready(outs, output_w, states, vectors)
    for k in range(4):
        attn[:, pl.ds(256 * k, 256)] = outs[(info[0] + 4 - k) & 3]
    forget = vectors[3:4, :]

    @pl.loop(0, 2)
    def _(b):
        here = pl.ds(pl.multiple_of(b * 256, 256), 256)
        mixed = product_t(attn[here, :], output_w[...])
        given = states[here, :].astype(F32)
        updated[here, :] = (given * forget + mixed * (1.0 - forget)).astype(BF16)


def forward_body(info, *refs):
    outs = refs[:4]
    tokens, vectors, output_w, down_w, grad_out, gate_w, up_w = refs[4:11]
    resid, ff_in, hidden, d_gate_up = refs[11:15]
    blocks = refs[15:19]
    d_ff_in, attn, values = refs[19:]
    for k in range(4):
        attn[:, pl.ds(256 * k, 256)] = outs[k][...]
    ready(tokens, vectors, output_w)
    for c in range(2):
        at = pl.ds(c * 512, 512)
        values[:, at] = tokens[:, at].astype(F32) + product_t(attn[...], output_w[at, :])

    @pl.loop(0, 4)
    def _(b):
        here = pl.ds(pl.multiple_of(b * 128, 128), 128)
        rows = values[here, :]
        ff_in[here, :] = (rows * inv_rms(rows) * vectors[2:3, :]).astype(BF16)

    ff_in.send()
    resid[...] = values[block_rows(info[0], 0), :]
    resid.send()
    for c in range(2):
        at, beyond = pl.ds(c * 512, 512), pl.ds(D + c * 512, 512)
        d_hidden = product(grad_out[...], down_w[:, at])
        gate = product(ff_in[...], gate_w[:, at])
        up = product(ff_in[...], up_w[:, at])
        sigma = jax.nn.sigmoid(gate)
        active = gate * sigma
        hidden[:, at] = (active * up).astype(BF16)
        d_gate = d_hidden * up * sigma * (1.0 + gate * (1.0 - sigma))
        d_gate_up[:, at] = d_gate.astype(BF16)
        d_gate_up[:, beyond] = (d_hidden * active).astype(BF16)
    send(hidden, d_gate_up)
    for c in range(2):
        at = pl.ds(c * 512, 512)
        d_ff_in[:, at] = (
            product_t(d_gate_up[:, :D], gate_w[at, :]) + product_t(d_gate_up[:, D:], up_w[at, :])
        ).astype(BF16)
    for k in range(4):
        blocks[k][...] = d_ff_in[block_rows(info[0], k), :]
        blocks[k].send()


def forward_out_body(info, hidden, down_w, d_mix, *refs):
    shared, out = refs[:4], refs[4]
    ready(hidden, down_w)
    for c in range(4):
        at = pl.ds(c * 256, 256)
        out[:, at] = product_t(hidden[...], down_w[at, :]).astype(BF16)
    for k in range(4):
        shared[k][:BLOCK, :] = out[block_rows(info[0], k), :]
        shared[k][BLOCK:, :] = d_mix[...]


def resid_back_body(info, *refs):
    pieces, resid, vectors, grad_out, output_w = refs[:4], refs[4], refs[5], refs[6], refs[7]
    d_resid, d_forward, d_mix = refs[8:11]
    blocks = refs[11:]
    grad, values = total_of(pieces), resid[...]
    scale = inv_rms(values)
    total = grad_out[block_rows(info[0], 0), :].astype(F32) + norm_back(values, scale, vectors[2:3, :], grad)
    rounded = total.astype(BF16)
    for k in range(4):
        at = pl.ds(256 * ((4 - k) % 4), 256)
        blocks[k][...] = product(rounded, output_w[:, at]).astype(BF16)
    d_mix[...] = rounded
    d_resid[...] = total
    d_forward[...] = jnp.sum(grad * values * scale, axis=0, keepdims=True)


def part_back(query, turned_query, key, value, d_out, turned_d_out, logsum, center, mask):
    scores = product_t(query, key) * SCALE
    if mask is not None:
        scores = jnp.where(mask, scores, NEG)
    probs = jnp.exp(scores - logsum)
    d_probs = product_t(d_out, value)
    d_scores = (probs * (d_probs - center)).astype(BF16)
    d_query = product(d_scores, key) * SCALE
    d_key = product(turned_query, d_scores) * SCALE
    d_value = product(turned_d_out, probs.astype(BF16))
    return d_query, d_key.T, d_value.T


def turned(values):
    return values.astype(F32).T.astype(BF16)


def center_of(d_out, out):
    return jnp.sum(d_out.astype(F32) * out.astype(F32), axis=-1, keepdims=True)


def state_back_body(
    info, output_w, vectors, grad_new, states, attn, query, pair_tok, logsum, *refs
):
    d_mix, d_query, d_pair, d_forget, d_attn = refs
    ready(output_w, vectors, grad_new, attn)
    forget = vectors[3:4, :]
    own = block_rows(info[0], 0)
    d_forget[...] = jnp.sum(
        grad_new[own, :].astype(F32) * states[own, :].astype(F32), axis=0, keepdims=True
    )

    @pl.loop(0, 2)
    def _(b):
        here = pl.ds(pl.multiple_of(b * 256, 256), 256)
        grad = grad_new[here, :].astype(F32)
        rounded = (grad * (1.0 - forget)).astype(BF16)
        d_mix[here, :] = rounded
        d_attn[here, :] = product(rounded, output_w[...]).astype(BF16)
        mixed = product_t(attn[here, :], output_w[...])
        d_forget[...] -= jnp.sum(grad * mixed, axis=0, keepdims=True)

    d_mix.send()
    d_forget[...] *= forget * (1.0 - forget)
    for head in range(2):
        lanes = pl.ds(head * HD, HD)
        far = pl.ds(256 + head * HD, HD)
        rows, d_out = query[:, lanes], d_attn[:, lanes]
        center = center_of(d_out, attn[:, lanes])
        total = logsum[:, pl.ds(head * HD, 1)]
        d_rows, d_key, d_value = part_back(
            rows, turned(rows), pair_tok[:, lanes], pair_tok[:, far], d_out, turned(d_out),
            total, center, None,
        )
        d_query[:, lanes] = d_rows.astype(BF16)
        d_pair[:, lanes] = d_key
        d_pair[:, far] = d_value


def prev_back_body(info, *refs):
    pieces, query, pair_prev, attn, logsum = refs[:4], refs[4], refs[5], refs[6], refs[7]
    d_pair, d_query, d_attn = refs[8:]
    for k in range(4):
        d_attn[block_rows(info[0], k), :] = pieces[k][...]
    d_attn.send()
    prev, _ = nearby_masks(info, 0, W)
    for head in range(2):
        lanes = pl.ds(head * HD, HD)
        far = pl.ds(256 + head * HD, HD)
        rows, d_out = query[:, lanes], d_attn[:, lanes]
        center = center_of(d_out, attn[:, lanes])
        total = logsum[:, pl.ds(head * HD, 1)]
        d_rows, d_key, d_value = part_back(
            rows, turned(rows), pair_prev[:, lanes], pair_prev[:, far], d_out, turned(d_out),
            total, center, prev,
        )
        d_query[:, lanes] = d_rows
        d_pair[:, lanes] = d_key.astype(BF16)
        d_pair[:, far] = d_value.astype(BF16)


def rows_back(info, given, qkv_w, d_qkv, d_gain, blocks):
    d_gain[...] = jnp.zeros(d_gain.shape, F32)
    for k in range(4):
        rows = block_rows(info[0], k)
        grad = product_t(d_qkv[rows, :], qkv_w[...])
        values = given[rows, :].astype(F32)
        d_gain[...] += jnp.sum(grad * values * inv_rms(values), axis=0, keepdims=True)
        blocks[k][...] = grad.astype(BF16)
        blocks[k].send()


def own_back_body(
    info, query, pair_state, d_attn, attn, logsum, pair_tok, d_query_part, d_pair_more,
    d_query_state, qkv_w, states, *refs,
):
    d_query, d_pair_tok, d_qkv, d_gain = refs[:4]
    blocks = refs[4:]
    _, own = nearby_masks(info, 0, W)
    for head in range(2):
        lanes = pl.ds(head * HD, HD)
        far = pl.ds(256 + head * HD, HD)
        rows, d_out = query[:, lanes], d_attn[:, lanes]
        rows_t, d_out_t = turned(rows), turned(d_out)
        center = center_of(d_out, attn[:, lanes])
        total = logsum[:, pl.ds(head * HD, 1)]
        more, d_key, d_value = part_back(
            rows, rows_t, pair_state[:, lanes], pair_state[:, far], d_out, d_out_t, total, center,
            None,
        )
        d_qkv[:, pl.ds(256 + head * HD, HD)] = d_key.astype(BF16)
        d_qkv[:, pl.ds(512 + head * HD, HD)] = d_value.astype(BF16)
        d_rows, d_key, d_value = part_back(
            rows, rows_t, pair_tok[:, lanes], pair_tok[:, far], d_out, d_out_t, total, center, own
        )
        d_pair_tok[:, lanes] = d_key + d_pair_more[:, lanes]
        d_pair_tok[:, far] = d_value + d_pair_more[:, far]
        d_query[:, lanes] = (d_query_part[:, lanes] + d_rows + more).astype(BF16)
    send(d_pair_tok, d_query)
    d_qkv[:, :256] = d_query_state[...]
    d_qkv.send()

    rows_back(info, states, qkv_w, d_qkv, d_gain, blocks)


def token_rows_body(
    info, d_query, d_pair, d_pair_back, qkv_w, tokens, d_state, d_forward, d_forget, d_qkv, *refs
):
    blocks, d_gain = refs[:4], refs[4]
    d_qkv[:, :256] = d_query[...]
    d_qkv[:, 256:] = (d_pair[...] + d_pair_back[...].astype(F32)).astype(BF16)
    tops = [Held(block.ref.at[pl.ds(0, BLOCK), :]) for block in blocks]
    rows_back(info, tokens, qkv_w, d_qkv, d_gain, tops)
    gains = jnp.concatenate(
        [d_gain[...], d_state[...], d_forward[...], d_forget[...], jnp.zeros((12, D), F32)], axis=0
    ).astype(BF16)
    for block in blocks:
        block[BLOCK:, :] = gains


def attn_grads_body(
    info, normed, d_qkv_tok, d_qkv_state, d_mix_state, attn_tok, attn_state, *refs
):
    shared, keep, give, whole = refs[:4], refs[4], refs[5], refs[6]
    for k in range(4):
        whole[block_rows(info[0], 4 - k), :] = shared[k][BLOCK:, :]
    first = info[3] == 0
    ready(normed, d_qkv_tok, d_qkv_state, d_mix_state, attn_tok, attn_state)

    @pl.loop(0, 4)
    def _(c):
        at = pl.ds(pl.multiple_of(c * 256, 256), 256)
        groups = pl.ds(pl.multiple_of(c * 4, 4), 4)
        sums = (
            outer_sum(normed[:W, at], d_qkv_tok[...]) + outer_sum(normed[W:, at], d_qkv_state[...]),
            outer_sum(whole[:, at], attn_tok[...]) + outer_sum(d_mix_state[:, at], attn_state[...]),
        )
        for part, lanes in zip(sums, (pl.ds(0, QKV), pl.ds(QKV, 256))):
            split = part.astype(BF16).reshape(4, 2, 32, part.shape[1])
            even, odd = split[:, 0], split[:, 1]
            keep[groups, :, lanes] = jnp.where(first, even, odd)
            give[groups, :, lanes] = jnp.where(first, odd, even)


def scatter_z_body(info, keep, came, gains, *refs):
    pieces, rows, across = refs[:4], refs[4], refs[5]
    rows[...] = jnp.zeros_like(rows)
    rows[0:8, :] = gains[...]
    rows[8:16, :] = gains[...]
    across[...] = rows[...].T
    near = lax.broadcasted_iota(jnp.int32, (32, 128), 1) < 8
    for k in range(4):
        z = (info[2] + k) & 3
        for y in range(4):
            group = y * 4 + z
            pieces[k][y, :, :D] = (keep[group].astype(F32) + came[group].astype(F32)).astype(BF16)
            own = across[pl.ds(pl.multiple_of((group * 2 + info[3]) * 32, 32), 32), :]
            other = across[pl.ds(pl.multiple_of((group * 2 + 1 - info[3]) * 32, 32), 32), :]
            pieces[k][y, :, D:] = jnp.where(near, own, other).astype(BF16)
        pieces[k].send()


def scatter_y_body(info, *refs):
    pieces, outs = refs[:4], refs[4:]
    for k in range(4):
        y = (info[1] + k) & 3
        total = pieces[0][y].astype(F32)
        for piece in pieces[1:]:
            total = total + piece[y].astype(F32)
        outs[k][...] = total.astype(BF16)


def scatter_end_body(info, *refs):
    total = total_of(refs[:4])
    d_query, d_key, d_value, d_output, d_vectors = refs[4:]
    d_query[...] = total[:, :256]
    d_key[...] = total[:, 256:512]
    d_value[...] = total[:, 512:768]
    d_output[...] = total[:, 768:1024]
    d_vectors[...] = total[:, 1024:].T[:16]


def ends_body(info, *refs):
    from_states, shared, resid, states, grad_new, vectors, tokens, d_resid, from_tokens = (
        refs[:4], refs[4:8], refs[8], refs[9], refs[10], refs[11], refs[12], refs[13], refs[14:18],
    )
    d_own, result, gains = refs[18:]
    values = states[...].astype(F32)
    d_own[BLOCK:, :] = (
        grad_new[...].astype(F32) * vectors[3:4, :]
        + norm_back(values, inv_rms(values), vectors[1:2, :], total_of(from_states))
    ).astype(BF16)
    values = tokens[...].astype(F32)
    total = total_of(from_tokens)
    d_own[:BLOCK, :] = (
        d_resid[...] + norm_back(values, inv_rms(values), vectors[0:1, :], total[:BLOCK])
    ).astype(BF16)
    gains[...] = total[BLOCK : BLOCK + 8]
    result[...] = (resid[...] + total_of(shared)).astype(BF16)


def collect_body(info, own, left, right, far_tok, far_state, d_tokens, d_states):
    for k, piece in ((0, own), (1, left), (3, right)):
        rows = block_rows(info[0], k)
        d_tokens[rows, :] = piece[:BLOCK, :].astype(F32)
        d_states[rows, :] = piece[BLOCK:, :].astype(F32)
    rows = block_rows(info[0], 2)
    d_tokens[rows, :] = far_tok[...].astype(F32)
    d_states[rows, :] = far_state[...].astype(F32)


def local(
    tokens,
    states,
    doc_lengths,
    w_query,
    w_key,
    w_value,
    w_output,
    w_gate,
    w_up,
    w_down,
    attention_gain,
    state_gain,
    forward_gain,
    forget_bias,
    d_output,
    d_new_states,
):
    place = lax.axis_index("mp")
    y = lax.axis_index("dp")
    z, core = lax.axis_index("z"), lax.axis_index("core")
    info = jnp.concatenate(
        [jnp.stack([place, y, z, core, 2 * z + core]), doc_lengths[0]]
    ).astype(jnp.int32)
    tokens, states = tokens[0], states[0, 0]
    grad_out, grad_new = d_output[0], d_new_states[0, 0]
    gains = jnp.stack([attention_gain, state_gain, forward_gain, forget_bias], axis=1)
    gains = jnp.pad(gains, ((0, 0), (0, 124)))
    packed = jnp.concatenate([w_query, w_key, w_value, gains], axis=1)
    output_shard = w_output.T
    late_shard = jnp.concatenate(
        [w_gate, w_up, w_down.T] + sent_on([output_shard] * 4), axis=1
    )
    late_w = lax.all_gather(late_shard, PLANE, axis=0, tiled=True)
    half = lax.dynamic_slice_in_dim(tokens, (place % 2) * 256, 256, 0)
    half = passed_along(half, 1)
    before = [half, lax.ppermute(half, "mp", [(0, 1), (1, 0), (2, 3), (3, 2)])]
    packed = jnp.stack([after(packed, half)] + [shifted(packed, "dp", k) for k in (1, 2, 3)])
    mine = [packed] + [shifted(packed, "z", k) for k in (1, 2, 3)]
    theirs = [other_core(piece) for piece in mine]

    normed, query, pair_tok, pair_state, pair_prev, qkv_w, vectors, attn_tok, sums_tok = run_early(
        attend_body,
        [
            ((2 * W, D), BF16), ((2 * W, 256), BF16), ((W, 512), BF16), ((W, 512), BF16),
            ((W, 512), BF16), ((D, QKV), BF16), ((8, D), F32), ((W, 256), BF16), ((W, 256), F32),
        ],
        [info] + mine + theirs + before + [tokens, states],
        [((D, 128), BF16)],
    )
    query_tok, query_state = Rows(query, 0, W), Rows(query, W, NS)
    attn_state, sums_state = run(
        state_fwd_body, [((NS, 256), BF16), ((NS, 256), F32)],
        [info, query_state, pair_tok],
    )
    outs_tok = sent_on([attn_tok] * 4)
    outs_state = lax.all_gather(after(attn_state, late_w[0]), "mp", axis=0)
    output_w, own_output_w = Part(late_w, D, 3), Part(late_w, 256, 12)
    down_w = Part(late_w, D, 2)
    d_mix_state, d_query_state, d_pair_more, d_forget = run(
        state_back_body,
        [((NS, D), BF16), ((NS, 256), BF16), ((NS, 512), F32), ((1, D), F32)],
        [
            info, own_output_w, vectors, grad_new, states, attn_state, query_state, pair_tok,
            sums_state,
        ],
        [((NS, 256), BF16)],
    )
    outs_tok[0] = after(outs_tok[0], d_query_state)
    resid, ff_in, hidden, d_gate_up, *blocks = run_early(
        forward_body,
        [((BLOCK, D), F32), ((W, D), BF16), ((W, D), BF16), ((W, 2 * D), BF16)]
        + [((BLOCK, D), BF16)] * 4,
        [info] + outs_tok
        + [tokens, vectors, output_w, down_w, grad_out, Part(late_w, D, 0), Part(late_w, D, 1)],
        [((W, D), BF16), ((W, D), BF16), ((W, D), F32)],
    )
    pieces = sent_back(blocks)

    d_ff_w = jnp.concatenate(
        [outer_sum(ff_in, d_gate_up).astype(BF16), outer_sum(grad_out, hidden).astype(BF16)], axis=1
    )
    pieces[0] = after(pieces[0], d_ff_w)
    d_ff_w = after(d_ff_w, *pieces[1:])
    d_ff_w = lax.psum_scatter(d_ff_w, PLANE, scatter_dimension=0, tiled=True).astype(F32)

    d_resid, d_forward, d_mix_own, *blocks = run(
        resid_back_body,
        [((BLOCK, D), F32), ((1, D), F32), ((BLOCK, D), BF16)] + [((BLOCK, 256), BF16)] * 4,
        [info] + pieces + [resid, vectors, grad_out, output_w],
    )
    pieces = sent_on(blocks)
    blocks = run(
        forward_out_body, [((2 * BLOCK, D), BF16)] * 4, [info, hidden, down_w, d_mix_own],
        [((W, D), BF16)],
    )
    pieces[0] = after(pieces[0], blocks[0])
    shared = sent_back([after(block, *pieces[1:]) for block in blocks])

    d_pair_prev, d_query_part, d_attn_tok = run(
        prev_back_body,
        [((W, 512), BF16), ((W, 256), F32), ((W, 256), BF16)],
        [info] + pieces + [query_tok, pair_prev, attn_tok, sums_tok],
    )
    d_pair_back = passed_along(d_pair_prev, -1)
    d_query_tok, d_pair_tok, d_qkv_state, d_state_gain, *blocks = run_early(
        own_back_body,
        [((W, 256), BF16), ((W, 512), F32), ((NS, QKV), BF16), ((1, D), F32)]
        + [((BLOCK, D), BF16)] * 4,
        [
            info, query_tok, pair_state, d_attn_tok, attn_tok, sums_tok, pair_tok, d_query_part,
            d_pair_more, d_query_state, qkv_w, states,
        ],
    )
    pieces_state = sent_back(blocks)
    d_pair_back = after(d_pair_back, d_state_gain, *shared[1:])
    d_qkv_tok, *blocks = run(
        token_rows_body,
        [((W, QKV), BF16)] + [((BLOCK + 16, D), BF16)] * 4,
        [
            info, d_query_tok, d_pair_tok, d_pair_back, qkv_w, tokens, d_state_gain, d_forward,
            d_forget,
        ],
        [((1, D), F32)],
    )
    pieces_tok = sent_back([after(block, *pieces_state[1:]) for block in blocks])

    keep, give = run(
        attn_grads_body,
        [((16, 32, D), BF16)] * 2,
        [
            info, normed, d_qkv_tok, d_qkv_state, d_mix_state, attn_tok,
            attn_state,
        ]
        + shared,
        [((W, D), BF16)],
    )
    own_tokens, own_states, own_grad_new = [
        lax.dynamic_slice_in_dim(rows, place * BLOCK, BLOCK, 0)
        for rows in (after(tokens, give), states, grad_new)
    ]
    d_own, result, d_gains = run(
        ends_body,
        [((2 * BLOCK, D), BF16), ((BLOCK, D), BF16), ((8, D), F32)],
        [info, after(pieces_state[0], give)] + pieces_state[1:]
        + [Rows(piece, 0, BLOCK) for piece in shared]
        + [resid, own_states, own_grad_new, vectors, own_tokens, d_resid] + pieces_tok,
    )
    came = other_core(after(give, d_own))
    result = lax.all_gather(result, "mp", axis=0, tiled=True)
    left, right = shifted_x(d_own, 1), shifted_x(d_own, -1)
    shards = run(
        scatter_z_body, [((4, 32, PACK), BF16)] * 4, [info, keep, came, d_gains],
        [((128, D), F32), ((D, 128), F32)], limit=12,
    )
    sent = shards[0]
    (updated,) = run(
        state_mix_body, [((NS, D), BF16)],
        [info, outs_state, Part(after(late_w, sent), D, 3), states, vectors],
        [((NS, D), BF16)],
    )
    shards = [shards[0]] + [shifted(after(shards[k], updated), "z", k) for k in (1, 2, 3)]
    far_tok, far_state = shifted_x(left[:BLOCK], 1), shifted_x(right[BLOCK:], -1)
    d_gate_w, d_up_w, d_down_w = d_ff_w[:, :D], d_ff_w[:, D : 2 * D], d_ff_w[:, 2 * D :].T
    shards[0] = after(shards[0], d_gate_w, d_up_w, d_down_w)
    shards = run(scatter_y_body, [((32, PACK), BF16)] * 4, [info] + shards, limit=6)
    shards = [shards[0]] + [shifted(shards[k], "dp", k) for k in (1, 2, 3)]
    d_tokens, d_states = run(
        collect_body, [((W, D), F32)] * 2,
        [info, after(d_own, shards[0]), left, right, far_tok, far_state],
    )
    shards[0] = after(shards[0], d_states)
    d_query_w, d_key_w, d_value_w, d_output_w, d_vectors = run(
        scatter_end_body, [((32, 256), F32)] * 4 + [((16, 32), F32)], [info] + shards, limit=6)
    came = other_core(d_vectors[8:12])
    d_vectors = [d_vectors[k] + came[k] for k in range(4)]
    return (
        result[None],
        updated[None, None],
        d_tokens[None],
        d_states[None, None],
        d_query_w,
        d_key_w,
        d_value_w,
        d_output_w.T,
        d_gate_w,
        d_up_w,
        d_down_w,
        d_vectors[0],
        d_vectors[1],
        d_vectors[2],
        d_vectors[3],
    )


def solution(mesh):
    plane = PLANE
    mesh = Mesh(mesh.devices.reshape(4, 4, 2, 4), PLANE + ("mp",))
    placed = (
        P("dp", SEQ, None),
        P("dp", SEQ, None, None),
        P("dp", None),
        P(plane, "mp"),
        P(plane, "mp"),
        P(plane, "mp"),
        P("mp", plane),
        P(plane, "mp"),
        P(plane, "mp"),
        P("mp", plane),
        P(plane),
        P(plane),
        P(plane),
        P(plane),
        P("dp", SEQ, None),
        P("dp", SEQ, None, None),
    )
    return jax.shard_map(
        local,
        mesh=mesh,
        in_specs=placed,
        out_specs=(
            P("dp", SEQ, None),
            P("dp", SEQ, None, None),
            P("dp", SEQ, None),
            P("dp", SEQ, None, None),
            P(plane, "mp"),
            P(plane, "mp"),
            P(plane, "mp"),
            P("mp", plane),
            P(plane, "mp"),
            P(plane, "mp"),
            P("mp", plane),
            P(plane),
            P(plane),
            P(plane),
            P(plane),
        ),
        check_vma=False,
    )
```

```python
import functools

import jax
import jax.numpy as jnp
from jax import lax
from jax.experimental import pallas as pl
from jax.experimental.pallas import tpu as pltpu
from jax.sharding import Mesh
from jax.sharding import PartitionSpec as P

D = 1024
HD = 128
W = 512
NS = 512
PARTS = 4
BLOCK = W // PARTS
QKV = 768
PACK = 1152
SHARD = 896
SCALE = HD ** (-0.5)


EPS = 1e-05
NEG = -1e30
BF16, F32 = jnp.bfloat16, jnp.float32


SEQ = ("z", "core")
CHIPS = ("dp", "z")
PLANE = ("dp", "z", "core")


def passed_along(value, steps):
    count = lax.axis_size(SEQ)
    leading, last = (max(0, -steps), min(count, count - steps))
    return lax.ppermute(value, SEQ, [(source, source + steps) for source in range(leading, last)])


def shifted_x(value, steps):
    return lax.ppermute(value, "mp", [(i, (i + steps) % PARTS) for i in range(PARTS)])


def shifted(value, axis, steps):
    return lax.ppermute(value, axis, [(i, (i + steps) % 4) for i in range(4)])


def other_core(value):
    return lax.ppermute(value, "core", [(0, 1), (1, 0)])


def sent_back(blocks):
    return [blocks[0]] + [shifted_x(blocks[k], -k) for k in (1, 2, 3)]


def sent_on(blocks):
    return [blocks[0]] + [shifted_x(blocks[k], k) for k in (1, 2, 3)]


def product(left, right):
    return jnp.dot(left, right, preferred_element_type=F32)


def product_t(left, right):
    return lax.dot_general(left, right, (((1,), (1,)), ((), ())), preferred_element_type=F32)


def outer_sum(left, right):
    return lax.dot_general(left, right, (((0,), (0,)), ((), ())), preferred_element_type=F32)


def inv_rms(values):
    return lax.rsqrt(jnp.mean(values * values, axis=-1, keepdims=True) + EPS)


def norm_back(values, scale, gain, grad):
    inner = grad * gain
    along = jnp.mean(inner * values, axis=-1, keepdims=True)
    return scale * inner - values * (scale * scale * scale) * along


def block_rows(place, k):
    return pl.ds(pl.multiple_of(((place + PARTS - k) & 3) * BLOCK, BLOCK), BLOCK)


def total_of(pieces):
    total = pieces[0][...].astype(F32)
    for piece in pieces[1:]:
        total = total + piece[...].astype(F32)
    return total


def after(value, *others):
    return lax.optimization_barrier((value, *others))[0]


class Part:
    def __init__(self, array, width, index):
        self.array, self.shape = array, (array.shape[0], width)
        self.where = lambda ref, info: ref.at[:, pl.ds(index * width, width)]
        self.block = lambda _: (0, index)


class Rows:
    def __init__(self, array, start, size):
        self.array, self.shape = array, (size, array.shape[1])
        self.where = lambda ref, info: ref.at[pl.ds(start, size), :]
        self.block = lambda _: (start // size, 0)


class Source:
    def __init__(self, copy, ref):
        self.copy, self.ref = copy, ref
        copy.start()

    def ready(self):
        if self.copy is not None:
            self.copy.wait()
            self.copy = None
        return self.ref

    def __getitem__(self, index):
        return self.ready()[index]


class Target:
    def __init__(self, copy, ref):
        self.copy, self.ref, self.sent = copy, ref, False
        self.shape, self.dtype = ref.shape, ref.dtype

    def send(self):
        if not self.sent:
            self.copy.start()
            self.sent = True

    def __getitem__(self, index):
        return self.ref[index]

    def __setitem__(self, index, value):
        self.ref[index] = value


class Held:
    def __init__(self, ref):
        self.ref, self.shape, self.dtype = ref, ref.shape, ref.dtype

    def ready(self):
        return self.ref

    def send(self):
        pass

    def __getitem__(self, index):
        return self.ref[index]

    def __setitem__(self, index, value):
        self.ref[index] = value


def ready(*sources):
    for source in sources:
        source.ready()


def send(*targets):
    for target in targets:
        target.send()


def run(body, outs, args, scratch=(), limit=60):
    n_refs = len(args) - 1 + len(outs)

    def kernel(info, *refs):
        body(info, *[Held(ref) for ref in refs[:n_refs]], *refs[n_refs:])

    def spec(arg):
        if hasattr(arg, "block"):
            return pl.BlockSpec(arg.shape, arg.block)
        return pl.BlockSpec(arg.shape, lambda _: (0,) * len(arg.shape))

    call = pl.pallas_call(
        kernel,
        out_shape=[jax.ShapeDtypeStruct(shape, kind) for shape, kind in outs],
        grid=(1,),
        in_specs=[pl.BlockSpec(memory_space=pltpu.SMEM)] + [spec(arg) for arg in args[1:]],
        out_specs=[spec(jax.ShapeDtypeStruct(shape, kind)) for shape, kind in outs],
        scratch_shapes=[pltpu.VMEM(shape, kind) for shape, kind in scratch],
        compiler_params=pltpu.CompilerParams(vmem_limit_bytes=limit << 20),
        cost_estimate=pl.CostEstimate(flops=1, bytes_accessed=1, transcendentals=0),
        name=body.__name__.replace("_body", ""),
    )
    return list(call(*[arg.array if hasattr(arg, "block") else arg for arg in args]))


def run_early(body, outs, args, scratch=(), limit=60):
    n_in, n_out = len(args) - 1, len(outs)

    def kernel(info, *refs):
        given, results = refs[:n_in], refs[n_in : n_in + n_out]
        held = refs[n_in + n_out : 2 * (n_in + n_out)]
        extra, (in_sems, out_sems) = refs[2 * (n_in + n_out) : -2], refs[-2:]
        sources = []
        for index, (arg, ref) in enumerate(zip(args[1:], given)):
            where = arg.where(ref, info) if hasattr(arg, "where") else ref
            copy = pltpu.make_async_copy(where, held[index], in_sems.at[index])
            sources.append(Source(copy, held[index]))
        targets = []
        for index, ref in enumerate(results):
            copy = pltpu.make_async_copy(held[n_in + index], ref, out_sems.at[index])
            targets.append(Target(copy, held[n_in + index]))
        body(info, *sources, *targets, *extra)
        ready(*sources)
        send(*targets)
        for target in targets:
            target.copy.wait()

    arrays = [arg.array if hasattr(arg, "where") else arg for arg in args]
    buffers = [pltpu.VMEM(arg.shape, array.dtype) for arg, array in zip(args[1:], arrays[1:])]
    buffers += [pltpu.VMEM(shape, kind) for shape, kind in outs]
    call = pl.pallas_call(
        kernel,
        out_shape=[jax.ShapeDtypeStruct(shape, kind) for shape, kind in outs],
        in_specs=[pl.BlockSpec(memory_space=pltpu.SMEM)] + [pl.BlockSpec(memory_space=pl.ANY)] * n_in,
        out_specs=[pl.BlockSpec(memory_space=pl.ANY)] * n_out,
        scratch_shapes=buffers
        + [pltpu.VMEM(shape, kind) for shape, kind in scratch]
        + [pltpu.SemaphoreType.DMA((n_in,)), pltpu.SemaphoreType.DMA((n_out,))],
        compiler_params=pltpu.CompilerParams(vmem_limit_bytes=limit << 20),
        cost_estimate=pl.CostEstimate(flops=1, bytes_accessed=1, transcendentals=0),
        name=body.__name__.replace("_body", ""),
    )
    return list(call(*arrays))


def softmax_parts(scores):
    peak = functools.reduce(
        jnp.maximum, [jnp.max(part, axis=-1, keepdims=True) for part in scores]
    )
    grown = [jnp.exp(part - peak) for part in scores]
    total = functools.reduce(jnp.add, [jnp.sum(part, axis=-1, keepdims=True) for part in grown])
    inverse = 1.0 / total
    return [(part * inverse).astype(BF16) for part in grown], peak + jnp.log(total)


def state_fwd_body(info, query, pair_tok, attn, logsum):
    ready(query, pair_tok)
    for head in range(2):
        lanes = pl.ds(head * HD, HD)
        key, value = pair_tok[:, lanes], pair_tok[:, pl.ds(256 + head * HD, HD)]

        @pl.loop(0, 2)
        def _(b):
            here = pl.ds(pl.multiple_of(b * 256, 256), 256)
            scores = product_t(query[here, lanes], key) * SCALE
            (probs,), total = softmax_parts([scores])
            attn[here, lanes] = product(probs, value).astype(BF16)
            logsum[here, lanes] = jnp.broadcast_to(total, (256, HD))


def documents(info, positions):
    count, end = jnp.zeros_like(positions), 0
    for index in range(4):
        end = end + info[5 + index]
        count = count + (positions >= end).astype(jnp.int32)
    return count


def nearby_masks(info, first_row, rows):
    start = info[4] * W
    query_pos = start + first_row + lax.broadcasted_iota(jnp.int32, (rows, 1), 0)
    key_pos = start + lax.broadcasted_iota(jnp.int32, (1, W), 1)
    query_doc = documents(info, query_pos)
    prev = (key_pos >= W) & (documents(info, key_pos - W) == query_doc)
    own = (key_pos <= query_pos) & (documents(info, key_pos) == query_doc)
    return prev, own


def attend_body(info, *refs):
    mine, theirs, before, tokens, states = refs[:4], refs[4:8], refs[8:10], refs[10], refs[11]
    normed, query, pair_tok, pair_state, pair_prev, qkv_w, vectors = refs[12:19]
    attn, logsum, gains = refs[19:]
    y, z, core = info[1], info[2], info[3]
    for kz in range(4):
        for side, pieces in ((0, mine), (1, theirs)):
            for ky in range(4):
                shard = ((y + 4 - ky) & 3) * 8 + ((z + 4 - kz) & 3) * 2 + (core ^ side)
                rows = pl.ds(pl.multiple_of(shard * 32, 32), 32)
                qkv_w[rows, :] = pieces[kz][ky, :, :QKV]
                gains[rows, :] = pieces[kz][ky, :, QKV:]
    qkv_w.send()
    across = gains[...].astype(F32).T
    vectors[0:3, :] = across[0:3]
    vectors[3:4, :] = jax.nn.sigmoid(across[3:4])
    vectors[4:8, :] = jnp.zeros((4, D), F32)
    vectors.send()

    def normalized(values, lane):
        values = values.astype(F32)
        return (values * inv_rms(values) * vectors[lane : lane + 1, :]).astype(BF16)

    for part, (rows, pair) in enumerate(((tokens, pair_tok), (states, pair_state))):
        ready(rows)

        @pl.loop(0, 2)
        def _(b):
            here = pl.ds(pl.multiple_of(b * 256, 256), 256)
            there = pl.ds(pl.multiple_of(part * W + b * 256, 256), 256)
            normed[there, :] = normalized(rows[here, :], part)
            out = product(normed[there, :], qkv_w[...]).astype(BF16)
            query[there, :] = out[:, :256]
            pair[here, :] = out[:, 256:]

        pair.send()
    send(normed, query)
    for b, half in enumerate(before):
        here = pl.ds(pl.multiple_of(((info[0] + b) & 1) * 256, 256), 256)
        pair_prev[here, :] = product(normalized(half[...], 0), qkv_w[:, 256:]).astype(BF16)
    pair_prev.send()

    for head in range(2):
        lanes = pl.ds(head * HD, HD)
        far = pl.ds(256 + head * HD, HD)

        @pl.loop(0, 2)
        def _(b):
            here = pl.ds(pl.multiple_of(b * 256, 256), 256)
            prev, own = nearby_masks(info, b * 256, 256)
            rows = query[here, lanes]
            scores = [
                jnp.where(prev, product_t(rows, pair_prev[:, lanes]) * SCALE, NEG),
                jnp.where(own, product_t(rows, pair_tok[:, lanes]) * SCALE, NEG),
                product_t(rows, pair_state[:, lanes]) * SCALE,
            ]
            probs, total = softmax_parts(scores)
            out = (
                product(probs[0], pair_prev[:, far])
                + product(probs[1], pair_tok[:, far])
                + product(probs[2], pair_state[:, far])
            )
            attn[here, lanes] = out.astype(BF16)
            logsum[here, lanes] = jnp.broadcast_to(total, (256, HD))


def state_mix_body(info, outs, output_w, states, vectors, updated, attn):
    ready(outs, output_w, states, vectors)
    for k in range(4):
        attn[:, pl.ds(256 * k, 256)] = outs[(info[0] + 4 - k) & 3]
    forget = vectors[3:4, :]

    @pl.loop(0, 2)
    def _(b):
        here = pl.ds(pl.multiple_of(b * 256, 256), 256)
        mixed = product_t(attn[here, :], output_w[...])
        given = states[here, :].astype(F32)
        updated[here, :] = (given * forget + mixed * (1.0 - forget)).astype(BF16)


def forward_body(info, *refs):
    outs = refs[:4]
    tokens, vectors, output_w, down_w, grad_out, gate_w, up_w = refs[4:11]
    resid, ff_in, hidden, d_gate_up = refs[11:15]
    blocks = refs[15:19]
    d_ff_in, attn, values = refs[19:]
    for k in range(4):
        attn[:, pl.ds(256 * k, 256)] = outs[k][...]
    ready(tokens, vectors, output_w)
    for c in range(2):
        at = pl.ds(c * 512, 512)
        values[:, at] = tokens[:, at].astype(F32) + product_t(attn[...], output_w[at, :])

    @pl.loop(0, 4)
    def _(b):
        here = pl.ds(pl.multiple_of(b * 128, 128), 128)
        rows = values[here, :]
        ff_in[here, :] = (rows * inv_rms(rows) * vectors[2:3, :]).astype(BF16)

    ff_in.send()
    resid[...] = values[block_rows(info[0], 0), :]
    resid.send()
    for c in range(2):
        at, beyond = pl.ds(c * 512, 512), pl.ds(D + c * 512, 512)
        d_hidden = product(grad_out[...], down_w[:, at])
        gate = product(ff_in[...], gate_w[:, at])
        up = product(ff_in[...], up_w[:, at])
        sigma = jax.nn.sigmoid(gate)
        active = gate * sigma
        hidden[:, at] = (active * up).astype(BF16)
        d_gate = d_hidden * up * sigma * (1.0 + gate * (1.0 - sigma))
        d_gate_up[:, at] = d_gate.astype(BF16)
        d_gate_up[:, beyond] = (d_hidden * active).astype(BF16)
    send(hidden, d_gate_up)
    for c in range(2):
        at = pl.ds(c * 512, 512)
        d_ff_in[:, at] = (
            product_t(d_gate_up[:, :D], gate_w[at, :]) + product_t(d_gate_up[:, D:], up_w[at, :])
        ).astype(BF16)
    for k in range(4):
        blocks[k][...] = d_ff_in[block_rows(info[0], k), :]
        blocks[k].send()


def forward_out_body(info, hidden, down_w, d_mix, *refs):
    shared, out = refs[:4], refs[4]
    ready(hidden, down_w)
    for c in range(4):
        at = pl.ds(c * 256, 256)
        out[:, at] = product_t(hidden[...], down_w[at, :]).astype(BF16)
    for k in range(4):
        shared[k][:BLOCK, :] = out[block_rows(info[0], k), :]
        shared[k][BLOCK:, :] = d_mix[...]


def resid_back_body(info, *refs):
    pieces, resid, vectors, grad_out, output_w = refs[:4], refs[4], refs[5], refs[6], refs[7]
    d_resid, d_forward, d_mix = refs[8:11]
    blocks = refs[11:]
    grad, values = total_of(pieces), resid[...]
    scale = inv_rms(values)
    total = grad_out[block_rows(info[0], 0), :].astype(F32) + norm_back(values, scale, vectors[2:3, :], grad)
    rounded = total.astype(BF16)
    for k in range(4):
        at = pl.ds(256 * ((4 - k) % 4), 256)
        blocks[k][...] = product(rounded, output_w[:, at]).astype(BF16)
    d_mix[...] = rounded
    d_resid[...] = total
    d_forward[...] = jnp.sum(grad * values * scale, axis=0, keepdims=True)


def part_back(query, turned_query, key, value, d_out, turned_d_out, logsum, center, mask):
    scores = product_t(query, key) * SCALE
    if mask is not None:
        scores = jnp.where(mask, scores, NEG)
    probs = jnp.exp(scores - logsum)
    d_probs = product_t(d_out, value)
    d_scores = (probs * (d_probs - center)).astype(BF16)
    d_query = product(d_scores, key) * SCALE
    d_key = product(turned_query, d_scores) * SCALE
    d_value = product(turned_d_out, probs.astype(BF16))
    return d_query, d_key.T, d_value.T


def turned(values):
    return values.astype(F32).T.astype(BF16)


def center_of(d_out, out):
    return jnp.sum(d_out.astype(F32) * out.astype(F32), axis=-1, keepdims=True)


def state_back_body(
    info, output_w, vectors, grad_new, states, attn, query, pair_tok, logsum, *refs
):
    d_mix, d_query, d_pair, d_forget, d_attn = refs
    ready(output_w, vectors, grad_new, attn)
    forget = vectors[3:4, :]
    own = block_rows(info[0], 0)
    d_forget[...] = jnp.sum(
        grad_new[own, :].astype(F32) * states[own, :].astype(F32), axis=0, keepdims=True
    )

    @pl.loop(0, 2)
    def _(b):
        here = pl.ds(pl.multiple_of(b * 256, 256), 256)
        grad = grad_new[here, :].astype(F32)
        rounded = (grad * (1.0 - forget)).astype(BF16)
        d_mix[here, :] = rounded
        d_attn[here, :] = product(rounded, output_w[...]).astype(BF16)
        mixed = product_t(attn[here, :], output_w[...])
        d_forget[...] -= jnp.sum(grad * mixed, axis=0, keepdims=True)

    d_mix.send()
    d_forget[...] *= forget * (1.0 - forget)
    for head in range(2):
        lanes = pl.ds(head * HD, HD)
        far = pl.ds(256 + head * HD, HD)
        rows, d_out = query[:, lanes], d_attn[:, lanes]
        center = center_of(d_out, attn[:, lanes])
        total = logsum[:, pl.ds(head * HD, 1)]
        d_rows, d_key, d_value = part_back(
            rows, turned(rows), pair_tok[:, lanes], pair_tok[:, far], d_out, turned(d_out),
            total, center, None,
        )
        d_query[:, lanes] = d_rows.astype(BF16)
        d_pair[:, lanes] = d_key
        d_pair[:, far] = d_value


def prev_back_body(info, *refs):
    pieces, query, pair_prev, attn, logsum = refs[:4], refs[4], refs[5], refs[6], refs[7]
    d_pair, d_query, d_attn = refs[8:]
    for k in range(4):
        d_attn[block_rows(info[0], k), :] = pieces[k][...]
    d_attn.send()
    prev, _ = nearby_masks(info, 0, W)
    for head in range(2):
        lanes = pl.ds(head * HD, HD)
        far = pl.ds(256 + head * HD, HD)
        rows, d_out = query[:, lanes], d_attn[:, lanes]
        center = center_of(d_out, attn[:, lanes])
        total = logsum[:, pl.ds(head * HD, 1)]
        d_rows, d_key, d_value = part_back(
            rows, turned(rows), pair_prev[:, lanes], pair_prev[:, far], d_out, turned(d_out),
            total, center, prev,
        )
        d_query[:, lanes] = d_rows
        d_pair[:, lanes] = d_key.astype(BF16)
        d_pair[:, far] = d_value.astype(BF16)


def rows_back(info, given, qkv_w, d_qkv, d_gain, blocks):
    d_gain[...] = jnp.zeros(d_gain.shape, F32)
    for k in range(4):
        rows = block_rows(info[0], k)
        grad = product_t(d_qkv[rows, :], qkv_w[...])
        values = given[rows, :].astype(F32)
        d_gain[...] += jnp.sum(grad * values * inv_rms(values), axis=0, keepdims=True)
        blocks[k][...] = grad.astype(BF16)
        blocks[k].send()


def own_back_body(
    info, query, pair_state, d_attn, attn, logsum, pair_tok, d_query_part, d_pair_more,
    d_query_state, qkv_w, states, *refs,
):
    d_query, d_pair_tok, d_qkv, d_gain = refs[:4]
    blocks = refs[4:]
    _, own = nearby_masks(info, 0, W)
    for head in range(2):
        lanes = pl.ds(head * HD, HD)
        far = pl.ds(256 + head * HD, HD)
        rows, d_out = query[:, lanes], d_attn[:, lanes]
        rows_t, d_out_t = turned(rows), turned(d_out)
        center = center_of(d_out, attn[:, lanes])
        total = logsum[:, pl.ds(head * HD, 1)]
        more, d_key, d_value = part_back(
            rows, rows_t, pair_state[:, lanes], pair_state[:, far], d_out, d_out_t, total, center,
            None,
        )
        d_qkv[:, pl.ds(256 + head * HD, HD)] = d_key.astype(BF16)
        d_qkv[:, pl.ds(512 + head * HD, HD)] = d_value.astype(BF16)
        d_rows, d_key, d_value = part_back(
            rows, rows_t, pair_tok[:, lanes], pair_tok[:, far], d_out, d_out_t, total, center, own
        )
        d_pair_tok[:, lanes] = d_key + d_pair_more[:, lanes]
        d_pair_tok[:, far] = d_value + d_pair_more[:, far]
        d_query[:, lanes] = (d_query_part[:, lanes] + d_rows + more).astype(BF16)
    send(d_pair_tok, d_query)
    d_qkv[:, :256] = d_query_state[...]
    d_qkv.send()

    rows_back(info, states, qkv_w, d_qkv, d_gain, blocks)


def token_rows_body(
    info, d_query, d_pair, d_pair_back, qkv_w, tokens, d_state, d_forward, d_forget, d_qkv, *refs
):
    blocks, d_gain = refs[:4], refs[4]
    d_qkv[:, :256] = d_query[...]
    d_qkv[:, 256:] = (d_pair[...] + d_pair_back[...].astype(F32)).astype(BF16)
    tops = [Held(block.ref.at[pl.ds(0, BLOCK), :]) for block in blocks]
    rows_back(info, tokens, qkv_w, d_qkv, d_gain, tops)
    gains = jnp.concatenate(
        [d_gain[...], d_state[...], d_forward[...], d_forget[...], jnp.zeros((12, D), F32)], axis=0
    ).astype(BF16)
    for block in blocks:
        block[BLOCK:, :] = gains


def attn_grads_body(
    info, normed, d_qkv_tok, d_qkv_state, d_mix_state, attn_tok, attn_state, *refs
):
    shared, keep, give, whole = refs[:4], refs[4], refs[5], refs[6]
    for k in range(4):
        whole[block_rows(info[0], 4 - k), :] = shared[k][BLOCK:, :]
    first = info[3] == 0
    ready(normed, d_qkv_tok, d_qkv_state, d_mix_state, attn_tok, attn_state)

    @pl.loop(0, 4)
    def _(c):
        at = pl.ds(pl.multiple_of(c * 256, 256), 256)
        groups = pl.ds(pl.multiple_of(c * 4, 4), 4)
        sums = (
            outer_sum(normed[:W, at], d_qkv_tok[...]) + outer_sum(normed[W:, at], d_qkv_state[...]),
            outer_sum(whole[:, at], attn_tok[...]) + outer_sum(d_mix_state[:, at], attn_state[...]),
        )
        for part, lanes in zip(sums, (pl.ds(0, QKV), pl.ds(QKV, 256))):
            split = part.astype(BF16).reshape(4, 2, 32, part.shape[1])
            even, odd = split[:, 0], split[:, 1]
            keep[groups, :, lanes] = jnp.where(first, even, odd)
            give[groups, :, lanes] = jnp.where(first, odd, even)


def scatter_z_body(info, keep, came, gains, *refs):
    pieces, rows, across = refs[:4], refs[4], refs[5]
    rows[...] = jnp.zeros_like(rows)
    rows[0:8, :] = gains[...]
    rows[8:16, :] = gains[...]
    across[...] = rows[...].T
    near = lax.broadcasted_iota(jnp.int32, (32, 128), 1) < 8
    for k in range(4):
        z = (info[2] + k) & 3
        for y in range(4):
            group = y * 4 + z
            pieces[k][y, :, :D] = (keep[group].astype(F32) + came[group].astype(F32)).astype(BF16)
            own = across[pl.ds(pl.multiple_of((group * 2 + info[3]) * 32, 32), 32), :]
            other = across[pl.ds(pl.multiple_of((group * 2 + 1 - info[3]) * 32, 32), 32), :]
            pieces[k][y, :, D:] = jnp.where(near, own, other).astype(BF16)
        pieces[k].send()


def scatter_y_body(info, *refs):
    pieces, outs = refs[:4], refs[4:]
    for k in range(4):
        y = (info[1] + k) & 3
        total = pieces[0][y].astype(F32)
        for piece in pieces[1:]:
            total = total + piece[y].astype(F32)
        outs[k][...] = total.astype(BF16)


def scatter_end_body(info, *refs):
    total = total_of(refs[:4])
    d_query, d_key, d_value, d_output, d_vectors = refs[4:]
    d_query[...] = total[:, :256]
    d_key[...] = total[:, 256:512]
    d_value[...] = total[:, 512:768]
    d_output[...] = total[:, 768:1024]
    d_vectors[...] = total[:, 1024:].T[:16]


def ends_body(info, *refs):
    from_states, shared, resid, states, grad_new, vectors, tokens, d_resid, from_tokens = (
        refs[:4], refs[4:8], refs[8], refs[9], refs[10], refs[11], refs[12], refs[13], refs[14:18],
    )
    d_own, result, gains = refs[18:]
    values = states[...].astype(F32)
    d_own[BLOCK:, :] = (
        grad_new[...].astype(F32) * vectors[3:4, :]
        + norm_back(values, inv_rms(values), vectors[1:2, :], total_of(from_states))
    ).astype(BF16)
    values = tokens[...].astype(F32)
    total = total_of(from_tokens)
    d_own[:BLOCK, :] = (
        d_resid[...] + norm_back(values, inv_rms(values), vectors[0:1, :], total[:BLOCK])
    ).astype(BF16)
    gains[...] = total[BLOCK : BLOCK + 8]
    result[...] = (resid[...] + total_of(shared)).astype(BF16)


def collect_body(info, own, left, right, d_tokens, d_states):
    for k, piece in ((0, own), (1, left), (3, right)):
        rows = block_rows(info[0], k)
        d_tokens[rows, :] = piece[:BLOCK, :].astype(F32)
        d_states[rows, :] = piece[BLOCK:, :].astype(F32)
    rows = block_rows(info[0], 2)
    d_tokens[rows, :] = jnp.zeros((BLOCK, D), F32)
    d_states[rows, :] = jnp.zeros((BLOCK, D), F32)


def completed(info, far_tok, far_state, d_tokens, d_states):
    def kernel(info, tok, state, old_tokens, old_states, out_tokens, out_states, wide, sems):
        copies = []
        for index, (piece, out) in enumerate(((tok, out_tokens), (state, out_states))):
            wide[index] = piece[...].astype(F32)
            rows = out.at[block_rows(info[0], 2), :]
            copies.append(pltpu.make_async_copy(wide.at[index], rows, sems.at[index]))
            copies[-1].start()
        for copy in copies:
            copy.wait()

    held = pl.BlockSpec(memory_space=pl.ANY)
    near = pl.BlockSpec(memory_space=pltpu.VMEM)
    return pl.pallas_call(
        kernel,
        out_shape=[jax.ShapeDtypeStruct((W, D), F32)] * 2,
        in_specs=[pl.BlockSpec(memory_space=pltpu.SMEM), near, near, held, held],
        out_specs=[held, held],
        scratch_shapes=[pltpu.VMEM((2, BLOCK, D), F32), pltpu.SemaphoreType.DMA((2,))],
        input_output_aliases={3: 0, 4: 1},
        compiler_params=pltpu.CompilerParams(vmem_limit_bytes=60 << 20),
        name="completed",
    )(info, far_tok, far_state, d_tokens, d_states)


def local(
    tokens,
    states,
    doc_lengths,
    w_query,
    w_key,
    w_value,
    w_output,
    w_gate,
    w_up,
    w_down,
    attention_gain,
    state_gain,
    forward_gain,
    forget_bias,
    d_output,
    d_new_states,
):
    place = lax.axis_index("mp")
    y = lax.axis_index("dp")
    z, core = lax.axis_index("z"), lax.axis_index("core")
    info = jnp.concatenate(
        [jnp.stack([place, y, z, core, 2 * z + core]), doc_lengths[0]]
    ).astype(jnp.int32)
    tokens, states = tokens[0], states[0, 0]
    grad_out, grad_new = d_output[0], d_new_states[0, 0]
    gains = jnp.stack([attention_gain, state_gain, forward_gain, forget_bias], axis=1)
    gains = jnp.pad(gains, ((0, 0), (0, 124)))
    packed = jnp.concatenate([w_query, w_key, w_value, gains], axis=1)
    output_shard = w_output.T
    late_shard = jnp.concatenate(
        [w_gate, w_up, w_down.T] + sent_on([output_shard] * 4), axis=1
    )
    late_w = lax.all_gather(late_shard, PLANE, axis=0, tiled=True)
    half = lax.dynamic_slice_in_dim(tokens, (place % 2) * 256, 256, 0)
    half = passed_along(half, 1)
    before = [half, lax.ppermute(half, "mp", [(0, 1), (1, 0), (2, 3), (3, 2)])]
    packed = jnp.stack([after(packed, half)] + [shifted(packed, "dp", k) for k in (1, 2, 3)])
    mine = [packed] + [shifted(packed, "z", k) for k in (1, 2, 3)]
    theirs = [other_core(piece) for piece in mine]

    normed, query, pair_tok, pair_state, pair_prev, qkv_w, vectors, attn_tok, sums_tok = run_early(
        attend_body,
        [
            ((2 * W, D), BF16), ((2 * W, 256), BF16), ((W, 512), BF16), ((W, 512), BF16),
            ((W, 512), BF16), ((D, QKV), BF16), ((8, D), F32), ((W, 256), BF16), ((W, 256), F32),
        ],
        [info] + mine + theirs + before + [tokens, states],
        [((D, 128), BF16)],
    )
    query_tok, query_state = Rows(query, 0, W), Rows(query, W, NS)
    attn_state, sums_state = run(
        state_fwd_body, [((NS, 256), BF16), ((NS, 256), F32)],
        [info, query_state, pair_tok],
    )
    outs_tok = sent_on([attn_tok] * 4)
    outs_state = lax.all_gather(after(attn_state, late_w[0]), "mp", axis=0)
    output_w, own_output_w = Part(late_w, D, 3), Part(late_w, 256, 12)
    down_w = Part(late_w, D, 2)
    d_mix_state, d_query_state, d_pair_more, d_forget = run(
        state_back_body,
        [((NS, D), BF16), ((NS, 256), BF16), ((NS, 512), F32), ((1, D), F32)],
        [
            info, own_output_w, vectors, grad_new, states, attn_state, query_state, pair_tok,
            sums_state,
        ],
        [((NS, 256), BF16)],
    )
    outs_tok[0] = after(outs_tok[0], d_query_state)
    resid, ff_in, hidden, d_gate_up, *blocks = run_early(
        forward_body,
        [((BLOCK, D), F32), ((W, D), BF16), ((W, D), BF16), ((W, 2 * D), BF16)]
        + [((BLOCK, D), BF16)] * 4,
        [info] + outs_tok
        + [tokens, vectors, output_w, down_w, grad_out, Part(late_w, D, 0), Part(late_w, D, 1)],
        [((W, D), BF16), ((W, D), BF16), ((W, D), F32)],
    )
    pieces = sent_back(blocks)

    d_ff_w = jnp.concatenate(
        [outer_sum(ff_in, d_gate_up).astype(BF16), outer_sum(grad_out, hidden).astype(BF16)], axis=1
    )
    pieces[0] = after(pieces[0], d_ff_w)
    d_ff_w = after(d_ff_w, *pieces[1:])
    d_ff_w = lax.psum_scatter(d_ff_w, PLANE, scatter_dimension=0, tiled=True).astype(F32)

    d_resid, d_forward, d_mix_own, *blocks = run(
        resid_back_body,
        [((BLOCK, D), F32), ((1, D), F32), ((BLOCK, D), BF16)] + [((BLOCK, 256), BF16)] * 4,
        [info] + pieces + [resid, vectors, grad_out, output_w],
    )
    pieces = sent_on(blocks)
    blocks = run(
        forward_out_body, [((2 * BLOCK, D), BF16)] * 4, [info, hidden, down_w, d_mix_own],
        [((W, D), BF16)],
    )
    pieces[0] = after(pieces[0], blocks[0])
    shared = sent_back([after(block, *pieces[1:]) for block in blocks])

    d_pair_prev, d_query_part, d_attn_tok = run(
        prev_back_body,
        [((W, 512), BF16), ((W, 256), F32), ((W, 256), BF16)],
        [info] + pieces + [query_tok, pair_prev, attn_tok, sums_tok],
    )
    d_pair_back = passed_along(d_pair_prev, -1)
    d_query_tok, d_pair_tok, d_qkv_state, d_state_gain, *blocks = run_early(
        own_back_body,
        [((W, 256), BF16), ((W, 512), F32), ((NS, QKV), BF16), ((1, D), F32)]
        + [((BLOCK, D), BF16)] * 4,
        [
            info, query_tok, pair_state, d_attn_tok, attn_tok, sums_tok, pair_tok, d_query_part,
            d_pair_more, d_query_state, qkv_w, states,
        ],
    )
    pieces_state = sent_back(blocks)
    d_pair_back = after(d_pair_back, d_state_gain, *shared[1:])
    d_qkv_tok, *blocks = run(
        token_rows_body,
        [((W, QKV), BF16)] + [((BLOCK + 16, D), BF16)] * 4,
        [
            info, d_query_tok, d_pair_tok, d_pair_back, qkv_w, tokens, d_state_gain, d_forward,
            d_forget,
        ],
        [((1, D), F32)],
    )
    pieces_tok = sent_back([after(block, *pieces_state[1:]) for block in blocks])

    keep, give = run(
        attn_grads_body,
        [((16, 32, D), BF16)] * 2,
        [
            info, normed, d_qkv_tok, d_qkv_state, d_mix_state, attn_tok,
            attn_state,
        ]
        + shared,
        [((W, D), BF16)],
    )
    own_tokens, own_states, own_grad_new = [
        lax.dynamic_slice_in_dim(rows, place * BLOCK, BLOCK, 0)
        for rows in (after(tokens, give), states, grad_new)
    ]
    d_own, result, d_gains = run(
        ends_body,
        [((2 * BLOCK, D), BF16), ((BLOCK, D), BF16), ((8, D), F32)],
        [info, after(pieces_state[0], give)] + pieces_state[1:]
        + [Rows(piece, 0, BLOCK) for piece in shared]
        + [resid, own_states, own_grad_new, vectors, own_tokens, d_resid] + pieces_tok,
    )
    came = other_core(after(give, d_own))
    result = lax.all_gather(result, "mp", axis=0, tiled=True)
    left, right = shifted_x(d_own, 1), shifted_x(d_own, -1)
    shards = run(
        scatter_z_body, [((4, 32, PACK), BF16)] * 4, [info, keep, came, d_gains],
        [((128, D), F32), ((D, 128), F32)], limit=12,
    )
    sent = shards[0]
    (updated,) = run(
        state_mix_body, [((NS, D), BF16)],
        [info, outs_state, Part(after(late_w, sent), D, 3), states, vectors],
        [((NS, D), BF16)],
    )
    shards = [shards[0]] + [shifted(after(shards[k], updated), "z", k) for k in (1, 2, 3)]
    d_gate_w, d_up_w, d_down_w = d_ff_w[:, :D], d_ff_w[:, D : 2 * D], d_ff_w[:, 2 * D :].T
    d_tokens, d_states = run(
        collect_body, [((W, D), F32)] * 2, [info, after(d_own, d_gate_w), left, right]
    )
    far_tok = shifted_x(after(left, d_states)[:BLOCK], 1)
    far_state = shifted_x(after(right, d_states)[BLOCK:], -1)
    shards[0] = after(shards[0], d_gate_w, d_up_w, d_down_w, d_states)
    shards = run(scatter_y_body, [((32, PACK), BF16)] * 4, [info] + shards, limit=6)
    shards = [shards[0]] + [shifted(shards[k], "dp", k) for k in (1, 2, 3)]
    d_tokens, d_states = completed(
        info, after(far_tok, shards[0]), far_state, d_tokens, d_states
    )
    shards[0] = after(shards[0], d_states)
    d_query_w, d_key_w, d_value_w, d_output_w, d_vectors = run(
        scatter_end_body, [((32, 256), F32)] * 4 + [((16, 32), F32)], [info] + shards, limit=6)
    came = other_core(d_vectors[8:12])
    d_vectors = [d_vectors[k] + came[k] for k in range(4)]
    return (
        result[None],
        updated[None, None],
        d_tokens[None],
        d_states[None, None],
        d_query_w,
        d_key_w,
        d_value_w,
        d_output_w.T,
        d_gate_w,
        d_up_w,
        d_down_w,
        d_vectors[0],
        d_vectors[1],
        d_vectors[2],
        d_vectors[3],
    )


def solution(mesh):
    plane = PLANE
    mesh = Mesh(mesh.devices.reshape(4, 4, 2, 4), PLANE + ("mp",))
    placed = (
        P("dp", SEQ, None),
        P("dp", SEQ, None, None),
        P("dp", None),
        P(plane, "mp"),
        P(plane, "mp"),
        P(plane, "mp"),
        P("mp", plane),
        P(plane, "mp"),
        P(plane, "mp"),
        P("mp", plane),
        P(plane),
        P(plane),
        P(plane),
        P(plane),
        P("dp", SEQ, None),
        P("dp", SEQ, None, None),
    )
    return jax.shard_map(
        local,
        mesh=mesh,
        in_specs=placed,
        out_specs=(
            P("dp", SEQ, None),
            P("dp", SEQ, None, None),
            P("dp", SEQ, None),
            P("dp", SEQ, None, None),
            P(plane, "mp"),
            P(plane, "mp"),
            P(plane, "mp"),
            P("mp", plane),
            P(plane, "mp"),
            P(plane, "mp"),
            P("mp", plane),
            P(plane),
            P(plane),
            P(plane),
            P(plane),
        ),
        check_vma=False,
    )
```
